128 devices in a mesh: grp: 2 (over x_hi), prompt: 8 (over y, core), resp: 8 (over z, x_lo).
Axes of the slice: x: 4 (x_hi: 2, x_lo: 2; x = x_hi * 2 + x_lo), y: 4, z: 4, core: 2. Of those that a mesh axis runs over, the one named last changes fastest.
Arguments:
- prompt_states: bfloat16 [2, 512, 4096], P('grp', 'prompt'), may hold values from -6 to 6
- response_states: bfloat16 [2, 64, 512, 4096], P('grp', ('prompt', 'resp')), may hold values from -6 to 6
- queries: bfloat16 [2, 64, 512, 2048], P('grp', ('prompt', 'resp'))
- grad_output: bfloat16 [2, 64, 512, 2048], P('grp', ('prompt', 'resp')), may hold values from -24 to 24
- key_weight: bfloat16 [4096, 512], replicated, may hold values from -0.09375 to 0.09375
- value_weight: bfloat16 [4096, 512], replicated, may hold values from -0.09375 to 0.09375
- rewards: float32 [2, 64], P('grp', ('prompt', 'resp'))
- lengths: int32 [2, 64], P('grp', ('prompt', 'resp')), may hold values from 1 to 512, 19660 in all within a row
- group_ids: int32 [2, 64], P('grp', ('prompt', 'resp')), may hold values from 0 to 7
Outputs:
- query_grad: bfloat16 [2, 64, 512, 2048], P('grp', ('prompt', 'resp'))
- key_weight_grad: float32 [4096, 512], P(('prompt', 'resp'))
- value_weight_grad: float32 [4096, 512], P(('prompt', 'resp'))
The draws below stay inside these ranges and needn't reach their ends.
Inputs may be any that keep to these rules, and one draw needn't show every extreme that they name: `lengths`: token slots at and above a response's length are padding; in every rollout group some response has all 512.
All inputs are finite; a program needn't handle non-finite values.
Results may differ from the reference program's by a relative error of at most 0.009.
The reference program's roundings to bfloat16 on the way (of `dout`, `probs_b` and `dscores`) count: a program that leaves them out, or rounds other values in their place, can miss the bound.
Values may be sent and summed in bfloat16 or wider, within the bound.
A program may use at most 128 MiB of HBM per device.

```python
import math
import jax
import jax.numpy as jnp
import numpy as np
from jax import lax

D = 4096
HEADS = 16
KV_HEADS = 4
HEAD_DIM = 128
RLEN = 512
NADV = 8
PSHARD = 64
PROMPT = 512
RESPS = 64
GROUPS = 2
N_GRP = 2
N_PROMPT = 8


def advantage_ids(key):
    return jax.random.randint(key, (GROUPS, RESPS), 0, NADV, dtype=jnp.int32)


def draw_group_ids(key, part):
    return advantage_ids(key)


def draw_rewards(key, part):
    labels = advantage_ids(key)
    key = jax.random.fold_in(key, 11)
    first_key, second_key, third_key, fourth_key = jax.random.split(key, 4)
    rising = 1.0 + 2.0 * jnp.arange(RESPS, dtype=jnp.float32) / max(RESPS - 1, 1)
    index = jnp.arange(NADV, dtype=jnp.int32)
    failing = jax.random.randint(first_key, (GROUPS, 1), 0, NADV, dtype=jnp.int32)
    closed = (index[None, :] == failing) | (index[None, :] == (failing + NADV // 2) % NADV)
    rate = jnp.where(closed, 0.0, jax.random.uniform(second_key, (GROUPS, NADV), jnp.float32, 0.3, 0.7))
    onehot = (labels[:, :, None] == index[None, None, :]).astype(jnp.float32)
    own_rate = jnp.sum(onehot * rate[:, None, :], axis=-1)
    success = jnp.where(jax.random.uniform(third_key, (GROUPS, RESPS), jnp.float32) < own_rate, 1.0, 0.0)
    noise = 0.15 * jax.random.normal(fourth_key, (GROUPS, RESPS), jnp.float32)
    return (success + noise) * rising[None, :]


def draw_queries(key, part):
    key = jax.random.fold_in(key, 23)
    first_key = jax.random.fold_in(key, 0)
    shape = (GROUPS, RESPS, RLEN, HEADS * HEAD_DIM)
    base = jax.random.normal(first_key, shape, jnp.float32)
    return base.astype(jnp.bfloat16)


def block_scale(stream_key, extent, cuts, smallest, high):
    loudness = 1.0
    for position, parts in cuts:
        draws = jax.random.uniform(jax.random.fold_in(jax.random.fold_in(stream_key, 6), position), (parts,), jnp.float32, smallest / len(cuts), high / len(cuts))
        loudness = loudness * jnp.repeat(jnp.exp(draws), extent[position] // parts).reshape((-1,) + (1,) * (len(extent) - 1 - position))
    return loudness


def length_profile(amount, total, reach, slope):
    loads = [(1 << 20) // math.isqrt(rank ** slope) + 1 for rank in range(2, amount + 1)]
    rest, counts = total - reach - (amount - 1), [1] * (amount - 1)
    while rest > 0:
        candidates = [i for i in range(amount - 1) if counts[i] < reach]
        mass, budget = sum([loads[i] for i in candidates]), rest
        for i in candidates:
            more = min(reach - counts[i], max(1, budget * loads[i] // mass), rest)
            counts[i] = counts[i] + more
            rest = rest - more
    return np.array([reach] + counts)


def uneven_parts(rng, number_of, total, bound, skew):
    if number_of == 2:
        one = jax.random.randint(rng, (), max(1, total - bound), min(bound, total - 1) + 1)
        return jnp.stack([one, total - one])
    tallies = jnp.asarray(length_profile(number_of, total, bound, skew), jnp.int32)
    couples = (number_of - 1) // 2
    donor, sink = tallies[1:1 + 2 * couples:2], tallies[2:2 + 2 * couples:2]
    margin = jnp.minimum(donor - 1, bound - sink)
    passed = jax.random.randint(jax.random.fold_in(rng, 1), (couples,), 0, 1 << 20) % (margin + 1)
    tallies = tallies.at[1:1 + 2 * couples:2].set(donor - passed).at[2:2 + 2 * couples:2].set(sink + passed)
    return tallies[jax.random.permutation(jax.random.fold_in(rng, 2), number_of)]


def gaussian(stream_key, shape, scale, limit, cuts=(), kind=jnp.bfloat16):
    array = scale * jax.random.normal(stream_key, shape, jnp.float32)
    if cuts:
        array = array * block_scale(stream_key, shape, cuts, -0.22, 0.18)
    return jnp.clip(array, -limit, limit).astype(kind)


def setup_inputs(seed: int = 0) -> dict:
    key_of = jax.random.split(jax.random.key(seed), 10)
    return {
        "prompt_states": gaussian(key_of[0], (GROUPS, PROMPT, D), 1.0, 6.0, ((0, 2), (1, 8))),
        "response_states": gaussian(key_of[1], (GROUPS, RESPS, RLEN, D), 1.0, 6.0, ((0, 2), (1, 64))),
        "queries": draw_queries(jax.random.fold_in(key_of[9], 71), 0),
        "grad_output": gaussian(key_of[3], (GROUPS, RESPS, RLEN, HEADS * HEAD_DIM), 4.0, 24.0, ((0, 2), (1, 64))),
        "key_weight": gaussian(key_of[4], (D, KV_HEADS * HEAD_DIM), D ** -0.5, 0.09375),
        "value_weight": gaussian(key_of[5], (D, KV_HEADS * HEAD_DIM), D ** -0.5, 0.09375),
        "rewards": draw_rewards(jax.random.fold_in(key_of[9], 71), 0),
        "lengths": jax.vmap(lambda own: uneven_parts(own, RESPS, RESPS * RLEN * 3 // 5, RLEN, 2))(jax.random.split(key_of[7], GROUPS)).reshape((GROUPS, RESPS)).astype(jnp.int32),
        "group_ids": draw_group_ids(jax.random.fold_in(key_of[9], 71), 0),
    }


THETA = 1000000.0
EPS = 1e-06

def rotary_tables(positions, half):
    steps = jnp.arange(half, dtype=jnp.float32)
    freq = THETA ** (-2.0 * steps / (2.0 * half))
    angle = positions.astype(jnp.float32)[:, None] * freq[None, :]
    return (jnp.cos(angle)[:, None, :], jnp.sin(angle)[:, None, :])

def finish_keys(raw, positions):
    count = raw.shape[0]
    heads = raw.reshape(count, -1, HEAD_DIM)
    factor = lax.rsqrt(lax.optimization_barrier(jnp.mean(heads * heads, axis=-1, keepdims=True)) + EPS)
    normed = heads * factor
    half = HEAD_DIM // 2
    cosine, sine = rotary_tables(positions, half)
    first = normed[..., :half]
    second = normed[..., half:]
    turned = jnp.concatenate([first * cosine - second * sine, second * cosine + first * sine], axis=-1)
    return turned.reshape(count, -1)

def keys_backward(grad, raw, positions):
    count = raw.shape[0]
    heads = raw.reshape(count, -1, HEAD_DIM)
    factor = lax.rsqrt(lax.optimization_barrier(jnp.mean(heads * heads, axis=-1, keepdims=True)) + EPS)
    normed = heads * factor
    half = HEAD_DIM // 2
    cosine, sine = rotary_tables(positions, half)
    upper = grad.reshape(count, -1, HEAD_DIM)
    grad_a = upper[..., :half]
    grad_b = upper[..., half:]
    unturned = jnp.concatenate([grad_a * cosine + grad_b * sine, grad_b * cosine - grad_a * sine], axis=-1)
    inner = lax.optimization_barrier(jnp.mean(unturned * normed, axis=-1, keepdims=True))
    return (factor * (unturned - normed * inner)).reshape(count, -1)

def attend(query, dout, keys, values, row_start, prompt_len):
    rows = query.shape[0]
    total = keys.shape[0]
    kv_heads = keys.shape[1] // HEAD_DIM
    fold = query.shape[1] // keys.shape[1]
    scale = HEAD_DIM ** (-0.5)
    q_all = query.reshape(rows, kv_heads, fold, HEAD_DIM).astype(jnp.float32)
    k_all = keys.reshape(total, kv_heads, HEAD_DIM).astype(jnp.float32)
    v_all = values.reshape(total, kv_heads, HEAD_DIM).astype(jnp.float32)
    d_all = dout.reshape(rows, kv_heads, fold, HEAD_DIM).astype(jnp.float32)
    scores = jnp.einsum('rhgd,nhd->hgrn', q_all, k_all) * scale
    key_pos = jnp.arange(total, dtype=jnp.int32)
    row_pos = row_start + jnp.arange(rows, dtype=jnp.int32)
    visible = (key_pos[None, :] < prompt_len) | (key_pos[None, :] - prompt_len <= row_pos[:, None])
    scores = jnp.where(visible, scores, -jnp.inf)
    peak = lax.optimization_barrier(jnp.max(scores, axis=-1, keepdims=True))
    expo = jnp.exp(scores - peak)
    probs = expo / lax.optimization_barrier(jnp.sum(expo, axis=-1, keepdims=True))
    probs_b = probs.astype(jnp.bfloat16).astype(jnp.float32)
    attn = jnp.einsum('hgrn,nhd->rhgd', probs_b, v_all)
    delta = lax.optimization_barrier(jnp.sum(d_all * attn, axis=-1))
    dprobs = jnp.einsum('rhgd,nhd->hgrn', d_all, v_all)
    dscores = (probs * (dprobs - jnp.transpose(delta, (1, 2, 0))[..., None])).astype(jnp.bfloat16).astype(jnp.float32)
    grad_q = jnp.einsum('hgrn,nhd->rhgd', dscores, k_all) * scale
    grad_k = jnp.einsum('hgrn,rhgd->nhd', dscores, q_all) * scale
    grad_v = jnp.einsum('hgrn,rhgd->nhd', probs_b, d_all)
    return (grad_q.reshape(rows, -1).astype(jnp.bfloat16), grad_k.reshape(total, -1), grad_v.reshape(total, -1))

def from_sums(rewards, onehot, count, total, square):
    members = jnp.maximum(count, 1.0)
    mean = total / members
    spread = jnp.sqrt(jnp.maximum(square / members - mean * mean, 0.0))
    own_mean = lax.optimization_barrier(jnp.sum(onehot * mean[None, :], axis=1))
    own_spread = lax.optimization_barrier(jnp.sum(onehot * spread[None, :], axis=1))
    return (rewards - own_mean) / jnp.maximum(own_spread, 0.5)

def group_advantage(rewards, group_ids):
    onehot = (group_ids[:, None] == jnp.arange(NADV, dtype=jnp.int32)[None, :]).astype(jnp.float32)
    count = lax.optimization_barrier(jnp.sum(onehot, axis=0))
    total = lax.optimization_barrier(jnp.sum(onehot * rewards[:, None], axis=0))
    square = lax.optimization_barrier(jnp.sum(onehot * (rewards * rewards)[:, None], axis=0))
    return from_sums(rewards, onehot, count, total, square)

def reference(prompt_states, response_states, queries, grad_output, key_weight, value_weight, rewards, lengths, group_ids):
    prompt_len = PSHARD * N_PROMPT
    width = KV_HEADS * HEAD_DIM
    grad_wk = jnp.zeros((D, width), jnp.float32)
    grad_wv = jnp.zeros((D, width), jnp.float32)
    query_grads = []
    for group in range(N_GRP):
        states = prompt_states[group]
        prompt_positions = jnp.arange(prompt_len, dtype=jnp.int32)
        prompt_raw = jnp.dot(states, key_weight, preferred_element_type=jnp.float32)
        prompt_keys = finish_keys(prompt_raw, prompt_positions).astype(jnp.bfloat16)
        prompt_values = jnp.dot(states, value_weight, preferred_element_type=jnp.float32).astype(jnp.bfloat16)
        advantage = group_advantage(rewards[group], group_ids[group])

        def one_response(carry, item):
            sum_k, sum_v, acc_wk, acc_wv = carry
            own_states, query, probe, length, weight = item
            positions = prompt_len + jnp.arange(RLEN, dtype=jnp.int32)
            own_raw = jnp.dot(own_states, key_weight, preferred_element_type=jnp.float32)
            own_keys = finish_keys(own_raw, positions).astype(jnp.bfloat16)
            own_values = jnp.dot(own_states, value_weight, preferred_element_type=jnp.float32).astype(jnp.bfloat16)
            keys = jnp.concatenate([prompt_keys, own_keys], axis=0)
            values = jnp.concatenate([prompt_values, own_values], axis=0)
            live = jnp.arange(RLEN, dtype=jnp.int32) < length
            coef = jnp.where(live, weight / length.astype(jnp.float32), jnp.float32(0.0))
            dout = (probe.astype(jnp.float32) * coef[:, None]).astype(jnp.bfloat16)
            grad_q, grad_k, grad_v = attend(query, dout, keys, values, 0, prompt_len)
            own_dk = keys_backward(grad_k[prompt_len:], own_raw, positions).astype(jnp.bfloat16)
            own_dv = grad_v[prompt_len:].astype(jnp.bfloat16)
            acc_wk = acc_wk + jnp.dot(own_states.T, own_dk, preferred_element_type=jnp.float32)
            acc_wv = acc_wv + jnp.dot(own_states.T, own_dv, preferred_element_type=jnp.float32)
            return ((sum_k + grad_k[:prompt_len], sum_v + grad_v[:prompt_len], acc_wk, acc_wv), grad_q)
        start = (jnp.zeros((prompt_len, width), jnp.float32), jnp.zeros((prompt_len, width), jnp.float32), jnp.zeros((D, width), jnp.float32), jnp.zeros((D, width), jnp.float32))
        items = (response_states[group], queries[group], grad_output[group], lengths[group], advantage)
        (sum_k, sum_v, acc_wk, acc_wv), grad_q = lax.scan(one_response, start, items)
        query_grads.append(grad_q)
        prompt_dk = keys_backward(sum_k, prompt_raw, prompt_positions).astype(jnp.bfloat16)
        prompt_dv = sum_v.astype(jnp.bfloat16)
        grad_wk = grad_wk + acc_wk + jnp.dot(states.T, prompt_dk, preferred_element_type=jnp.float32)
        grad_wv = grad_wv + acc_wv + jnp.dot(states.T, prompt_dv, preferred_element_type=jnp.float32)
    return (jnp.stack(query_grads, axis=0), grad_wk, grad_wv)
```

```python
import functools
import math

import jax
import jax.numpy as jnp
import numpy as np
from jax import lax
from jax.experimental import pallas as pl
from jax.experimental.pallas import tpu as pltpu
from jax.sharding import PartitionSpec as P

HEAD_DIM = 128
KVH = 4
RLEN = 512
PLEN = 512
PSH = 64
D = 4096
NADV = 8
THETA = 1000000.0
EPS = 1e-06
SCALE = 1.0 / math.sqrt(HEAD_DIM)
EXP2_SCALE = math.log2(math.e) / math.sqrt(HEAD_DIM)

F32 = jnp.float32
BF16 = jnp.bfloat16
NT = (((1,), (1,)), ((), ()))
MESH = pl.DeviceIdType.MESH


def rotary_tables():
    half = HEAD_DIM // 2
    steps = np.arange(half, dtype=np.float32)
    freq = np.power(np.float32(THETA), np.float32(-2.0) * steps / np.float32(2.0 * half))
    positions = np.arange(PLEN + RLEN, dtype=np.float32)
    angle = (positions[:, None] * freq.astype(np.float32)[None, :]).astype(np.float64)
    cosine, sine = np.cos(angle), np.sin(angle)
    return (
        np.concatenate([cosine, cosine], axis=1).astype(np.float32),
        np.concatenate([-sine, sine], axis=1).astype(np.float32),
    )


def finish_head(raw, cosine, sine):
    factor = lax.rsqrt(jnp.mean(raw * raw, axis=-1, keepdims=True) + EPS)
    normed = raw * factor
    return normed * cosine + pltpu.roll(normed, HEAD_DIM // 2, 1) * sine


def head_backward(grad, raw, cosine, sine):
    factor = lax.rsqrt(jnp.mean(raw * raw, axis=-1, keepdims=True) + EPS)
    normed = raw * factor
    unturned = grad * cosine - pltpu.roll(grad, HEAD_DIM // 2, 1) * sine
    inner = jnp.mean(unturned * normed, axis=-1, keepdims=True)
    return factor * (unturned - normed * inner)


def kernel(
    ps_h, st_h, q_h, go_h, wk_h, wv_h, rew, lens, ids, cos_t, sin_t,
    dq_h, gk_o, gv_o,
    ps_v, st_v, q_v, d_v, w_v, dq_v, x_v, xt, praw, oraw, kv, kt, dk, dv,
    g_b, pgs, pgr, sk, sv, rk1, rv1, sk2, sv2, rk2, rv2, s3, r3, st_s, st_r,
    lsem, xloc, dqsem, xs, xr, ags, agr, sts, strr, gs, gr, pss, psr,
    k1s, k1r, v1s, v1r, k2s, k2r, v2s, v2r, x3s, x3r,
):
    grp = lax.axis_index("grp")
    pr = lax.axis_index("prompt")
    rs = lax.axis_index("resp")
    y = pr // 2
    c = pr % 2
    z = rs // 2
    xlo = rs % 2
    x = grp * 2 + xlo

    def prompt_peer(k):
        return (grp, (pr + k) % 8, rs)

    def core_peer():
        return (grp, y * 2 + (1 - c), rs)

    def y_peer(k):
        return (grp, ((y + k) % 4) * 2 + c, rs)

    def z_peer(k):
        return (grp, pr, ((z + k) % 4) * 2 + xlo)

    def x_peer(k):
        other = (x + k) % 4
        return (other // 2, pr, z * 2 + other % 2)

    def pair_peer():
        return (grp, pr, z * 2 + (1 - xlo))

    def rcopy(src, dst, send, recv, dev):
        return pltpu.make_async_remote_copy(
            src_ref=src, dst_ref=dst, send_sem=send, recv_sem=recv,
            device_id=dev, device_id_type=MESH,
        )

    loads = [
        pltpu.make_async_copy(ps_h, ps_v, lsem.at[0]),
        pltpu.make_async_copy(wk_h, w_v.at[:, pl.ds(0, 512)], lsem.at[1]),
        pltpu.make_async_copy(wv_h, w_v.at[:, pl.ds(512, 512)], lsem.at[2]),
        pltpu.make_async_copy(st_h, st_v, lsem.at[3]),
        pltpu.make_async_copy(go_h, d_v, lsem.at[4]),
        pltpu.make_async_copy(q_h, q_v, lsem.at[5]),
    ]
    for load in loads:
        load.start()

    def x_local(seg):
        cols = pl.ds(pl.multiple_of(seg * 1024 + c * 512, 512), 512)
        here = pl.ds(seg * 512, 512)
        return (
            pltpu.make_async_copy(st_h.at[:, cols], x_v.at[pl.ds(0, 512), here], xloc.at[seg]),
            pltpu.make_async_copy(ps_h.at[:, cols], x_v.at[pl.ds(1024, 64), here], xloc.at[4 + seg]),
        )

    def x_remote(seg):
        cols = pl.ds(pl.multiple_of(seg * 1024 + (1 - c) * 512, 512), 512)
        here = pl.ds(seg * 512, 512)
        return (
            rcopy(st_h.at[:, cols], x_v.at[pl.ds(512, 512), here], xs.at[seg], xr.at[seg], core_peer()),
            rcopy(ps_h.at[:, cols], x_v.at[pl.ds(1088, 64), here], xs.at[4 + seg], xr.at[4 + seg], core_peer()),
        )

    barrier = pltpu.get_barrier_semaphore()
    for k in range(1, 8):
        pl.semaphore_signal(barrier, inc=1, device_id=prompt_peer(k), device_id_type=MESH)
    for k in range(1, 4):
        pl.semaphore_signal(barrier, inc=1, device_id=z_peer(k), device_id_type=MESH)
        pl.semaphore_signal(barrier, inc=1, device_id=x_peer(k), device_id_type=MESH)
    pl.semaphore_wait(barrier, 13)

    lane = lax.broadcasted_iota(jnp.int32, (8, 128), 1)
    row = lax.broadcasted_iota(jnp.int32, (8, 128), 0)
    reward = jnp.broadcast_to(rew[...], (8, 128))
    onehot = jnp.where(lane == jnp.broadcast_to(ids[...], (8, 128)), 1.0, 0.0).astype(F32)
    st_s[0] = onehot * jnp.where(
        row == 0, 1.0, jnp.where(row == 1, reward, jnp.where(row == 2, reward * reward, 0.0))
    )

    def stat_copy(slot):
        if slot < 7:
            return rcopy(st_s.at[0], st_r.at[slot], sts.at[slot], strr.at[slot], prompt_peer(slot + 1))
        if slot < 10:
            return rcopy(st_s.at[1], st_r.at[slot], sts.at[slot], strr.at[slot], z_peer(slot - 6))
        return rcopy(st_s.at[2], st_r.at[slot], sts.at[slot], strr.at[slot], pair_peer())

    for slot in range(7):
        stat_copy(slot).start()

    loads[0].wait()
    loads[1].wait()
    loads[2].wait()

    def prompt_tile(n, carry):
        cols = pl.ds(pl.multiple_of(n * 256, 256), 256)
        praw[:, cols] = jnp.dot(ps_v[...], w_v[:, cols], preferred_element_type=F32)
        return carry

    lax.fori_loop(0, 4, prompt_tile, 0)
    prow = pl.ds(pl.multiple_of(pr * PSH, PSH), PSH)
    pcos, psin = cos_t[prow, :], sin_t[prow, :]
    for h in range(KVH):
        cols = pl.ds(h * 128, 128)
        kv[prow, cols] = finish_head(praw[:, cols], pcos, psin).astype(BF16)
    kv[prow, pl.ds(512, 512)] = praw[:, pl.ds(512, 512)].astype(BF16)

    def gather(k):
        return rcopy(kv.at[prow], kv.at[prow], ags.at[k - 1], agr.at[k - 1], prompt_peer(k))

    def gathered(k):
        theirs = pl.ds(pl.multiple_of(((pr + 8 - k) % 8) * PSH, PSH), PSH)
        return rcopy(kv.at[theirs], kv.at[theirs], ags.at[k - 1], agr.at[k - 1], prompt_peer(k))

    for k in range(1, 8):
        gather(k).start()
    for seg in range(4):
        for copy in x_remote(seg):
            copy.start()

    for slot in range(7):
        stat_copy(slot).wait_recv()
    st_s[1] = st_s[0] + (
        ((st_r[0] + st_r[1]) + (st_r[2] + st_r[3])) + ((st_r[4] + st_r[5]) + st_r[6])
    )
    for slot in range(7, 10):
        stat_copy(slot).start()

    loads[3].wait()
    for seg in range(4):
        for copy in x_local(seg):
            copy.start()

    def own_tile(n, carry):
        cols = pl.ds(pl.multiple_of(n * 256, 256), 256)
        oraw[:, cols] = jnp.dot(st_v[...], w_v[:, cols], preferred_element_type=F32)
        return carry

    lax.fori_loop(0, 4, own_tile, 0)

    for slot in range(7, 10):
        stat_copy(slot).wait_recv()
    st_s[2] = (st_s[1] + st_r[7]) + (st_r[8] + st_r[9])
    stat_copy(10).start()

    own = pl.ds(PLEN, RLEN)
    ocos, osin = cos_t.at[own], sin_t.at[own]

    def own_keys(h, carry):
        cols = pl.ds(pl.multiple_of(h * 128, 128), 128)
        kv[own, cols] = finish_head(oraw[:, cols], ocos[...], osin[...]).astype(BF16)
        return carry

    lax.fori_loop(0, KVH, own_keys, 0)
    kv[own, pl.ds(512, 512)] = oraw[:, pl.ds(512, 512)].astype(BF16)

    for seg in range(4):
        for copy in x_local(seg):
            copy.wait()
        for copy in x_remote(seg):
            copy.wait_recv()

    def turn(n, carry):
        cols = pl.ds(pl.multiple_of(n * 256, 256), 256)
        xt[cols, :] = x_v[:, cols].T
        return carry

    lax.fori_loop(0, 8, turn, 0)

    stat_copy(10).wait_recv()
    sums = st_s[2] + st_r[10]
    count, total, square = sums[0:1], sums[1:2], sums[2:3]
    members = jnp.maximum(count, 1.0)
    mean = total / members
    spread = jnp.sqrt(jnp.maximum(square / members - mean * mean, 0.0))
    mine = onehot[0:1]
    own_mean = jnp.sum(mine * mean, axis=1, keepdims=True)
    own_spread = jnp.sum(mine * spread, axis=1, keepdims=True)
    advantage = (rew[...] - own_mean) / jnp.maximum(own_spread, 0.5)
    weight = advantage / lens[...].astype(F32)
    token = lax.broadcasted_iota(jnp.int32, (RLEN, 128), 0)
    live = token < jnp.broadcast_to(lens[...], (RLEN, 128))
    coef = jnp.where(live, jnp.broadcast_to(weight, (RLEN, 128)), 0.0)
    loads[4].wait()
    for n in range(16):
        cols = pl.ds(n * 128, 128)
        d_v[:, cols] = (d_v[:, cols].astype(F32) * coef).astype(BF16)
    loads[5].wait()
    for k in range(1, 8):
        gathered(k).wait_recv()

    def attend(h, b):
        count = PLEN + 128 * (b + 1)
        rows = pl.ds(b * 128, 128)
        keys = kv[pl.ds(0, count), pl.ds(pl.multiple_of(h * 128, 128), 128)]
        vals = kv[pl.ds(0, count), pl.ds(pl.multiple_of(512 + h * 128, 128), 128)]
        cols = [pl.ds(pl.multiple_of((h * 4 + j) * 128, 128), 128) for j in range(4)]
        q = jnp.concatenate([q_v[rows, cc] for cc in cols], axis=0)
        do = jnp.concatenate([d_v[rows, cc] for cc in cols], axis=0)
        s = lax.dot_general(keys, q, NT, preferred_element_type=F32)
        key = lax.broadcasted_iota(jnp.int32, (128, 512), 0)
        query = lax.broadcasted_iota(jnp.int32, (128, 512), 1) % 128
        s = jnp.concatenate(
            [s[: count - 128], jnp.where(key <= query, s[count - 128 :], -jnp.inf)], axis=0
        )
        peak = jnp.max(s, axis=0, keepdims=True)
        e = jnp.exp2((s - peak) * EXP2_SCALE)
        p = e * (1.0 / jnp.sum(e, axis=0, keepdims=True))
        dp = lax.dot_general(vals, do, NT, preferred_element_type=F32)
        delta = jnp.sum(p * dp, axis=0, keepdims=True)
        ds = (p * (dp - delta)).astype(BF16)
        gv = jnp.dot(p.astype(BF16), do, preferred_element_type=F32)
        gk = jnp.dot(ds, q, preferred_element_type=F32)
        if b == 3:
            dv[...] = gv
            dk[...] = gk
        else:
            dv[pl.ds(0, count)] += gv
            dk[pl.ds(0, count)] += gk
        dq = (jnp.dot(kt[:, pl.ds(0, count)], ds, preferred_element_type=F32) * SCALE).T.astype(BF16)
        for j, cc in enumerate(cols):
            dq_v[rows, cc] = dq[j * 128 : (j + 1) * 128]

    def g_copy(h, part):
        mine = (pl.ds(0, 512), pl.ds(1024, 64))[part]
        theirs = (pl.ds(512, 512), pl.ds(1088, 64))[part]
        return rcopy(g_b.at[h, mine], g_b.at[h, theirs], gs.at[h, part], gr.at[h, part], core_peer())

    def pg_copy(h, k):
        return rcopy(pgs.at[h, (pr + k) % 8], pgr.at[h, k - 1], pss.at[h, k - 1], psr.at[h, k - 1], prompt_peer(k))

    def k1_copy(h, k):
        return rcopy(sk.at[h, (y + k) % 4], rk1.at[h, k - 1], k1s.at[h, k - 1], k1r.at[h, k - 1], y_peer(k))

    def v1_copy(h, k):
        return rcopy(sv.at[h, (z + k) % 4], rv1.at[h, k - 1], v1s.at[h, k - 1], v1r.at[h, k - 1], z_peer(k))

    def k2_copy(h, k):
        return rcopy(sk2.at[h, (z + k) % 4], rk2.at[h, k - 1], k2s.at[h, k - 1], k2r.at[h, k - 1], z_peer(k))

    def v2_copy(h, k):
        return rcopy(sv2.at[h, (y + k) % 4], rv2.at[h, k - 1], v2s.at[h, k - 1], v2r.at[h, k - 1], y_peer(k))

    def x3_copy(h, k):
        return rcopy(s3.at[h, (x + k) % 2], r3.at[h, k - 1], x3s.at[h, k - 1], x3r.at[h, k - 1], x_peer(k))

    def dq_copy(h):
        cols = pl.ds(pl.multiple_of(h * 512, 512), 512)
        return pltpu.make_async_copy(dq_v.at[:, cols], dq_h.at[:, cols], dqsem.at[h])

    def finish(h):
        cols = pl.ds(pl.multiple_of(h * 128, 128), 128)
        for t in range(8):
            pgs[h, t, :, pl.ds(0, 128)] = (dk[pl.ds(t * 64, 64)] * SCALE).astype(BF16)
            pgs[h, t, :, pl.ds(128, 128)] = dv[pl.ds(t * 64, 64)].astype(BF16)
        for k in range(1, 8):
            pg_copy(h, k).start()
        g_b[h, pl.ds(0, 512), pl.ds(0, 128)] = head_backward(
            dk[own] * SCALE, oraw[:, cols], ocos[...], osin[...]
        ).astype(BF16)
        g_b[h, pl.ds(0, 512), pl.ds(128, 128)] = dv[own].astype(BF16)
        g_copy(h, 0).start()
        dq_copy(h).start()

    def prompt_rows(h):
        cols = pl.ds(pl.multiple_of(h * 128, 128), 128)
        total = pgs[h, pr].astype(F32)
        for k in range(1, 8):
            pg_copy(h, k).wait_recv()
            total = total + pgr[h, k - 1].astype(F32)
        g_b[h, pl.ds(1024, 64), pl.ds(0, 128)] = head_backward(
            total[:, :128], praw[:, cols], cos_t[prow, :], sin_t[prow, :]
        ).astype(BF16)
        g_b[h, pl.ds(1024, 64), pl.ds(128, 128)] = total[:, 128:].astype(BF16)
        g_copy(h, 1).start()

    def contract(h):
        g_copy(h, 0).wait_recv()
        g_copy(h, 1).wait_recv()

        def segment(seg, carry):
            out = jnp.dot(
                xt[pl.ds(pl.multiple_of(seg * 512, 512), 512), :], g_b[h], preferred_element_type=F32
            ).astype(BF16)
            sk[h, seg] = out[:, :128]
            for t in range(4):
                sv[h, t, seg] = out[t * 128 : (t + 1) * 128, 128:]
            return carry

        lax.fori_loop(0, 4, segment, 0)
        for k in range(1, 4):
            k1_copy(h, k).start()
            v1_copy(h, k).start()

    def second(h):
        for k in range(1, 4):
            k1_copy(h, k).wait_recv()
            v1_copy(h, k).wait_recv()
        total = (sk[h, y].astype(F32) + rk1[h, 0].astype(F32)) + (
            rk1[h, 1].astype(F32) + rk1[h, 2].astype(F32)
        )
        for t in range(4):
            sk2[h, t] = total[t * 128 : (t + 1) * 128].astype(BF16)
        sv2[h] = (
            (sv[h, z].astype(F32) + rv1[h, 0].astype(F32))
            + (rv1[h, 1].astype(F32) + rv1[h, 2].astype(F32))
        ).astype(BF16)
        for k in range(1, 4):
            k2_copy(h, k).start()
            v2_copy(h, k).start()

    def third(h):
        for k in range(1, 4):
            k2_copy(h, k).wait_recv()
            v2_copy(h, k).wait_recv()
        for part, (own2, got) in enumerate(((sk2[h, z], rk2), (sv2[h, y], rv2))):
            total = (own2.astype(F32) + got[h, 0].astype(F32)) + (
                got[h, 1].astype(F32) + got[h, 2].astype(F32)
            )
            s3[h, 0, :, pl.ds(part * 128, 128)] = total[:64].astype(BF16)
            s3[h, 1, :, pl.ds(part * 128, 128)] = total[64:].astype(BF16)
        for k in range(1, 4):
            x3_copy(h, k).start()

    def output(h):
        for k in range(1, 4):
            x3_copy(h, k).wait_recv()
        total = (s3[h, xlo].astype(F32) + r3[h, 0].astype(F32)) + (
            r3[h, 1].astype(F32) + r3[h, 2].astype(F32)
        )
        cols = pl.ds(pl.multiple_of(h * 128, 128), 128)
        gk_o[:, cols] = total[:, :128]
        gv_o[:, cols] = total[:, 128:]

    def head(h, carry):
        kt[...] = kv[:, pl.ds(pl.multiple_of(h * 128, 128), 128)].T
        attend(h, 3)

        @pl.when(h > 0)
        def _():
            prompt_rows(h - 1)

        @pl.when(h > 1)
        def _():
            second(h - 2)

        attend(h, 2)

        @pl.when(h > 0)
        def _():
            contract(h - 1)

        attend(h, 1)

        @pl.when(h > 1)
        def _():
            third(h - 2)

        attend(h, 0)
        finish(h)
        return carry

    lax.fori_loop(0, KVH, head, 0)
    second(2)
    prompt_rows(3)
    contract(3)
    third(2)
    second(3)
    third(3)

    def wrap(h, carry):
        output(h)
        dq_copy(h).wait()
        for part in range(2):
            g_copy(h, part).wait_send()
        for k in range(1, 8):
            pg_copy(h, k).wait_send()
        for k in range(1, 4):
            for copy in (k1_copy, v1_copy, k2_copy, v2_copy, x3_copy):
                copy(h, k).wait_send()
        return carry

    lax.fori_loop(0, KVH, wrap, 0)
    for slot in range(11):
        stat_copy(slot).wait_send()
    for k in range(1, 8):
        gather(k).wait_send()
    for seg in range(4):
        for copy in x_remote(seg):
            copy.wait_send()


def body(
    prompt_states, response_states, queries, grad_output, key_weight, value_weight,
    rewards, lengths, group_ids,
):
    cosine, sine = rotary_tables()
    hbm = pl.BlockSpec(memory_space=pl.ANY)
    vmem = pl.BlockSpec(memory_space=pltpu.VMEM)
    dma = pltpu.SemaphoreType.DMA
    scratch = [
        pltpu.VMEM((PSH, D), BF16),
        pltpu.VMEM((RLEN, D), BF16),
        pltpu.VMEM((RLEN, 2048), BF16),
        pltpu.VMEM((RLEN, 2048), BF16),
        pltpu.VMEM((D, 1024), BF16),
        pltpu.VMEM((RLEN, 2048), BF16),
        pltpu.VMEM((1152, 2048), BF16),
        pltpu.VMEM((2048, 1152), BF16),
        pltpu.VMEM((PSH, 1024), F32),
        pltpu.VMEM((RLEN, 1024), F32),
        pltpu.VMEM((1024, 1024), BF16),
        pltpu.VMEM((128, 1024), BF16),
        pltpu.VMEM((1024, 128), F32),
        pltpu.VMEM((1024, 128), F32),
        pltpu.VMEM((KVH, 1152, 256), BF16),
        pltpu.VMEM((KVH, 8, PSH, 256), BF16),
        pltpu.VMEM((KVH, 7, PSH, 256), BF16),
        pltpu.VMEM((KVH, 4, 512, 128), BF16),
        pltpu.VMEM((KVH, 4, 4, 128, 128), BF16),
        pltpu.VMEM((KVH, 3, 512, 128), BF16),
        pltpu.VMEM((KVH, 3, 4, 128, 128), BF16),
        pltpu.VMEM((KVH, 4, 128, 128), BF16),
        pltpu.VMEM((KVH, 4, 128, 128), BF16),
        pltpu.VMEM((KVH, 3, 128, 128), BF16),
        pltpu.VMEM((KVH, 3, 128, 128), BF16),
        pltpu.VMEM((KVH, 2, 64, 256), BF16),
        pltpu.VMEM((KVH, 3, 64, 256), BF16),
        pltpu.VMEM((3, 8, 128), F32),
        pltpu.VMEM((11, 8, 128), F32),
        dma((6,)), dma((8,)), dma((KVH,)), dma((8,)), dma((8,)), dma((7,)), dma((7,)),
        dma((11,)), dma((11,)), dma((KVH, 2)), dma((KVH, 2)), dma((KVH, 7)), dma((KVH, 7)),
    ] + [dma((KVH, 3)) for _ in range(10)]
    dq, gk, gv = pl.pallas_call(
        kernel,
        out_shape=(
            jax.ShapeDtypeStruct((RLEN, 2048), BF16),
            jax.ShapeDtypeStruct((64, 512), F32),
            jax.ShapeDtypeStruct((64, 512), F32),
        ),
        in_specs=[hbm] * 6 + [vmem] * 5,
        out_specs=(hbm, vmem, vmem),
        scratch_shapes=scratch,
        compiler_params=pltpu.CompilerParams(
            collective_id=0, has_side_effects=True, vmem_limit_bytes=60 * 2**20
        ),
        name="surrogate_grad",
    )(
        prompt_states[0], response_states[0, 0], queries[0, 0], grad_output[0, 0],
        key_weight, value_weight, rewards, lengths, group_ids,
        jnp.asarray(cosine), jnp.asarray(sine),
    )
    return dq[None, None], gk, gv


def solution(mesh):
    row = P("grp", ("prompt", "resp"))
    tokens = P("grp", ("prompt", "resp"), None, None)
    return jax.shard_map(
        body,
        mesh=mesh,
        in_specs=(P("grp", "prompt", None), tokens, tokens, tokens, P(), P(), row, row, row),
        out_specs=(tokens, P(("prompt", "resp"), None), P(("prompt", "resp"), None)),
        check_vma=False,
    )
```

```python
import functools
import math

import jax
import jax.numpy as jnp
import numpy as np
from jax import lax
from jax.experimental import pallas as pl
from jax.experimental.pallas import tpu as pltpu
from jax.sharding import PartitionSpec as P

HEAD_DIM = 128
KVH = 4
RLEN = 512
PLEN = 512
PSH = 64
D = 4096
NADV = 8
THETA = 1000000.0
EPS = 1e-06
SCALE = 1.0 / math.sqrt(HEAD_DIM)
EXP2_SCALE = math.log2(math.e) / math.sqrt(HEAD_DIM)

F32 = jnp.float32
BF16 = jnp.bfloat16
NT = (((1,), (1,)), ((), ()))
MESH = pl.DeviceIdType.MESH


def rotary_tables():
    half = HEAD_DIM // 2
    steps = np.arange(half, dtype=np.float32)
    freq = np.power(np.float32(THETA), np.float32(-2.0) * steps / np.float32(2.0 * half))
    positions = np.arange(PLEN + RLEN, dtype=np.float32)
    angle = (positions[:, None] * freq.astype(np.float32)[None, :]).astype(np.float64)
    cosine, sine = np.cos(angle), np.sin(angle)
    return (
        np.concatenate([cosine, cosine], axis=1).astype(np.float32),
        np.concatenate([-sine, sine], axis=1).astype(np.float32),
    )


def finish_head(raw, cosine, sine):
    factor = lax.rsqrt(jnp.mean(raw * raw, axis=-1, keepdims=True) + EPS)
    normed = raw * factor
    return normed * cosine + pltpu.roll(normed, HEAD_DIM // 2, 1) * sine


def head_backward(grad, raw, cosine, sine):
    factor = lax.rsqrt(jnp.mean(raw * raw, axis=-1, keepdims=True) + EPS)
    normed = raw * factor
    unturned = grad * cosine - pltpu.roll(grad, HEAD_DIM // 2, 1) * sine
    inner = jnp.mean(unturned * normed, axis=-1, keepdims=True)
    return factor * (unturned - normed * inner)


def kernel(
    ps_h, st_h, q_h, go_h, wk_h, wv_h, rew, lens, ids, cos_t, sin_t,
    dq_h, gk_o, gv_o,
    ps_v, st_v, q_v, d_v, w_v, dq_v, x_v, xt, praw, oraw, kv, kt, dk, dv,
    g_b, pgs, pgr, sa, sb, sc, ra1, rb1, rc1, sa2, sb2, sc2, ra2, rb2, rc2, s3, r3, c3, rc3,
    st_s, st_r,
    lsem, dqsem, xs, xr, ags, agr, sts, strr, gs, gr, pss, psr, c3s, c3r,
    a1s, a1r, b1s, b1r, c1s, c1r, a2s, a2r, b2s, b2r, c2s, c2r, x3s, x3r,
):
    grp = lax.axis_index("grp")
    pr = lax.axis_index("prompt")
    rs = lax.axis_index("resp")
    y = pr // 2
    c = pr % 2
    z = rs // 2
    xlo = rs % 2
    x = grp * 2 + xlo

    def prompt_peer(k):
        return (grp, (pr + k) % 8, rs)

    def core_peer():
        return (grp, y * 2 + (1 - c), rs)

    def y_peer(k):
        return (grp, ((y + k) % 4) * 2 + c, rs)

    def z_peer(k):
        return (grp, pr, ((z + k) % 4) * 2 + xlo)

    def x_peer(k):
        other = (x + k) % 4
        return (other // 2, pr, z * 2 + other % 2)

    def cross_peer(k):
        return (1 - grp, ((y + k) % 4) * 2 + c, rs)

    def pair_peer():
        return (grp, pr, z * 2 + (1 - xlo))

    def rcopy(src, dst, send, recv, dev):
        return pltpu.make_async_remote_copy(
            src_ref=src, dst_ref=dst, send_sem=send, recv_sem=recv,
            device_id=dev, device_id_type=MESH,
        )

    loads = [
        pltpu.make_async_copy(ps_h, ps_v, lsem.at[0]),
        pltpu.make_async_copy(wk_h, w_v.at[:, pl.ds(0, 512)], lsem.at[1]),
        pltpu.make_async_copy(wv_h, w_v.at[:, pl.ds(512, 512)], lsem.at[2]),
        pltpu.make_async_copy(st_h, st_v, lsem.at[3]),
        pltpu.make_async_copy(go_h, d_v, lsem.at[4]),
        pltpu.make_async_copy(q_h, q_v, lsem.at[5]),
    ]
    for load in loads[:3]:
        load.start()

    def x_remote(seg):
        cols = pl.ds(pl.multiple_of(seg * 1024 + (1 - c) * 512, 512), 512)
        here = pl.ds(seg * 512, 512)
        return (
            rcopy(st_v.at[:, cols], x_v.at[pl.ds(0, 512), here], xs.at[seg], xr.at[seg], core_peer()),
            rcopy(ps_v.at[:, cols], x_v.at[pl.ds(512, 64), here], xs.at[4 + seg], xr.at[4 + seg], core_peer()),
        )

    barrier = pltpu.get_barrier_semaphore()
    for k in range(1, 8):
        pl.semaphore_signal(barrier, inc=1, device_id=prompt_peer(k), device_id_type=MESH)
    for k in range(1, 4):
        pl.semaphore_signal(barrier, inc=1, device_id=z_peer(k), device_id_type=MESH)
        pl.semaphore_signal(barrier, inc=1, device_id=x_peer(k), device_id_type=MESH)
        pl.semaphore_signal(barrier, inc=1, device_id=cross_peer(k), device_id_type=MESH)
    pl.semaphore_wait(barrier, 16)

    lane = lax.broadcasted_iota(jnp.int32, (8, 128), 1)
    row = lax.broadcasted_iota(jnp.int32, (8, 128), 0)
    reward = jnp.broadcast_to(rew[...], (8, 128))
    onehot = jnp.where(lane == jnp.broadcast_to(ids[...], (8, 128)), 1.0, 0.0).astype(F32)
    st_s[0] = onehot * jnp.where(
        row == 0, 1.0, jnp.where(row == 1, reward, jnp.where(row == 2, reward * reward, 0.0))
    )

    def stat_copy(slot):
        if slot < 7:
            return rcopy(st_s.at[0], st_r.at[slot], sts.at[slot], strr.at[slot], prompt_peer(slot + 1))
        if slot < 10:
            return rcopy(st_s.at[1], st_r.at[slot], sts.at[slot], strr.at[slot], z_peer(slot - 6))
        return rcopy(st_s.at[2], st_r.at[slot], sts.at[slot], strr.at[slot], pair_peer())

    for slot in range(7):
        stat_copy(slot).start()

    loads[0].wait()
    loads[1].wait()
    loads[2].wait()
    for load in loads[3:]:
        load.start()

    def prompt_tile(n, carry):
        cols = pl.ds(pl.multiple_of(n * 256, 256), 256)
        praw[:, cols] = jnp.dot(ps_v[...], w_v[:, cols], preferred_element_type=F32)
        return carry

    lax.fori_loop(0, 4, prompt_tile, 0)
    prow = pl.ds(pl.multiple_of(pr * PSH, PSH), PSH)
    pcos, psin = cos_t[prow, :], sin_t[prow, :]
    for h in range(KVH):
        cols = pl.ds(h * 128, 128)
        kv[prow, cols] = finish_head(praw[:, cols], pcos, psin).astype(BF16)
    kv[prow, pl.ds(512, 512)] = praw[:, pl.ds(512, 512)].astype(BF16)

    def gather(k):
        return rcopy(kv.at[prow], kv.at[prow], ags.at[k - 1], agr.at[k - 1], prompt_peer(k))

    def gathered(k):
        theirs = pl.ds(pl.multiple_of(((pr + 8 - k) % 8) * PSH, PSH), PSH)
        return rcopy(kv.at[theirs], kv.at[theirs], ags.at[k - 1], agr.at[k - 1], prompt_peer(k))

    for k in range(1, 8):
        gather(k).start()

    for slot in range(7):
        stat_copy(slot).wait_recv()
    st_s[1] = st_s[0] + (
        ((st_r[0] + st_r[1]) + (st_r[2] + st_r[3])) + ((st_r[4] + st_r[5]) + st_r[6])
    )
    for slot in range(7, 10):
        stat_copy(slot).start()

    loads[3].wait()
    for seg in range(4):
        for copy in x_remote(seg):
            copy.start()

    def own_tile(n, carry):
        cols = pl.ds(pl.multiple_of(n * 256, 256), 256)
        oraw[:, cols] = jnp.dot(st_v[...], w_v[:, cols], preferred_element_type=F32)
        for t in range(2):
            here = pl.ds(pl.multiple_of(n * 512 + t * 256, 256), 256)
            mine = pl.ds(pl.multiple_of(n * 1024 + c * 512 + t * 256, 256), 256)
            xt[here, pl.ds(0, 512)] = st_v[:, mine].T
        return carry

    lax.fori_loop(0, 4, own_tile, 0)

    for slot in range(7, 10):
        stat_copy(slot).wait_recv()
    st_s[2] = (st_s[1] + st_r[7]) + (st_r[8] + st_r[9])
    stat_copy(10).start()

    own = pl.ds(PLEN, RLEN)
    ocos, osin = cos_t.at[own], sin_t.at[own]

    def own_keys(h, carry):
        cols = pl.ds(pl.multiple_of(h * 128, 128), 128)
        kv[own, cols] = finish_head(oraw[:, cols], ocos[...], osin[...]).astype(BF16)
        return carry

    lax.fori_loop(0, KVH, own_keys, 0)
    kv[own, pl.ds(512, 512)] = oraw[:, pl.ds(512, 512)].astype(BF16)

    for seg in range(4):
        for copy in x_remote(seg):
            copy.wait_recv()

    def turn(n, carry):
        here = pl.ds(pl.multiple_of(n * 256, 256), 256)
        mine = pl.ds(pl.multiple_of((n // 2) * 1024 + c * 512 + (n % 2) * 256, 256), 256)
        xt[here, pl.ds(512, 512)] = x_v[pl.ds(0, 512), here].T
        xt[here, pl.ds(1024, 128)] = jnp.concatenate([ps_v[:, mine], x_v[pl.ds(512, 64), here]], axis=0).T
        return carry

    lax.fori_loop(0, 8, turn, 0)

    stat_copy(10).wait_recv()
    sums = st_s[2] + st_r[10]
    count, total, square = sums[0:1], sums[1:2], sums[2:3]
    members = jnp.maximum(count, 1.0)
    mean = total / members
    spread = jnp.sqrt(jnp.maximum(square / members - mean * mean, 0.0))
    mine = onehot[0:1]
    own_mean = jnp.sum(mine * mean, axis=1, keepdims=True)
    own_spread = jnp.sum(mine * spread, axis=1, keepdims=True)
    advantage = (rew[...] - own_mean) / jnp.maximum(own_spread, 0.5)
    weight = advantage / lens[...].astype(F32)
    token = lax.broadcasted_iota(jnp.int32, (RLEN, 128), 0)
    live = token < jnp.broadcast_to(lens[...], (RLEN, 128))
    coef = jnp.where(live, jnp.broadcast_to(weight, (RLEN, 128)), 0.0)
    loads[4].wait()
    for n in range(16):
        cols = pl.ds(n * 128, 128)
        d_v[:, cols] = (d_v[:, cols].astype(F32) * coef).astype(BF16)
    loads[5].wait()
    for k in range(1, 8):
        gathered(k).wait_recv()

    def attend(h, b):
        count = PLEN + 128 * (b + 1)
        rows = pl.ds(b * 128, 128)
        keys = kv[pl.ds(0, count), pl.ds(pl.multiple_of(h * 128, 128), 128)]
        vals = kv[pl.ds(0, count), pl.ds(pl.multiple_of(512 + h * 128, 128), 128)]
        cols = [pl.ds(pl.multiple_of((h * 4 + j) * 128, 128), 128) for j in range(4)]
        q = jnp.concatenate([q_v[rows, cc] for cc in cols], axis=0)
        do = jnp.concatenate([d_v[rows, cc] for cc in cols], axis=0)
        s = lax.dot_general(keys, q, NT, preferred_element_type=F32)
        key = lax.broadcasted_iota(jnp.int32, (128, 512), 0)
        query = lax.broadcasted_iota(jnp.int32, (128, 512), 1) % 128
        s = jnp.concatenate(
            [s[: count - 128], jnp.where(key <= query, s[count - 128 :], -jnp.inf)], axis=0
        )
        peak = jnp.max(s, axis=0, keepdims=True)
        e = jnp.exp2((s - peak) * EXP2_SCALE)
        p = e * (1.0 / jnp.sum(e, axis=0, keepdims=True))
        dp = lax.dot_general(vals, do, NT, preferred_element_type=F32)
        delta = jnp.sum(p * dp, axis=0, keepdims=True)
        ds = (p * (dp - delta)).astype(BF16)
        gv = jnp.dot(p.astype(BF16), do, preferred_element_type=F32)
        gk = jnp.dot(ds, q, preferred_element_type=F32)
        if b == 3:
            dv[...] = gv
            dk[...] = gk
        else:
            dv[pl.ds(0, count)] += gv
            dk[pl.ds(0, count)] += gk
        dq = (jnp.dot(kt[:, pl.ds(0, count)], ds, preferred_element_type=F32) * SCALE).T.astype(BF16)
        for j, cc in enumerate(cols):
            dq_v[rows, cc] = dq[j * 128 : (j + 1) * 128]

    def g_copy(h, part):
        mine = (pl.ds(0, 512), pl.ds(1024, 64))[part]
        theirs = (pl.ds(512, 512), pl.ds(1088, 64))[part]
        return rcopy(g_b.at[h, mine], g_b.at[h, theirs], gs.at[h, part], gr.at[h, part], core_peer())

    def pg_copy(h, k):
        return rcopy(pgs.at[h, (pr + k) % 8], pgr.at[h, k - 1], pss.at[h, k - 1], psr.at[h, k - 1], prompt_peer(k))

    def a1_copy(h, k):
        return rcopy(sa.at[h, (y + k) % 4], ra1.at[h, k - 1], a1s.at[h, k - 1], a1r.at[h, k - 1], y_peer(k))

    def b1_copy(h, k):
        return rcopy(sb.at[h, (z + k) % 4], rb1.at[h, k - 1], b1s.at[h, k - 1], b1r.at[h, k - 1], z_peer(k))

    def c1_copy(h, k):
        return rcopy(sc.at[h, (x + k) % 4], rc1.at[h, k - 1], c1s.at[h, k - 1], c1r.at[h, k - 1], x_peer(k))

    def a2_copy(h, k):
        return rcopy(sa2.at[h, (z + k) % 4], ra2.at[h, k - 1], a2s.at[h, k - 1], a2r.at[h, k - 1], z_peer(k))

    def b2_copy(h, k):
        return rcopy(sb2.at[h, (y + k) % 4], rb2.at[h, k - 1], b2s.at[h, k - 1], b2r.at[h, k - 1], y_peer(k))

    def c2_copy(h, k):
        return rcopy(sc2.at[h, (z + k) % 4], rc2.at[h, k - 1], c2s.at[h, k - 1], c2r.at[h, k - 1], z_peer(k))

    def x3_copy(h, k):
        return rcopy(s3.at[h, (x + k) % 2], r3.at[h, k - 1], x3s.at[h, k - 1], x3r.at[h, k - 1], x_peer(k))

    def c3_copy(h, slot):
        k = slot + 1 if slot < 3 else slot - 3
        dev = y_peer(k) if slot < 3 else cross_peer(k)
        return rcopy(c3.at[h, (y + k) % 4], rc3.at[h, slot], c3s.at[h, slot], c3r.at[h, slot], dev)

    def dq_copy(h):
        cols = pl.ds(pl.multiple_of(h * 512, 512), 512)
        return pltpu.make_async_copy(dq_v.at[:, cols], dq_h.at[:, cols], dqsem.at[h])

    def finish(h):
        cols = pl.ds(pl.multiple_of(h * 128, 128), 128)
        for t in range(8):
            pgs[h, t, :, pl.ds(0, 128)] = (dk[pl.ds(t * 64, 64)] * SCALE).astype(BF16)
            pgs[h, t, :, pl.ds(128, 128)] = dv[pl.ds(t * 64, 64)].astype(BF16)
        for k in range(1, 8):
            pg_copy(h, k).start()
        g_b[h, pl.ds(0, 512), pl.ds(0, 128)] = head_backward(
            dk[own] * SCALE, oraw[:, cols], ocos[...], osin[...]
        ).astype(BF16)
        g_b[h, pl.ds(0, 512), pl.ds(128, 128)] = dv[own].astype(BF16)
        g_copy(h, 0).start()
        dq_copy(h).start()

    def prompt_rows(h):
        cols = pl.ds(pl.multiple_of(h * 128, 128), 128)
        total = pgs[h, pr].astype(F32)
        for k in range(1, 8):
            pg_copy(h, k).wait_recv()
            total = total + pgr[h, k - 1].astype(F32)
        g_b[h, pl.ds(1024, 64), pl.ds(0, 128)] = head_backward(
            total[:, :128], praw[:, cols], cos_t[prow, :], sin_t[prow, :]
        ).astype(BF16)
        g_b[h, pl.ds(1024, 64), pl.ds(128, 128)] = total[:, 128:].astype(BF16)
        g_copy(h, 1).start()

    def contract(h):
        g_copy(h, 0).wait_recv()
        g_copy(h, 1).wait_recv()

        def segment(i, carry):
            seg = (y + 1 + i) % 4
            out = jnp.dot(
                xt[pl.ds(pl.multiple_of(seg * 512, 512), 512), :], g_b[h], preferred_element_type=F32
            ).astype(BF16)
            for zz in range(4):
                for xx in range(2):
                    at = zz * 128 + xx * 64
                    sa[h, seg, zz, xx] = out[at : at + 48, :128]
                    sb[h, zz, seg, xx] = out[at : at + 48, 128:]
                    sc[h, xx, zz, seg] = out[at + 48 : at + 64, :128]
                    sc[h, xx + 2, zz, seg] = out[at + 48 : at + 64, 128:]

            @pl.when(i < 3)
            def _():
                a1_copy(h, i + 1).start()

            return carry

        lax.fori_loop(0, 4, segment, 0)
        for k in range(1, 4):
            b1_copy(h, k).start()
            c1_copy(h, k).start()

    def four(own_block, got, h):
        return (own_block.astype(F32) + got[h, 0].astype(F32)) + (
            got[h, 1].astype(F32) + got[h, 2].astype(F32)
        )

    def second(h):
        for k in range(1, 4):
            c1_copy(h, k).wait_recv()
        sc2[h] = four(sc[h, x], rc1, h).astype(BF16)
        for k in range(1, 4):
            c2_copy(h, k).start()
        for k in range(1, 4):
            a1_copy(h, k).wait_recv()
        sa2[h] = four(sa[h, y], ra1, h).astype(BF16)
        for k in range(1, 4):
            a2_copy(h, k).start()
        for k in range(1, 4):
            b1_copy(h, k).wait_recv()
        sb2[h] = four(sb[h, z], rb1, h).astype(BF16)
        for k in range(1, 4):
            b2_copy(h, k).start()

    def third(h):
        for k in range(1, 4):
            c2_copy(h, k).wait_recv()
        c3[h] = four(sc2[h, z], rc2, h).astype(BF16)
        for slot in range(7):
            c3_copy(h, slot).start()
        for k in range(1, 4):
            a2_copy(h, k).wait_recv()
            b2_copy(h, k).wait_recv()
        s3[h, :, 0] = four(sa2[h, z], ra2, h).astype(BF16)
        s3[h, :, 1] = four(sb2[h, y], rb2, h).astype(BF16)
        for k in range(1, 4):
            x3_copy(h, k).start()

    def output(h):
        cols = pl.ds(pl.multiple_of(h * 128, 128), 128)
        for slot in range(7):
            c3_copy(h, slot).wait_recv()
        mine = four(c3[h, y], rc3, h)
        other = (rc3[h, 3].astype(F32) + rc3[h, 4].astype(F32)) + (
            rc3[h, 5].astype(F32) + rc3[h, 6].astype(F32)
        )
        gk_o[pl.ds(48, 16), cols] = jnp.where(grp == 0, mine, other)
        gv_o[pl.ds(48, 16), cols] = jnp.where(grp == 0, other, mine)
        for k in range(1, 4):
            x3_copy(h, k).wait_recv()
        total = four(s3[h, xlo], r3, h)
        gk_o[pl.ds(0, 48), cols] = total[0]
        gv_o[pl.ds(0, 48), cols] = total[1]

    def head(h, carry):
        kt[...] = kv[:, pl.ds(pl.multiple_of(h * 128, 128), 128)].T
        attend(h, 3)

        @pl.when(h > 0)
        def _():
            prompt_rows(h - 1)

        @pl.when(h > 1)
        def _():
            second(h - 2)

        attend(h, 2)

        @pl.when(h > 0)
        def _():
            contract(h - 1)

        attend(h, 1)

        @pl.when(h > 1)
        def _():
            third(h - 2)

        attend(h, 0)
        finish(h)
        return carry

    def wrap(h, carry):
        output(h)
        dq_copy(h).wait()
        for part in range(2):
            g_copy(h, part).wait_send()
        for k in range(1, 8):
            pg_copy(h, k).wait_send()
            c3_copy(h, k - 1).wait_send()
        for k in range(1, 4):
            for copy in (a1_copy, b1_copy, c1_copy, a2_copy, b2_copy, c2_copy, x3_copy):
                copy(h, k).wait_send()
        return carry

    lax.fori_loop(0, KVH, head, 0)
    second(2)
    prompt_rows(3)
    contract(3)
    third(2)
    for slot in range(11):
        stat_copy(slot).wait_send()
    for k in range(1, 8):
        gather(k).wait_send()
    for seg in range(4):
        for copy in x_remote(seg):
            copy.wait_send()
    lax.fori_loop(0, 2, wrap, 0)
    second(3)
    third(3)
    lax.fori_loop(2, KVH, wrap, 0)


def body(
    prompt_states, response_states, queries, grad_output, key_weight, value_weight,
    rewards, lengths, group_ids,
):
    cosine, sine = rotary_tables()
    hbm = pl.BlockSpec(memory_space=pl.ANY)
    vmem = pl.BlockSpec(memory_space=pltpu.VMEM)
    dma = pltpu.SemaphoreType.DMA
    scratch = [
        pltpu.VMEM((PSH, D), BF16),
        pltpu.VMEM((RLEN, D), BF16),
        pltpu.VMEM((RLEN, 2048), BF16),
        pltpu.VMEM((RLEN, 2048), BF16),
        pltpu.VMEM((D, 1024), BF16),
        pltpu.VMEM((RLEN, 2048), BF16),
        pltpu.VMEM((576, 2048), BF16),
        pltpu.VMEM((2048, 1152), BF16),
        pltpu.VMEM((PSH, 1024), F32),
        pltpu.VMEM((RLEN, 1024), F32),
        pltpu.VMEM((1024, 1024), BF16),
        pltpu.VMEM((128, 1024), BF16),
        pltpu.VMEM((1024, 128), F32),
        pltpu.VMEM((1024, 128), F32),
        pltpu.VMEM((KVH, 1152, 256), BF16),
        pltpu.VMEM((KVH, 8, PSH, 256), BF16),
        pltpu.VMEM((KVH, 7, PSH, 256), BF16),
        pltpu.VMEM((KVH, 4, 4, 2, 48, 128), BF16),
        pltpu.VMEM((KVH, 4, 4, 2, 48, 128), BF16),
        pltpu.VMEM((KVH, 4, 4, 4, 16, 128), BF16),
        pltpu.VMEM((KVH, 3, 4, 2, 48, 128), BF16),
        pltpu.VMEM((KVH, 3, 4, 2, 48, 128), BF16),
        pltpu.VMEM((KVH, 3, 4, 4, 16, 128), BF16),
        pltpu.VMEM((KVH, 4, 2, 48, 128), BF16),
        pltpu.VMEM((KVH, 4, 2, 48, 128), BF16),
        pltpu.VMEM((KVH, 4, 4, 16, 128), BF16),
        pltpu.VMEM((KVH, 3, 2, 48, 128), BF16),
        pltpu.VMEM((KVH, 3, 2, 48, 128), BF16),
        pltpu.VMEM((KVH, 3, 4, 16, 128), BF16),
        pltpu.VMEM((KVH, 2, 2, 48, 128), BF16),
        pltpu.VMEM((KVH, 3, 2, 48, 128), BF16),
        pltpu.VMEM((KVH, 4, 16, 128), BF16),
        pltpu.VMEM((KVH, 7, 16, 128), BF16),
        pltpu.VMEM((3, 8, 128), F32),
        pltpu.VMEM((11, 8, 128), F32),
        dma((6,)), dma((KVH,)), dma((8,)), dma((8,)), dma((7,)), dma((7,)),
        dma((11,)), dma((11,)), dma((KVH, 2)), dma((KVH, 2)), dma((KVH, 7)), dma((KVH, 7)),
        dma((KVH, 7)), dma((KVH, 7)),
    ] + [dma((KVH, 3)) for _ in range(14)]
    dq, gk, gv = pl.pallas_call(
        kernel,
        out_shape=(
            jax.ShapeDtypeStruct((RLEN, 2048), BF16),
            jax.ShapeDtypeStruct((64, 512), F32),
            jax.ShapeDtypeStruct((64, 512), F32),
        ),
        in_specs=[hbm] * 6 + [vmem] * 5,
        out_specs=(hbm, vmem, vmem),
        scratch_shapes=scratch,
        compiler_params=pltpu.CompilerParams(
            collective_id=0, has_side_effects=True, vmem_limit_bytes=60 * 2**20
        ),
        name="surrogate_grad",
    )(
        prompt_states[0], response_states[0, 0], queries[0, 0], grad_output[0, 0],
        key_weight, value_weight, rewards, lengths, group_ids,
        jnp.asarray(cosine), jnp.asarray(sine),
    )
    return dq[None, None], gk, gv


def solution(mesh):
    row = P("grp", ("prompt", "resp"))
    tokens = P("grp", ("prompt", "resp"), None, None)
    return jax.shard_map(
        body,
        mesh=mesh,
        in_specs=(P("grp", "prompt", None), tokens, tokens, tokens, P(), P(), row, row, row),
        out_specs=(tokens, P(("prompt", "resp"), None), P(("prompt", "resp"), None)),
        check_vma=False,
    )
```

```python
import functools
import math

import jax
import jax.numpy as jnp
import numpy as np
from jax import lax
from jax.experimental import pallas as pl
from jax.experimental.pallas import tpu as pltpu
from jax.sharding import PartitionSpec as P

HEAD_DIM = 128
KVH = 4
RLEN = 512
PLEN = 512
PSH = 64
D = 4096
NADV = 8
DBASE = 1024
THETA = 1000000.0
EPS = 1e-06
SCALE = 1.0 / math.sqrt(HEAD_DIM)
EXP2_SCALE = math.log2(math.e) / math.sqrt(HEAD_DIM)

F32 = jnp.float32
BF16 = jnp.bfloat16
NT = (((1,), (1,)), ((), ()))
MESH = pl.DeviceIdType.MESH


def rotary_tables():
    half = HEAD_DIM // 2
    steps = np.arange(half, dtype=np.float32)
    freq = np.power(np.float32(THETA), np.float32(-2.0) * steps / np.float32(2.0 * half))
    positions = np.arange(PLEN + RLEN, dtype=np.float32)
    angle = (positions[:, None] * freq.astype(np.float32)[None, :]).astype(np.float64)
    cosine, sine = np.cos(angle), np.sin(angle)
    return (
        np.concatenate([cosine, cosine], axis=1).astype(np.float32),
        np.concatenate([-sine, sine], axis=1).astype(np.float32),
    )


def finish_head(raw, cosine, sine):
    factor = lax.rsqrt(jnp.mean(raw * raw, axis=-1, keepdims=True) + EPS)
    normed = raw * factor
    return normed * cosine + pltpu.roll(normed, HEAD_DIM // 2, 1) * sine


def head_backward(grad, raw, cosine, sine):
    factor = lax.rsqrt(jnp.mean(raw * raw, axis=-1, keepdims=True) + EPS)
    normed = raw * factor
    unturned = grad * cosine - pltpu.roll(grad, HEAD_DIM // 2, 1) * sine
    inner = jnp.mean(unturned * normed, axis=-1, keepdims=True)
    return factor * (unturned - normed * inner)


def kernel(
    ps_h, st_h, q_h, go_h, wk_h, wv_h, cos_h, sin_h, rew, lens, ids,
    dq_o, gk_o, gv_o,
    ps_v, st_v, w_v, cos_t, sin_t, x_v, xt, praw, oraw, kv, kt, dk, dv,
    g_b, pgs, pgr, sa, sb, sc, ra1, rb1, rc1, sa2, sb2, sc2, ra2, rb2, rc2, s3, r3, c3, rc3,
    st_s, st_r,
    lsem, xs, xr, ags, agr, sts, strr, gs, gr, pss, psr, c3s, c3r,
    a1s, a1r, b1s, b1r, c1s, c1r, a2s, a2r, b2s, b2r, c2s, c2r, x3s, x3r,
):
    grp = lax.axis_index("grp")
    pr = lax.axis_index("prompt")
    rs = lax.axis_index("resp")
    y = pr // 2
    c = pr % 2
    z = rs // 2
    xlo = rs % 2
    x = grp * 2 + xlo

    def prompt_peer(k):
        return (grp, (pr + k) % 8, rs)

    def core_peer():
        return (grp, y * 2 + (1 - c), rs)

    def y_peer(k):
        return (grp, ((y + k) % 4) * 2 + c, rs)

    def z_peer(k):
        return (grp, pr, ((z + k) % 4) * 2 + xlo)

    def x_peer(k):
        other = (x + k) % 4
        return (other // 2, pr, z * 2 + other % 2)

    def cross_peer(k):
        return (1 - grp, ((y + k) % 4) * 2 + c, rs)

    def pair_peer():
        return (grp, pr, z * 2 + (1 - xlo))

    def rcopy(src, dst, send, recv, dev):
        return pltpu.make_async_remote_copy(
            src_ref=src, dst_ref=dst, send_sem=send, recv_sem=recv,
            device_id=dev, device_id_type=MESH,
        )

    loads = [
        pltpu.make_async_copy(ps_h, ps_v, lsem.at[0]),
        pltpu.make_async_copy(wk_h, w_v.at[:, pl.ds(0, 512)], lsem.at[1]),
        pltpu.make_async_copy(wv_h, w_v.at[:, pl.ds(512, 512)], lsem.at[2]),
        pltpu.make_async_copy(st_h, st_v, lsem.at[3]),
        pltpu.make_async_copy(cos_h, cos_t, lsem.at[4]),
        pltpu.make_async_copy(sin_h, sin_t, lsem.at[5]),
    ]
    for load in loads[:3] + loads[4:6]:
        load.start()

    def x_remote(seg):
        cols = pl.ds(pl.multiple_of(seg * 1024 + (1 - c) * 512, 512), 512)
        here = pl.ds(seg * 512, 512)
        return (
            rcopy(st_v.at[:, cols], x_v.at[pl.ds(0, 512), here], xs.at[seg], xr.at[seg], core_peer()),
            rcopy(ps_v.at[:, cols], x_v.at[pl.ds(512, 64), here], xs.at[4 + seg], xr.at[4 + seg], core_peer()),
        )

    barrier = pltpu.get_barrier_semaphore()
    for k in range(1, 8):
        pl.semaphore_signal(barrier, inc=1, device_id=prompt_peer(k), device_id_type=MESH)
    for k in range(1, 4):
        pl.semaphore_signal(barrier, inc=1, device_id=z_peer(k), device_id_type=MESH)
        pl.semaphore_signal(barrier, inc=1, device_id=x_peer(k), device_id_type=MESH)
        pl.semaphore_signal(barrier, inc=1, device_id=cross_peer(k), device_id_type=MESH)
    pl.semaphore_wait(barrier, 16)

    lane = lax.broadcasted_iota(jnp.int32, (8, 128), 1)
    row = lax.broadcasted_iota(jnp.int32, (8, 128), 0)
    reward = jnp.broadcast_to(rew[...], (8, 128))
    onehot = jnp.where(lane == jnp.broadcast_to(ids[...], (8, 128)), 1.0, 0.0).astype(F32)
    st_s[0] = onehot * jnp.where(
        row == 0, 1.0, jnp.where(row == 1, reward, jnp.where(row == 2, reward * reward, 0.0))
    )

    def stat_copy(slot):
        if slot < 7:
            return rcopy(st_s.at[0], st_r.at[slot], sts.at[slot], strr.at[slot], prompt_peer(slot + 1))
        if slot < 10:
            return rcopy(st_s.at[1], st_r.at[slot], sts.at[slot], strr.at[slot], z_peer(slot - 6))
        return rcopy(st_s.at[2], st_r.at[slot], sts.at[slot], strr.at[slot], pair_peer())

    for slot in range(7):
        stat_copy(slot).start()

    loads[0].wait()
    loads[1].wait()
    loads[2].wait()
    loads[3].start()

    def prompt_tile(n, carry):
        cols = pl.ds(pl.multiple_of(n * 256, 256), 256)
        praw[:, cols] = jnp.dot(ps_v[...], w_v[:, cols], preferred_element_type=F32)
        return carry

    lax.fori_loop(0, 4, prompt_tile, 0)
    prow = pl.ds(pl.multiple_of(pr * PSH, PSH), PSH)
    loads[4].wait()
    loads[5].wait()
    pcos, psin = cos_t[prow, :], sin_t[prow, :]
    for h in range(KVH):
        cols = pl.ds(h * 128, 128)
        kv[prow, cols] = finish_head(praw[:, cols], pcos, psin).astype(BF16)
    kv[prow, pl.ds(512, 512)] = praw[:, pl.ds(512, 512)].astype(BF16)

    def shard(index):
        return kv.at[pl.ds(pl.multiple_of(index * PSH, PSH), PSH)]

    def y_shard(k, core):
        return shard(((y + 4 - k) % 4) * 2 + core)

    def gather(k):
        dev = core_peer() if k == 0 else y_peer(k)
        return rcopy(shard(pr), shard(pr), ags.at[k], agr.at[k], dev)

    def gathered(k):
        theirs = shard(y * 2 + (1 - c)) if k == 0 else y_shard(k, c)
        return rcopy(theirs, theirs, ags.at[k], agr.at[k], core_peer())

    def forward(k):
        return rcopy(y_shard(k, c), y_shard(k, c), ags.at[3 + k], agr.at[3 + k], core_peer())

    def forwarded(k):
        theirs = y_shard(k, 1 - c)
        return rcopy(theirs, theirs, ags.at[3 + k], agr.at[3 + k], core_peer())

    for k in (1, 2, 3, 0):
        gather(k).start()

    for slot in range(7):
        stat_copy(slot).wait_recv()
    st_s[1] = st_s[0] + (
        ((st_r[0] + st_r[1]) + (st_r[2] + st_r[3])) + ((st_r[4] + st_r[5]) + st_r[6])
    )
    for slot in range(7, 10):
        stat_copy(slot).start()

    loads[3].wait()
    for seg in range(4):
        for copy in x_remote(seg):
            copy.start()

    def own_tile(n, carry):
        cols = pl.ds(pl.multiple_of(n * 256, 256), 256)
        oraw[:, cols] = jnp.dot(st_v[...], w_v[:, cols], preferred_element_type=F32)
        for t in range(2):
            here = pl.ds(pl.multiple_of(n * 512 + t * 256, 256), 256)
            mine = pl.ds(pl.multiple_of(n * 1024 + c * 512 + t * 256, 256), 256)
            xt[here, pl.ds(0, 512)] = st_v[:, mine].T
        return carry

    lax.fori_loop(0, 4, own_tile, 0)
    late = [
        pltpu.make_async_copy(
            array.at[:, pl.ds(half * 1024, 1024)], w_v.at[pl.ds(base + half * 512, 512)], lsem.at[6 + n * 2 + half]
        )
        for n, (array, base) in enumerate(((go_h, DBASE), (q_h, 0)))
        for half in range(2)
    ]
    for load in late:
        load.start()
    for k in range(1, 4):
        gathered(k).wait_recv()
        forward(k).start()

    for slot in range(7, 10):
        stat_copy(slot).wait_recv()
    st_s[2] = (st_s[1] + st_r[7]) + (st_r[8] + st_r[9])
    stat_copy(10).start()

    own = pl.ds(PLEN, RLEN)
    ocos, osin = cos_t.at[own], sin_t.at[own]

    def own_keys(h, carry):
        cols = pl.ds(pl.multiple_of(h * 128, 128), 128)
        kv[own, cols] = finish_head(oraw[:, cols], ocos[...], osin[...]).astype(BF16)
        return carry

    lax.fori_loop(0, KVH, own_keys, 0)
    kv[own, pl.ds(512, 512)] = oraw[:, pl.ds(512, 512)].astype(BF16)

    for seg in range(4):
        for copy in x_remote(seg):
            copy.wait_recv()

    def turn(n, carry):
        here = pl.ds(pl.multiple_of(n * 256, 256), 256)
        mine = pl.ds(pl.multiple_of((n // 2) * 1024 + c * 512 + (n % 2) * 256, 256), 256)
        xt[here, pl.ds(512, 512)] = x_v[pl.ds(0, 512), here].T
        xt[here, pl.ds(1024, 128)] = jnp.concatenate([ps_v[:, mine], x_v[pl.ds(512, 64), here]], axis=0).T
        return carry

    lax.fori_loop(0, 8, turn, 0)

    stat_copy(10).wait_recv()
    sums = st_s[2] + st_r[10]
    count, total, square = sums[0:1], sums[1:2], sums[2:3]
    members = jnp.maximum(count, 1.0)
    mean = total / members
    spread = jnp.sqrt(jnp.maximum(square / members - mean * mean, 0.0))
    mine = onehot[0:1]
    own_mean = jnp.sum(mine * mean, axis=1, keepdims=True)
    own_spread = jnp.sum(mine * spread, axis=1, keepdims=True)
    advantage = (rew[...] - own_mean) / jnp.maximum(own_spread, 0.5)
    weight = advantage / lens[...].astype(F32)
    token = lax.broadcasted_iota(jnp.int32, (RLEN, 128), 0)
    live = token < jnp.broadcast_to(lens[...], (RLEN, 128))
    coef = jnp.where(live, jnp.broadcast_to(weight, (RLEN, 128)), 0.0)
    for half in range(2):
        late[half].wait()
        rows = pl.ds(DBASE + half * 512, 512)
        for n in range(8):
            cols = pl.ds(n * 128, 128)
            w_v[rows, cols] = (w_v[rows, cols].astype(F32) * coef).astype(BF16)
    late[2].wait()
    late[3].wait()
    gathered(0).wait_recv()
    for k in range(1, 4):
        forwarded(k).wait_recv()

    def attend(h, b):
        count = PLEN + 128 * (b + 1)
        rows = pl.ds(b * 128, 128)
        keys = kv[pl.ds(0, count), pl.ds(pl.multiple_of(h * 128, 128), 128)]
        vals = kv[pl.ds(0, count), pl.ds(pl.multiple_of(512 + h * 128, 128), 128)]
        cols = [pl.ds(pl.multiple_of((h * 4 + j) * 128, 128), 128) for j in range(4)]
        part = [pl.ds(pl.multiple_of((h % 2) * 512 + j * 128, 128), 128) for j in range(4)]
        start = (h // 2) * 512 + b * 128
        qrows = pl.ds(pl.multiple_of(start, 128), 128)
        drows = pl.ds(pl.multiple_of(DBASE + start, 128), 128)
        q = jnp.concatenate([w_v[qrows, cc] for cc in part], axis=0)
        do = jnp.concatenate([w_v[drows, cc] for cc in part], axis=0)
        s = lax.dot_general(keys, q, NT, preferred_element_type=F32)
        key = lax.broadcasted_iota(jnp.int32, (128, 512), 0)
        query = lax.broadcasted_iota(jnp.int32, (128, 512), 1) % 128
        s = jnp.concatenate(
            [s[: count - 128], jnp.where(key <= query, s[count - 128 :], -jnp.inf)], axis=0
        )
        peak = jnp.max(s, axis=0, keepdims=True)
        e = jnp.exp2((s - peak) * EXP2_SCALE)
        p = e * (1.0 / jnp.sum(e, axis=0, keepdims=True))
        dp = lax.dot_general(vals, do, NT, preferred_element_type=F32)
        delta = jnp.sum(p * dp, axis=0, keepdims=True)
        ds = (p * (dp - delta)).astype(BF16)
        gv = jnp.dot(p.astype(BF16), do, preferred_element_type=F32)
        gk = jnp.dot(ds, q, preferred_element_type=F32)
        if b == 3:
            dv[...] = gv
            dk[...] = gk
        else:
            dv[pl.ds(0, count)] += gv
            dk[pl.ds(0, count)] += gk
        dq = (jnp.dot(kt[:, pl.ds(0, count)], ds, preferred_element_type=F32) * SCALE).T.astype(BF16)
        for j, cc in enumerate(cols):
            dq_o[rows, cc] = dq[j * 128 : (j + 1) * 128]

    def g_copy(h, part):
        mine = (pl.ds(0, 512), pl.ds(1024, 64))[part]
        theirs = (pl.ds(512, 512), pl.ds(1088, 64))[part]
        return rcopy(g_b.at[h, mine], g_b.at[h, theirs], gs.at[h, part], gr.at[h, part], core_peer())

    def pg_copy(h, k):
        return rcopy(pgs.at[h, (pr + k) % 8], pgr.at[h, k - 1], pss.at[h, k - 1], psr.at[h, k - 1], prompt_peer(k))

    def a1_copy(h, k):
        return rcopy(sa.at[h, (y + k) % 4], ra1.at[h, k - 1], a1s.at[h, k - 1], a1r.at[h, k - 1], y_peer(k))

    def b1_copy(h, k):
        return rcopy(sb.at[h, (z + k) % 4], rb1.at[h, k - 1], b1s.at[h, k - 1], b1r.at[h, k - 1], z_peer(k))

    def c1_copy(h, k):
        return rcopy(sc.at[h, (x + k) % 4], rc1.at[h, k - 1], c1s.at[h, k - 1], c1r.at[h, k - 1], x_peer(k))

    def a2_copy(h, k):
        return rcopy(sa2.at[h, (z + k) % 4], ra2.at[h, k - 1], a2s.at[h, k - 1], a2r.at[h, k - 1], z_peer(k))

    def b2_copy(h, k):
        return rcopy(sb2.at[h, (y + k) % 4], rb2.at[h, k - 1], b2s.at[h, k - 1], b2r.at[h, k - 1], y_peer(k))

    def c2_copy(h, k):
        return rcopy(sc2.at[h, (z + k) % 4], rc2.at[h, k - 1], c2s.at[h, k - 1], c2r.at[h, k - 1], z_peer(k))

    def x3_copy(h, k):
        return rcopy(s3.at[h, (x + k) % 2], r3.at[h, k - 1], x3s.at[h, k - 1], x3r.at[h, k - 1], x_peer(k))

    def c3_copy(h, slot):
        k = slot + 1 if slot < 3 else slot - 3
        dev = y_peer(k) if slot < 3 else cross_peer(k)
        return rcopy(c3.at[h, (y + k) % 4], rc3.at[h, slot], c3s.at[h, slot], c3r.at[h, slot], dev)

    def finish(h):
        cols = pl.ds(pl.multiple_of(h * 128, 128), 128)
        for t in range(8):
            pgs[h, t, :, pl.ds(0, 128)] = (dk[pl.ds(t * 64, 64)] * SCALE).astype(BF16)
            pgs[h, t, :, pl.ds(128, 128)] = dv[pl.ds(t * 64, 64)].astype(BF16)
        for k in range(1, 8):
            pg_copy(h, k).start()
        g_b[h, pl.ds(0, 512), pl.ds(0, 128)] = head_backward(
            dk[own] * SCALE, oraw[:, cols], ocos[...], osin[...]
        ).astype(BF16)
        g_b[h, pl.ds(0, 512), pl.ds(128, 128)] = dv[own].astype(BF16)
        g_copy(h, 0).start()

        @pl.when(h > 0)
        def _():
            for k in range(1, 4):
                a1_copy(h - 1, k).start()


    def prompt_rows(h):
        cols = pl.ds(pl.multiple_of(h * 128, 128), 128)
        total = pgs[h, pr].astype(F32)
        for k in range(1, 8):
            pg_copy(h, k).wait_recv()
            total = total + pgr[h, k - 1].astype(F32)
        g_b[h, pl.ds(1024, 64), pl.ds(0, 128)] = head_backward(
            total[:, :128], praw[:, cols], cos_t[prow, :], sin_t[prow, :]
        ).astype(BF16)
        g_b[h, pl.ds(1024, 64), pl.ds(128, 128)] = total[:, 128:].astype(BF16)
        g_copy(h, 1).start()

    def emit(h, seg, out):
        out = out.astype(BF16)
        for zz in range(4):
            for xx in range(2):
                at = zz * 128 + xx * 64
                sa[h, seg, zz, xx] = out[at : at + 48, :128]
                sb[h, zz, seg, xx] = out[at : at + 48, 128:]
                sc[h, xx, zz, seg] = out[at + 48 : at + 64, :128]
                sc[h, xx + 2, zz, seg] = out[at + 48 : at + 64, 128:]

    def contract(h):
        g_copy(h, 0).wait_recv()
        g_copy(h, 1).wait_recv()

        def segment(seg, carry):
            rows = pl.ds(pl.multiple_of(seg * 512, 512), 512)
            emit(h, seg, jnp.dot(xt[rows, :], g_b[h], preferred_element_type=F32))
            return carry

        lax.fori_loop(0, 4, segment, 0)
        for k in range(1, 4):
            b1_copy(h, k).start()
            c1_copy(h, k).start()

    def contract_last(h):
        g_copy(h, 0).wait_recv()

        def responses(seg, carry):
            rows = pl.ds(pl.multiple_of(seg * 512, 512), 512)
            cols = pl.ds(pl.multiple_of(seg * 256, 256), 256)
            oraw[:, cols] = jnp.dot(
                xt[rows, pl.ds(0, 1024)], g_b[h, pl.ds(0, 1024)], preferred_element_type=F32
            )
            return carry

        lax.fori_loop(0, 4, responses, 0)
        prompt_rows(h)
        second_a(h - 2)
        g_copy(h, 1).wait_recv()

        def prompts(i, carry):
            seg = (y + 1 + i) % 4
            rows = pl.ds(pl.multiple_of(seg * 512, 512), 512)
            cols = pl.ds(pl.multiple_of(seg * 256, 256), 256)
            part = jnp.dot(
                xt[rows, pl.ds(1024, 128)], g_b[h, pl.ds(1024, 128)], preferred_element_type=F32
            )
            emit(h, seg, oraw[:, cols] + part)

            @pl.when(i < 3)
            def _():
                a1_copy(h, i + 1).start()

            return carry

        lax.fori_loop(0, 4, prompts, 0)
        for k in range(1, 4):
            b1_copy(h, k).start()
            c1_copy(h, k).start()

    def four(own_block, got, h):
        return (own_block.astype(F32) + got[h, 0].astype(F32)) + (
            got[h, 1].astype(F32) + got[h, 2].astype(F32)
        )

    def second_bc(h):
        for k in range(1, 4):
            c1_copy(h, k).wait_recv()
        sc2[h] = four(sc[h, x], rc1, h).astype(BF16)
        for k in range(1, 4):
            c2_copy(h, k).start()
        for k in range(1, 4):
            b1_copy(h, k).wait_recv()
        sb2[h] = four(sb[h, z], rb1, h).astype(BF16)
        for k in range(1, 4):
            b2_copy(h, k).start()

    def second_a(h):
        for k in range(1, 4):
            a1_copy(h, k).wait_recv()
        sa2[h] = four(sa[h, y], ra1, h).astype(BF16)
        for k in range(1, 4):
            a2_copy(h, k).start()

    def third(h):
        for k in range(1, 4):
            c2_copy(h, k).wait_recv()
        c3[h] = four(sc2[h, z], rc2, h).astype(BF16)
        for slot in range(7):
            c3_copy(h, slot).start()
        for k in range(1, 4):
            a2_copy(h, k).wait_recv()
            b2_copy(h, k).wait_recv()
        s3[h, :, 0] = four(sa2[h, z], ra2, h).astype(BF16)
        s3[h, :, 1] = four(sb2[h, y], rb2, h).astype(BF16)
        for k in range(1, 4):
            x3_copy(h, k).start()

    def output(h):
        cols = pl.ds(pl.multiple_of(h * 128, 128), 128)
        for slot in range(7):
            c3_copy(h, slot).wait_recv()
        mine = four(c3[h, y], rc3, h)
        other = (rc3[h, 3].astype(F32) + rc3[h, 4].astype(F32)) + (
            rc3[h, 5].astype(F32) + rc3[h, 6].astype(F32)
        )
        gk_o[pl.ds(48, 16), cols] = jnp.where(grp == 0, mine, other)
        gv_o[pl.ds(48, 16), cols] = jnp.where(grp == 0, other, mine)
        for k in range(1, 4):
            x3_copy(h, k).wait_recv()
        total = four(s3[h, xlo], r3, h)
        gk_o[pl.ds(0, 48), cols] = total[0]
        gv_o[pl.ds(0, 48), cols] = total[1]

    def head(h, carry):
        kt[...] = kv[:, pl.ds(pl.multiple_of(h * 128, 128), 128)].T
        attend(h, 3)

        @pl.when(h > 2)
        def _():
            second_a(h - 3)

        attend(h, 2)
        attend(h, 1)

        @pl.when(h > 0)
        def _():
            prompt_rows(h - 1)

        @pl.when(h > 1)
        def _():
            second_bc(h - 2)

        attend(h, 0)

        @pl.when(h > 2)
        def _():
            third(h - 3)

        @pl.when(h > 0)
        def _():
            contract(h - 1)

        finish(h)
        return carry

    def wrap(h, carry):
        output(h)
        for part in range(2):
            g_copy(h, part).wait_send()
        for k in range(1, 8):
            pg_copy(h, k).wait_send()
            c3_copy(h, k - 1).wait_send()
        for k in range(1, 4):
            for copy in (a1_copy, b1_copy, c1_copy, a2_copy, b2_copy, c2_copy, x3_copy):
                copy(h, k).wait_send()
        return carry

    lax.fori_loop(0, KVH, head, 0)
    contract_last(3)
    second_bc(2)
    third(1)
    second_a(2)
    for slot in range(11):
        stat_copy(slot).wait_send()
    for k in range(4):
        gather(k).wait_send()
    for k in range(1, 4):
        forward(k).wait_send()
    for seg in range(4):
        for copy in x_remote(seg):
            copy.wait_send()
    lax.fori_loop(0, 2, wrap, 0)
    third(2)
    second_bc(3)
    second_a(3)
    third(3)
    lax.fori_loop(2, KVH, wrap, 0)


def body(
    prompt_states, response_states, queries, grad_output, key_weight, value_weight,
    rewards, lengths, group_ids,
):
    cosine, sine = rotary_tables()
    hbm = pl.BlockSpec(memory_space=pltpu.HBM)
    vmem = pl.BlockSpec(memory_space=pltpu.VMEM)
    dma = pltpu.SemaphoreType.DMA
    scratch = [
        pltpu.VMEM((PSH, D), BF16),
        pltpu.VMEM((RLEN, D), BF16),
        pltpu.VMEM((D, 1024), BF16),
        pltpu.VMEM((PLEN + RLEN, 128), F32),
        pltpu.VMEM((PLEN + RLEN, 128), F32),
        pltpu.VMEM((576, 2048), BF16),
        pltpu.VMEM((2048, 1152), BF16),
        pltpu.VMEM((PSH, 1024), F32),
        pltpu.VMEM((RLEN, 1024), F32),
        pltpu.VMEM((1024, 1024), BF16),
        pltpu.VMEM((128, 1024), BF16),
        pltpu.VMEM((1024, 128), F32),
        pltpu.VMEM((1024, 128), F32),
        pltpu.VMEM((KVH, 1152, 256), BF16),
        pltpu.VMEM((KVH, 8, PSH, 256), BF16),
        pltpu.VMEM((KVH, 7, PSH, 256), BF16),
        pltpu.VMEM((KVH, 4, 4, 2, 48, 128), BF16),
        pltpu.VMEM((KVH, 4, 4, 2, 48, 128), BF16),
        pltpu.VMEM((KVH, 4, 4, 4, 16, 128), BF16),
        pltpu.VMEM((KVH, 3, 4, 2, 48, 128), BF16),
        pltpu.VMEM((KVH, 3, 4, 2, 48, 128), BF16),
        pltpu.VMEM((KVH, 3, 4, 4, 16, 128), BF16),
        pltpu.VMEM((KVH, 4, 2, 48, 128), BF16),
        pltpu.VMEM((KVH, 4, 2, 48, 128), BF16),
        pltpu.VMEM((KVH, 4, 4, 16, 128), BF16),
        pltpu.VMEM((KVH, 3, 2, 48, 128), BF16),
        pltpu.VMEM((KVH, 3, 2, 48, 128), BF16),
        pltpu.VMEM((KVH, 3, 4, 16, 128), BF16),
        pltpu.VMEM((KVH, 2, 2, 48, 128), BF16),
        pltpu.VMEM((KVH, 3, 2, 48, 128), BF16),
        pltpu.VMEM((KVH, 4, 16, 128), BF16),
        pltpu.VMEM((KVH, 7, 16, 128), BF16),
        pltpu.VMEM((3, 8, 128), F32),
        pltpu.VMEM((11, 8, 128), F32),
        dma((10,)), dma((8,)), dma((8,)), dma((7,)), dma((7,)),
        dma((11,)), dma((11,)), dma((KVH, 2)), dma((KVH, 2)), dma((KVH, 7)), dma((KVH, 7)),
        dma((KVH, 7)), dma((KVH, 7)),
    ] + [dma((KVH, 3)) for _ in range(14)]
    dq, gk, gv = pl.pallas_call(
        kernel,
        out_shape=(
            jax.ShapeDtypeStruct((RLEN, 2048), BF16),
            jax.ShapeDtypeStruct((64, 512), F32),
            jax.ShapeDtypeStruct((64, 512), F32),
        ),
        in_specs=[hbm] * 8 + [vmem] * 3,
        out_specs=(vmem, vmem, vmem),
        scratch_shapes=scratch,
        compiler_params=pltpu.CompilerParams(
            collective_id=0, has_side_effects=True, vmem_limit_bytes=51 * 2**20
        ),
        name="surrogate_grad",
    )(
        *[pltpu.with_memory_space_constraint(a, pltpu.HBM) for a in (prompt_states[0], response_states[0, 0], queries[0, 0], grad_output[0, 0])],
        key_weight, value_weight, *[pltpu.with_memory_space_constraint(jnp.asarray(a), pltpu.HBM) for a in (cosine, sine)],
        rewards, lengths, group_ids,
    )
    return dq[None, None], gk, gv


def solution(mesh):
    row = P("grp", ("prompt", "resp"))
    tokens = P("grp", ("prompt", "resp"), None, None)
    return jax.shard_map(
        body,
        mesh=mesh,
        in_specs=(P("grp", "prompt", None), tokens, tokens, tokens, P(), P(), row, row, row),
        out_specs=(tokens, P(("prompt", "resp"), None), P(("prompt", "resp"), None)),
        check_vma=False,
    )
```

```python
import functools
import math

import jax
import jax.numpy as jnp
import numpy as np
from jax import lax
from jax.experimental import pallas as pl
from jax.experimental.pallas import tpu as pltpu
from jax.sharding import PartitionSpec as P

HEAD_DIM = 128
KVH = 4
RLEN = 512
PLEN = 512
PSH = 64
D = 4096
NADV = 8
DBASE = 1024
THETA = 1000000.0
EPS = 1e-06
SCALE = 1.0 / math.sqrt(HEAD_DIM)
EXP2_SCALE = math.log2(math.e) / math.sqrt(HEAD_DIM)

F32 = jnp.float32
BF16 = jnp.bfloat16
NT = (((1,), (1,)), ((), ()))
MESH = pl.DeviceIdType.MESH


def rotary_tables():
    half = HEAD_DIM // 2
    steps = np.arange(half, dtype=np.float32)
    freq = np.power(np.float32(THETA), np.float32(-2.0) * steps / np.float32(2.0 * half))
    positions = np.arange(PLEN + RLEN, dtype=np.float32)
    angle = (positions[:, None] * freq.astype(np.float32)[None, :]).astype(np.float64)
    cosine, sine = np.cos(angle), np.sin(angle)
    return (
        np.concatenate([cosine, cosine], axis=1).astype(np.float32),
        np.concatenate([-sine, sine], axis=1).astype(np.float32),
    )


def finish_head(raw, cosine, sine):
    factor = lax.rsqrt(jnp.mean(raw * raw, axis=-1, keepdims=True) + EPS)
    normed = raw * factor
    return normed * cosine + pltpu.roll(normed, HEAD_DIM // 2, 1) * sine


def head_backward(grad, raw, cosine, sine):
    factor = lax.rsqrt(jnp.mean(raw * raw, axis=-1, keepdims=True) + EPS)
    normed = raw * factor
    unturned = grad * cosine - pltpu.roll(grad, HEAD_DIM // 2, 1) * sine
    inner = jnp.mean(unturned * normed, axis=-1, keepdims=True)
    return factor * (unturned - normed * inner)


def kernel(
    ps_h, st_h, q_h, go_h, wk_h, wv_h, cos_h, sin_h, rew, lens, ids,
    dq_o, gk_o, gv_o,
    ps_v, st_v, w_v, cos_t, sin_t, x_v, xt, praw, oraw, kv, kt, dk, dv,
    g_b, pgs, pgr, sa, sb, sc, ra1, rb1, rc1, sa2, sb2, sc2, ra2, rb2, rc2, s3, r3, c3, rc3,
    st_s, st_r,
    lsem, xs, xr, ags, agr, sts, strr, gs, gr, pss, psr, c3s, c3r,
    a1s, a1r, b1s, b1r, c1s, c1r, a2s, a2r, b2s, b2r, c2s, c2r, x3s, x3r,
):
    grp = lax.axis_index("grp")
    pr = lax.axis_index("prompt")
    rs = lax.axis_index("resp")
    y = pr // 2
    c = pr % 2
    z = rs // 2
    xlo = rs % 2
    x = grp * 2 + xlo

    def prompt_peer(k):
        return (grp, (pr + k) % 8, rs)

    def core_peer():
        return (grp, y * 2 + (1 - c), rs)

    def y_peer(k):
        return (grp, ((y + k) % 4) * 2 + c, rs)

    def z_peer(k):
        return (grp, pr, ((z + k) % 4) * 2 + xlo)

    def x_peer(k):
        other = (x + k) % 4
        return (other // 2, pr, z * 2 + other % 2)

    def cross_peer(k):
        return (1 - grp, ((y + k) % 4) * 2 + c, rs)

    def pair_peer():
        return (grp, pr, z * 2 + (1 - xlo))

    def rcopy(src, dst, send, recv, dev):
        return pltpu.make_async_remote_copy(
            src_ref=src, dst_ref=dst, send_sem=send, recv_sem=recv,
            device_id=dev, device_id_type=MESH,
        )

    loads = [
        pltpu.make_async_copy(ps_h, ps_v, lsem.at[0]),
        pltpu.make_async_copy(wk_h, w_v.at[:, pl.ds(0, 512)], lsem.at[1]),
        pltpu.make_async_copy(wv_h, w_v.at[:, pl.ds(512, 512)], lsem.at[2]),
        pltpu.make_async_copy(st_h, st_v, lsem.at[3]),
        pltpu.make_async_copy(cos_h, cos_t, lsem.at[4]),
        pltpu.make_async_copy(sin_h, sin_t, lsem.at[5]),
    ]
    for load in loads[:3] + loads[4:6]:
        load.start()

    def x_remote(seg):
        cols = pl.ds(pl.multiple_of(seg * 1024 + (1 - c) * 512, 512), 512)
        here = pl.ds(seg * 512, 512)
        return (
            rcopy(st_v.at[:, cols], x_v.at[pl.ds(0, 512), here], xs.at[seg], xr.at[seg], core_peer()),
            rcopy(ps_v.at[:, cols], x_v.at[pl.ds(512, 64), here], xs.at[4 + seg], xr.at[4 + seg], core_peer()),
        )

    barrier = pltpu.get_barrier_semaphore()
    for k in range(1, 8):
        pl.semaphore_signal(barrier, inc=1, device_id=prompt_peer(k), device_id_type=MESH)
    for k in range(1, 4):
        pl.semaphore_signal(barrier, inc=1, device_id=z_peer(k), device_id_type=MESH)
        pl.semaphore_signal(barrier, inc=1, device_id=x_peer(k), device_id_type=MESH)
        pl.semaphore_signal(barrier, inc=1, device_id=cross_peer(k), device_id_type=MESH)
    pl.semaphore_wait(barrier, 16)

    lane = lax.broadcasted_iota(jnp.int32, (8, 128), 1)
    row = lax.broadcasted_iota(jnp.int32, (8, 128), 0)
    reward = jnp.broadcast_to(rew[...], (8, 128))
    onehot = jnp.where(lane == jnp.broadcast_to(ids[...], (8, 128)), 1.0, 0.0).astype(F32)
    st_s[0] = onehot * jnp.where(
        row == 0, 1.0, jnp.where(row == 1, reward, jnp.where(row == 2, reward * reward, 0.0))
    )

    def stat_copy(slot):
        if slot < 7:
            return rcopy(st_s.at[0], st_r.at[slot], sts.at[slot], strr.at[slot], prompt_peer(slot + 1))
        if slot < 10:
            return rcopy(st_s.at[1], st_r.at[slot], sts.at[slot], strr.at[slot], z_peer(slot - 6))
        return rcopy(st_s.at[2], st_r.at[slot], sts.at[slot], strr.at[slot], pair_peer())

    for slot in range(7):
        stat_copy(slot).start()

    loads[0].wait()
    loads[1].wait()
    loads[3].start()

    def prompt_tile(n, carry):
        cols = pl.ds(pl.multiple_of(n * 256, 256), 256)
        praw[:, cols] = jnp.dot(ps_v[...], w_v[:, cols], preferred_element_type=F32)
        return carry

    lax.fori_loop(0, 2, prompt_tile, 0)
    loads[2].wait()
    lax.fori_loop(2, 4, prompt_tile, 0)
    prow = pl.ds(pl.multiple_of(pr * PSH, PSH), PSH)
    loads[4].wait()
    loads[5].wait()
    pcos, psin = cos_t[prow, :], sin_t[prow, :]
    for h in range(KVH):
        cols = pl.ds(h * 128, 128)
        kv[prow, cols] = finish_head(praw[:, cols], pcos, psin).astype(BF16)
    kv[prow, pl.ds(512, 512)] = praw[:, pl.ds(512, 512)].astype(BF16)

    def shard(index):
        return kv.at[pl.ds(pl.multiple_of(index * PSH, PSH), PSH)]

    def y_shard(k, core):
        return shard(((y + 4 - k) % 4) * 2 + core)

    def gather(k):
        dev = core_peer() if k == 0 else y_peer(k)
        return rcopy(shard(pr), shard(pr), ags.at[k], agr.at[k], dev)

    def gathered(k):
        theirs = shard(y * 2 + (1 - c)) if k == 0 else y_shard(k, c)
        return rcopy(theirs, theirs, ags.at[k], agr.at[k], core_peer())

    def forward(k):
        return rcopy(y_shard(k, c), y_shard(k, c), ags.at[3 + k], agr.at[3 + k], core_peer())

    def forwarded(k):
        theirs = y_shard(k, 1 - c)
        return rcopy(theirs, theirs, ags.at[3 + k], agr.at[3 + k], core_peer())

    for k in (1, 2, 3, 0):
        gather(k).start()

    for slot in range(7):
        stat_copy(slot).wait_recv()
    st_s[1] = st_s[0] + (
        ((st_r[0] + st_r[1]) + (st_r[2] + st_r[3])) + ((st_r[4] + st_r[5]) + st_r[6])
    )
    for slot in range(7, 10):
        stat_copy(slot).start()

    loads[3].wait()
    for seg in range(4):
        for copy in x_remote(seg):
            copy.start()

    def own_tile(n, carry):
        cols = pl.ds(pl.multiple_of(n * 256, 256), 256)
        oraw[:, cols] = jnp.dot(st_v[...], w_v[:, cols], preferred_element_type=F32)
        for t in range(2):
            here = pl.ds(pl.multiple_of(n * 512 + t * 256, 256), 256)
            mine = pl.ds(pl.multiple_of(n * 1024 + c * 512 + t * 256, 256), 256)
            xt[here, pl.ds(0, 512)] = st_v[:, mine].T
        return carry

    lax.fori_loop(0, 4, own_tile, 0)
    late = [
        pltpu.make_async_copy(
            array.at[:, pl.ds(half * 1024, 1024)], w_v.at[pl.ds(base + half * 512, 512)], lsem.at[6 + n * 2 + half]
        )
        for n, (array, base) in enumerate(((go_h, DBASE), (q_h, 0)))
        for half in range(2)
    ]
    for load in late:
        load.start()
    for k in range(1, 4):
        gathered(k).wait_recv()
        forward(k).start()

    for slot in range(7, 10):
        stat_copy(slot).wait_recv()
    st_s[2] = (st_s[1] + st_r[7]) + (st_r[8] + st_r[9])
    stat_copy(10).start()

    own = pl.ds(PLEN, RLEN)
    ocos, osin = cos_t.at[own], sin_t.at[own]

    def own_keys(h, carry):
        cols = pl.ds(pl.multiple_of(h * 128, 128), 128)
        kv[own, cols] = finish_head(oraw[:, cols], ocos[...], osin[...]).astype(BF16)
        return carry

    lax.fori_loop(0, KVH, own_keys, 0)
    kv[own, pl.ds(512, 512)] = oraw[:, pl.ds(512, 512)].astype(BF16)

    for seg in range(4):
        for copy in x_remote(seg):
            copy.wait_recv()

    def turn(n, carry):
        here = pl.ds(pl.multiple_of(n * 256, 256), 256)
        mine = pl.ds(pl.multiple_of((n // 2) * 1024 + c * 512 + (n % 2) * 256, 256), 256)
        xt[here, pl.ds(512, 512)] = x_v[pl.ds(0, 512), here].T
        xt[here, pl.ds(1024, 128)] = jnp.concatenate([ps_v[:, mine], x_v[pl.ds(512, 64), here]], axis=0).T
        return carry

    lax.fori_loop(0, 8, turn, 0)

    stat_copy(10).wait_recv()
    sums = st_s[2] + st_r[10]
    count, total, square = sums[0:1], sums[1:2], sums[2:3]
    members = jnp.maximum(count, 1.0)
    mean = total / members
    spread = jnp.sqrt(jnp.maximum(square / members - mean * mean, 0.0))
    mine = onehot[0:1]
    own_mean = jnp.sum(mine * mean, axis=1, keepdims=True)
    own_spread = jnp.sum(mine * spread, axis=1, keepdims=True)
    advantage = (rew[...] - own_mean) / jnp.maximum(own_spread, 0.5)
    weight = advantage / lens[...].astype(F32)
    token = lax.broadcasted_iota(jnp.int32, (RLEN, 128), 0)
    live = token < jnp.broadcast_to(lens[...], (RLEN, 128))
    coef = jnp.where(live, jnp.broadcast_to(weight, (RLEN, 128)), 0.0)
    for half in range(2):
        late[half].wait()
        rows = pl.ds(DBASE + half * 512, 512)
        for n in range(8):
            cols = pl.ds(n * 128, 128)
            w_v[rows, cols] = (w_v[rows, cols].astype(F32) * coef).astype(BF16)
    late[2].wait()
    late[3].wait()
    gathered(0).wait_recv()
    for k in range(1, 4):
        forwarded(k).wait_recv()

    def attend(h, b):
        count = PLEN + 128 * (b + 1)
        rows = pl.ds(b * 128, 128)
        keys = kv[pl.ds(0, count), pl.ds(pl.multiple_of(h * 128, 128), 128)]
        vals = kv[pl.ds(0, count), pl.ds(pl.multiple_of(512 + h * 128, 128), 128)]
        cols = [pl.ds(pl.multiple_of((h * 4 + j) * 128, 128), 128) for j in range(4)]
        part = [pl.ds(pl.multiple_of((h % 2) * 512 + j * 128, 128), 128) for j in range(4)]
        start = (h // 2) * 512 + b * 128
        qrows = pl.ds(pl.multiple_of(start, 128), 128)
        drows = pl.ds(pl.multiple_of(DBASE + start, 128), 128)
        q = jnp.concatenate([w_v[qrows, cc] for cc in part], axis=0)
        do = jnp.concatenate([w_v[drows, cc] for cc in part], axis=0)
        s = lax.dot_general(keys, q, NT, preferred_element_type=F32)
        key = lax.broadcasted_iota(jnp.int32, (128, 512), 0)
        query = lax.broadcasted_iota(jnp.int32, (128, 512), 1) % 128
        s = jnp.concatenate(
            [s[: count - 128], jnp.where(key <= query, s[count - 128 :], -jnp.inf)], axis=0
        )
        peak = jnp.max(s, axis=0, keepdims=True)
        e = jnp.exp2((s - peak) * EXP2_SCALE)
        inverse = 1.0 / jnp.sum(e, axis=0, keepdims=True)
        dp = lax.dot_general(vals, do, NT, preferred_element_type=F32)
        delta = jnp.sum(e * dp, axis=0, keepdims=True) * inverse
        p = e * inverse
        ds = (p * (dp - delta)).astype(BF16)
        gv = jnp.dot(p.astype(BF16), do, preferred_element_type=F32)
        gk = jnp.dot(ds, q, preferred_element_type=F32)
        if b == 3:
            dv[...] = gv
            dk[...] = gk
        else:
            dv[pl.ds(0, count)] += gv
            dk[pl.ds(0, count)] += gk
        dq = (jnp.dot(kt[:, pl.ds(0, count)], ds, preferred_element_type=F32) * SCALE).T.astype(BF16)
        for j, cc in enumerate(cols):
            dq_o[rows, cc] = dq[j * 128 : (j + 1) * 128]

    def g_copy(h, part):
        mine = (pl.ds(0, 512), pl.ds(1024, 64))[part]
        theirs = (pl.ds(512, 512), pl.ds(1088, 64))[part]
        return rcopy(g_b.at[h, mine], g_b.at[h, theirs], gs.at[h, part], gr.at[h, part], core_peer())

    def pg_copy(h, k):
        return rcopy(pgs.at[h, (pr + k) % 8], pgr.at[h, k - 1], pss.at[h, k - 1], psr.at[h, k - 1], prompt_peer(k))

    def a1_copy(h, k):
        return rcopy(sa.at[h, (y + k) % 4], ra1.at[h, k - 1], a1s.at[h, k - 1], a1r.at[h, k - 1], y_peer(k))

    def b1_copy(h, k):
        return rcopy(sb.at[h, (z + k) % 4], rb1.at[h, k - 1], b1s.at[h, k - 1], b1r.at[h, k - 1], z_peer(k))

    def c1_copy(h, k):
        return rcopy(sc.at[h, (x + k) % 4], rc1.at[h, k - 1], c1s.at[h, k - 1], c1r.at[h, k - 1], x_peer(k))

    def a2_copy(h, k):
        return rcopy(sa2.at[h, (z + k) % 4], ra2.at[h, k - 1], a2s.at[h, k - 1], a2r.at[h, k - 1], z_peer(k))

    def b2_copy(h, k):
        return rcopy(sb2.at[h, (y + k) % 4], rb2.at[h, k - 1], b2s.at[h, k - 1], b2r.at[h, k - 1], y_peer(k))

    def c2_copy(h, k):
        return rcopy(sc2.at[h, (z + k) % 4], rc2.at[h, k - 1], c2s.at[h, k - 1], c2r.at[h, k - 1], z_peer(k))

    def x3_copy(h, k):
        return rcopy(s3.at[h, (x + k) % 2], r3.at[h, k - 1], x3s.at[h, k - 1], x3r.at[h, k - 1], x_peer(k))

    def c3_copy(h, slot):
        k = slot + 1 if slot < 3 else slot - 3
        dev = y_peer(k) if slot < 3 else cross_peer(k)
        return rcopy(c3.at[h, (y + k) % 4], rc3.at[h, slot], c3s.at[h, slot], c3r.at[h, slot], dev)

    def finish(h):
        cols = pl.ds(pl.multiple_of(h * 128, 128), 128)
        for t in range(8):
            pgs[h, t, :, pl.ds(0, 128)] = (dk[pl.ds(t * 64, 64)] * SCALE).astype(BF16)
            pgs[h, t, :, pl.ds(128, 128)] = dv[pl.ds(t * 64, 64)].astype(BF16)
        for k in range(1, 8):
            pg_copy(h, k).start()
        g_b[h, pl.ds(0, 512), pl.ds(0, 128)] = head_backward(
            dk[own] * SCALE, oraw[:, cols], ocos[...], osin[...]
        ).astype(BF16)
        g_b[h, pl.ds(0, 512), pl.ds(128, 128)] = dv[own].astype(BF16)
        g_copy(h, 0).start()

        @pl.when(h > 0)
        def _():
            for k in range(1, 4):
                a1_copy(h - 1, k).start()


    def prompt_rows(h):
        cols = pl.ds(pl.multiple_of(h * 128, 128), 128)
        total = pgs[h, pr].astype(F32)
        for k in range(1, 8):
            pg_copy(h, k).wait_recv()
            total = total + pgr[h, k - 1].astype(F32)
        g_b[h, pl.ds(1024, 64), pl.ds(0, 128)] = head_backward(
            total[:, :128], praw[:, cols], cos_t[prow, :], sin_t[prow, :]
        ).astype(BF16)
        g_b[h, pl.ds(1024, 64), pl.ds(128, 128)] = total[:, 128:].astype(BF16)
        g_copy(h, 1).start()

    def emit(h, seg, out):
        out = out.astype(BF16)
        for zz in range(4):
            for xx in range(2):
                at = zz * 128 + xx * 64
                sa[h, seg, zz, xx] = out[at : at + 48, :128]
                sb[h, zz, seg, xx] = out[at : at + 48, 128:]
                sc[h, xx, zz, seg] = out[at + 48 : at + 64, :128]
                sc[h, xx + 2, zz, seg] = out[at + 48 : at + 64, 128:]

    def contract(h):
        g_copy(h, 0).wait_recv()
        g_copy(h, 1).wait_recv()

        def segment(seg, carry):
            rows = pl.ds(pl.multiple_of(seg * 512, 512), 512)
            emit(h, seg, jnp.dot(xt[rows, :], g_b[h], preferred_element_type=F32))
            return carry

        lax.fori_loop(0, 4, segment, 0)
        for k in range(1, 4):
            b1_copy(h, k).start()
            c1_copy(h, k).start()

    def contract_last(h):
        g_copy(h, 0).wait_recv()

        def responses(seg, carry):
            rows = pl.ds(pl.multiple_of(seg * 512, 512), 512)
            cols = pl.ds(pl.multiple_of(seg * 256, 256), 256)
            oraw[:, cols] = jnp.dot(
                xt[rows, pl.ds(0, 1024)], g_b[h, pl.ds(0, 1024)], preferred_element_type=F32
            )
            return carry

        lax.fori_loop(0, 4, responses, 0)
        second_a(h - 2)
        prompt_rows(h)
        second_bc(h - 1)
        g_copy(h, 1).wait_recv()

        def prompts(i, carry):
            seg = (y + 1 + i) % 4
            rows = pl.ds(pl.multiple_of(seg * 512, 512), 512)
            cols = pl.ds(pl.multiple_of(seg * 256, 256), 256)
            part = jnp.dot(
                xt[rows, pl.ds(1024, 128)], g_b[h, pl.ds(1024, 128)], preferred_element_type=F32
            )
            emit(h, seg, oraw[:, cols] + part)

            @pl.when(i < 3)
            def _():
                a1_copy(h, i + 1).start()

            return carry

        lax.fori_loop(0, 4, prompts, 0)
        for k in range(1, 4):
            b1_copy(h, k).start()
            c1_copy(h, k).start()

    def four(own_block, got, h):
        return (own_block.astype(F32) + got[h, 0].astype(F32)) + (
            got[h, 1].astype(F32) + got[h, 2].astype(F32)
        )

    def second_bc(h):
        for k in range(1, 4):
            c1_copy(h, k).wait_recv()
        sc2[h] = four(sc[h, x], rc1, h).astype(BF16)
        for k in range(1, 4):
            c2_copy(h, k).start()
        for k in range(1, 4):
            b1_copy(h, k).wait_recv()
        sb2[h] = four(sb[h, z], rb1, h).astype(BF16)
        for k in range(1, 4):
            b2_copy(h, k).start()

    def second_a(h):
        for k in range(1, 4):
            a1_copy(h, k).wait_recv()
        sa2[h] = four(sa[h, y], ra1, h).astype(BF16)
        for k in range(1, 4):
            a2_copy(h, k).start()

    def third(h):
        for k in range(1, 4):
            c2_copy(h, k).wait_recv()
        c3[h] = four(sc2[h, z], rc2, h).astype(BF16)
        for slot in range(7):
            c3_copy(h, slot).start()
        for k in range(1, 4):
            a2_copy(h, k).wait_recv()
            b2_copy(h, k).wait_recv()
        s3[h, :, 0] = four(sa2[h, z], ra2, h).astype(BF16)
        s3[h, :, 1] = four(sb2[h, y], rb2, h).astype(BF16)
        for k in range(1, 4):
            x3_copy(h, k).start()

    def output(h):
        cols = pl.ds(pl.multiple_of(h * 128, 128), 128)
        for slot in range(7):
            c3_copy(h, slot).wait_recv()
        mine = four(c3[h, y], rc3, h)
        other = (rc3[h, 3].astype(F32) + rc3[h, 4].astype(F32)) + (
            rc3[h, 5].astype(F32) + rc3[h, 6].astype(F32)
        )
        gk_o[pl.ds(48, 16), cols] = jnp.where(grp == 0, mine, other)
        gv_o[pl.ds(48, 16), cols] = jnp.where(grp == 0, other, mine)
        for k in range(1, 4):
            x3_copy(h, k).wait_recv()
        total = four(s3[h, xlo], r3, h)
        gk_o[pl.ds(0, 48), cols] = total[0]
        gv_o[pl.ds(0, 48), cols] = total[1]

    def head(h, carry):
        kt[...] = kv[:, pl.ds(pl.multiple_of(h * 128, 128), 128)].T
        attend(h, 3)

        @pl.when(h > 2)
        def _():
            second_a(h - 3)

        attend(h, 2)
        attend(h, 1)

        @pl.when(h > 0)
        def _():
            prompt_rows(h - 1)

        @pl.when(h > 1)
        def _():
            second_bc(h - 2)

        attend(h, 0)

        @pl.when(h > 2)
        def _():
            third(h - 3)

        @pl.when(h > 0)
        def _():
            contract(h - 1)

        finish(h)
        return carry

    def wrap(h, carry):
        output(h)
        for part in range(2):
            g_copy(h, part).wait_send()
        for k in range(1, 8):
            pg_copy(h, k).wait_send()
            c3_copy(h, k - 1).wait_send()
        for k in range(1, 4):
            for copy in (a1_copy, b1_copy, c1_copy, a2_copy, b2_copy, c2_copy, x3_copy):
                copy(h, k).wait_send()
        return carry

    lax.fori_loop(0, KVH, head, 0)
    contract_last(3)
    third(1)
    second_a(2)
    for slot in range(11):
        stat_copy(slot).wait_send()
    for k in range(4):
        gather(k).wait_send()
    for k in range(1, 4):
        forward(k).wait_send()
    for seg in range(4):
        for copy in x_remote(seg):
            copy.wait_send()
    lax.fori_loop(0, 1, wrap, 0)
    second_bc(3)
    second_a(3)
    third(2)
    lax.fori_loop(1, 2, wrap, 0)
    third(3)
    lax.fori_loop(2, KVH, wrap, 0)


def body(
    prompt_states, response_states, queries, grad_output, key_weight, value_weight,
    rewards, lengths, group_ids,
):
    cosine, sine = rotary_tables()
    hbm = pl.BlockSpec(memory_space=pltpu.HBM)
    vmem = pl.BlockSpec(memory_space=pltpu.VMEM)
    dma = pltpu.SemaphoreType.DMA
    scratch = [
        pltpu.VMEM((PSH, D), BF16),
        pltpu.VMEM((RLEN, D), BF16),
        pltpu.VMEM((D, 1024), BF16),
        pltpu.VMEM((PLEN + RLEN, 128), F32),
        pltpu.VMEM((PLEN + RLEN, 128), F32),
        pltpu.VMEM((576, 2048), BF16),
        pltpu.VMEM((2048, 1152), BF16),
        pltpu.VMEM((PSH, 1024), F32),
        pltpu.VMEM((RLEN, 1024), F32),
        pltpu.VMEM((1024, 1024), BF16),
        pltpu.VMEM((128, 1024), BF16),
        pltpu.VMEM((1024, 128), F32),
        pltpu.VMEM((1024, 128), F32),
        pltpu.VMEM((KVH, 1152, 256), BF16),
        pltpu.VMEM((KVH, 8, PSH, 256), BF16),
        pltpu.VMEM((KVH, 7, PSH, 256), BF16),
        pltpu.VMEM((KVH, 4, 4, 2, 48, 128), BF16),
        pltpu.VMEM((KVH, 4, 4, 2, 48, 128), BF16),
        pltpu.VMEM((KVH, 4, 4, 4, 16, 128), BF16),
        pltpu.VMEM((KVH, 3, 4, 2, 48, 128), BF16),
        pltpu.VMEM((KVH, 3, 4, 2, 48, 128), BF16),
        pltpu.VMEM((KVH, 3, 4, 4, 16, 128), BF16),
        pltpu.VMEM((KVH, 4, 2, 48, 128), BF16),
        pltpu.VMEM((KVH, 4, 2, 48, 128), BF16),
        pltpu.VMEM((KVH, 4, 4, 16, 128), BF16),
        pltpu.VMEM((KVH, 3, 2, 48, 128), BF16),
        pltpu.VMEM((KVH, 3, 2, 48, 128), BF16),
        pltpu.VMEM((KVH, 3, 4, 16, 128), BF16),
        pltpu.VMEM((KVH, 2, 2, 48, 128), BF16),
        pltpu.VMEM((KVH, 3, 2, 48, 128), BF16),
        pltpu.VMEM((KVH, 4, 16, 128), BF16),
        pltpu.VMEM((KVH, 7, 16, 128), BF16),
        pltpu.VMEM((3, 8, 128), F32),
        pltpu.VMEM((11, 8, 128), F32),
        dma((10,)), dma((8,)), dma((8,)), dma((7,)), dma((7,)),
        dma((11,)), dma((11,)), dma((KVH, 2)), dma((KVH, 2)), dma((KVH, 7)), dma((KVH, 7)),
        dma((KVH, 7)), dma((KVH, 7)),
    ] + [dma((KVH, 3)) for _ in range(14)]
    dq, gk, gv = pl.pallas_call(
        kernel,
        out_shape=(
            jax.ShapeDtypeStruct((RLEN, 2048), BF16),
            jax.ShapeDtypeStruct((64, 512), F32),
            jax.ShapeDtypeStruct((64, 512), F32),
        ),
        in_specs=[hbm] * 8 + [vmem] * 3,
        out_specs=(vmem, vmem, vmem),
        scratch_shapes=scratch,
        compiler_params=pltpu.CompilerParams(
            collective_id=0, has_side_effects=True, vmem_limit_bytes=51 * 2**20
        ),
        name="surrogate_grad",
    )(
        *[pltpu.with_memory_space_constraint(a, pltpu.HBM) for a in (prompt_states[0], response_states[0, 0], queries[0, 0], grad_output[0, 0])],
        key_weight, value_weight, *[pltpu.with_memory_space_constraint(jnp.asarray(a), pltpu.HBM) for a in (cosine, sine)],
        rewards, lengths, group_ids,
    )
    return dq[None, None], gk, gv


def solution(mesh):
    row = P("grp", ("prompt", "resp"))
    tokens = P("grp", ("prompt", "resp"), None, None)
    return jax.shard_map(
        body,
        mesh=mesh,
        in_specs=(P("grp", "prompt", None), tokens, tokens, tokens, P(), P(), row, row, row),
        out_specs=(tokens, P(("prompt", "resp"), None), P(("prompt", "resp"), None)),
        check_vma=False,
    )
```

```python
import functools
import math

import jax
import jax.numpy as jnp
import numpy as np
from jax import lax
from jax.experimental import pallas as pl
from jax.experimental.pallas import tpu as pltpu
from jax.sharding import PartitionSpec as P

HEAD_DIM = 128
KVH = 4
RLEN = 512
PLEN = 512
PSH = 64
D = 4096
NADV = 8
DBASE = 1024
THETA = 1000000.0
EPS = 1e-06
SCALE = 1.0 / math.sqrt(HEAD_DIM)
EXP2_SCALE = math.log2(math.e) / math.sqrt(HEAD_DIM)

F32 = jnp.float32
BF16 = jnp.bfloat16
NT = (((1,), (1,)), ((), ()))
MESH = pl.DeviceIdType.MESH


def rotary_tables():
    half = HEAD_DIM // 2
    steps = np.arange(half, dtype=np.float32)
    freq = np.power(np.float32(THETA), np.float32(-2.0) * steps / np.float32(2.0 * half))
    positions = np.arange(PLEN + RLEN, dtype=np.float32)
    angle = (positions[:, None] * freq.astype(np.float32)[None, :]).astype(np.float64)
    cosine, sine = np.cos(angle), np.sin(angle)
    return (
        np.concatenate([cosine, cosine], axis=1).astype(np.float32),
        np.concatenate([-sine, sine], axis=1).astype(np.float32),
    )


def finish_head(raw, cosine, sine):
    factor = lax.rsqrt(jnp.mean(raw * raw, axis=-1, keepdims=True) + EPS)
    normed = raw * factor
    return normed * cosine + pltpu.roll(normed, HEAD_DIM // 2, 1) * sine


def head_backward(grad, raw, cosine, sine):
    factor = lax.rsqrt(jnp.mean(raw * raw, axis=-1, keepdims=True) + EPS)
    normed = raw * factor
    unturned = grad * cosine - pltpu.roll(grad, HEAD_DIM // 2, 1) * sine
    inner = jnp.mean(unturned * normed, axis=-1, keepdims=True)
    return factor * (unturned - normed * inner)


def kernel(
    ps_h, st_h, q_h, go_h, wk_h, wv_h, cos_h, sin_h, rew, lens, ids,
    dq_o, gk_o, gv_o,
    ps_v, st_v, w_v, cos_t, sin_t, x_v, xt, praw, oraw, kv, kt, dk, dv,
    g_b, pgs, pgr, sa, sb, sc, ra1, rb1, rc1, sa2, sb2, sc2, ra2, rb2, rc2, s3, r3, c3, rc3,
    st_s, st_r,
    lsem, xs, xr, ags, agr, sts, strr, gs, gr, pss, psr, c3s, c3r,
    a1s, a1r, b1s, b1r, c1s, c1r, a2s, a2r, b2s, b2r, c2s, c2r, x3s, x3r,
):
    grp = lax.axis_index("grp")
    pr = lax.axis_index("prompt")
    rs = lax.axis_index("resp")
    y = pr // 2
    c = pr % 2
    z = rs // 2
    xlo = rs % 2
    x = grp * 2 + xlo

    def prompt_peer(k):
        return (grp, (pr + k) % 8, rs)

    def core_peer():
        return (grp, y * 2 + (1 - c), rs)

    def y_peer(k):
        return (grp, ((y + k) % 4) * 2 + c, rs)

    def z_peer(k):
        return (grp, pr, ((z + k) % 4) * 2 + xlo)

    def x_peer(k):
        other = (x + k) % 4
        return (other // 2, pr, z * 2 + other % 2)

    def cross_peer(k):
        return (1 - grp, ((y + k) % 4) * 2 + c, rs)

    def pair_peer():
        return (grp, pr, z * 2 + (1 - xlo))

    def rcopy(src, dst, send, recv, dev):
        return pltpu.make_async_remote_copy(
            src_ref=src, dst_ref=dst, send_sem=send, recv_sem=recv,
            device_id=dev, device_id_type=MESH,
        )

    loads = [
        pltpu.make_async_copy(ps_h, ps_v, lsem.at[0]),
        pltpu.make_async_copy(wk_h, w_v.at[:, pl.ds(0, 512)], lsem.at[1]),
        pltpu.make_async_copy(wv_h, w_v.at[:, pl.ds(512, 512)], lsem.at[2]),
        pltpu.make_async_copy(st_h, st_v, lsem.at[3]),
        pltpu.make_async_copy(cos_h, cos_t, lsem.at[4]),
        pltpu.make_async_copy(sin_h, sin_t, lsem.at[5]),
    ]
    for load in loads[:3] + loads[4:6]:
        load.start()

    def x_remote(seg):
        cols = pl.ds(pl.multiple_of(seg * 1024 + (1 - c) * 512, 512), 512)
        here = pl.ds(seg * 512, 512)
        return (
            rcopy(st_v.at[:, cols], x_v.at[pl.ds(0, 512), here], xs.at[seg], xr.at[seg], core_peer()),
            rcopy(ps_v.at[:, cols], x_v.at[pl.ds(512, 64), here], xs.at[4 + seg], xr.at[4 + seg], core_peer()),
        )

    barrier = pltpu.get_barrier_semaphore()
    for k in range(1, 8):
        pl.semaphore_signal(barrier, inc=1, device_id=prompt_peer(k), device_id_type=MESH)
    for k in range(1, 4):
        pl.semaphore_signal(barrier, inc=1, device_id=z_peer(k), device_id_type=MESH)
        pl.semaphore_signal(barrier, inc=1, device_id=x_peer(k), device_id_type=MESH)
        pl.semaphore_signal(barrier, inc=1, device_id=cross_peer(k), device_id_type=MESH)
    pl.semaphore_wait(barrier, 16)

    lane = lax.broadcasted_iota(jnp.int32, (8, 128), 1)
    row = lax.broadcasted_iota(jnp.int32, (8, 128), 0)
    reward = jnp.broadcast_to(rew[...], (8, 128))
    onehot = jnp.where(lane == jnp.broadcast_to(ids[...], (8, 128)), 1.0, 0.0).astype(F32)
    st_s[0] = onehot * jnp.where(
        row == 0, 1.0, jnp.where(row == 1, reward, jnp.where(row == 2, reward * reward, 0.0))
    )

    def stat_copy(slot):
        if slot < 7:
            return rcopy(st_s.at[0], st_r.at[slot], sts.at[slot], strr.at[slot], prompt_peer(slot + 1))
        if slot < 10:
            return rcopy(st_s.at[1], st_r.at[slot], sts.at[slot], strr.at[slot], z_peer(slot - 6))
        return rcopy(st_s.at[2], st_r.at[slot], sts.at[slot], strr.at[slot], pair_peer())

    for slot in range(7):
        stat_copy(slot).start()

    loads[0].wait()
    loads[1].wait()
    loads[3].start()

    def prompt_tile(n, carry):
        cols = pl.ds(pl.multiple_of(n * 256, 256), 256)
        praw[:, cols] = jnp.dot(ps_v[...], w_v[:, cols], preferred_element_type=F32)
        return carry

    lax.fori_loop(0, 2, prompt_tile, 0)
    loads[2].wait()
    lax.fori_loop(2, 4, prompt_tile, 0)
    prow = pl.ds(pl.multiple_of(pr * PSH, PSH), PSH)
    loads[4].wait()
    loads[5].wait()
    pcos, psin = cos_t[prow, :], sin_t[prow, :]
    for h in range(KVH):
        cols = pl.ds(h * 128, 128)
        kv[prow, cols] = finish_head(praw[:, cols], pcos, psin).astype(BF16)
    kv[prow, pl.ds(512, 512)] = praw[:, pl.ds(512, 512)].astype(BF16)

    def shard(index):
        return kv.at[pl.ds(pl.multiple_of(index * PSH, PSH), PSH)]

    def y_shard(k, core):
        return shard(((y + 4 - k) % 4) * 2 + core)

    def gather(k):
        dev = core_peer() if k == 0 else y_peer(k)
        return rcopy(shard(pr), shard(pr), ags.at[k], agr.at[k], dev)

    def gathered(k):
        theirs = shard(y * 2 + (1 - c)) if k == 0 else y_shard(k, c)
        return rcopy(theirs, theirs, ags.at[k], agr.at[k], core_peer())

    def forward(k):
        return rcopy(y_shard(k, c), y_shard(k, c), ags.at[3 + k], agr.at[3 + k], core_peer())

    def forwarded(k):
        theirs = y_shard(k, 1 - c)
        return rcopy(theirs, theirs, ags.at[3 + k], agr.at[3 + k], core_peer())

    for k in (1, 2, 3, 0):
        gather(k).start()

    for slot in range(7):
        stat_copy(slot).wait_recv()
    st_s[1] = st_s[0] + (
        ((st_r[0] + st_r[1]) + (st_r[2] + st_r[3])) + ((st_r[4] + st_r[5]) + st_r[6])
    )
    for slot in range(7, 10):
        stat_copy(slot).start()

    loads[3].wait()
    for seg in range(4):
        for copy in x_remote(seg):
            copy.start()

    def own_tile(n, carry):
        cols = pl.ds(pl.multiple_of(n * 256, 256), 256)
        oraw[:, cols] = jnp.dot(st_v[...], w_v[:, cols], preferred_element_type=F32)
        for t in range(2):
            here = pl.ds(pl.multiple_of(n * 512 + t * 256, 256), 256)
            mine = pl.ds(pl.multiple_of(n * 1024 + c * 512 + t * 256, 256), 256)
            xt[here, pl.ds(0, 512)] = st_v[:, mine].T
        return carry

    lax.fori_loop(0, 4, own_tile, 0)
    late = [
        pltpu.make_async_copy(
            array.at[:, pl.ds(half * 1024, 1024)], w_v.at[pl.ds(base + half * 512, 512)], lsem.at[6 + n * 2 + half]
        )
        for n, (array, base) in enumerate(((go_h, DBASE), (q_h, 0)))
        for half in range(2)
    ]
    for load in late:
        load.start()
    for k in range(1, 4):
        gathered(k).wait_recv()
        forward(k).start()

    for slot in range(7, 10):
        stat_copy(slot).wait_recv()
    st_s[2] = (st_s[1] + st_r[7]) + (st_r[8] + st_r[9])
    stat_copy(10).start()

    own = pl.ds(PLEN, RLEN)
    ocos, osin = cos_t.at[own], sin_t.at[own]

    def own_keys(h, carry):
        cols = pl.ds(pl.multiple_of(h * 128, 128), 128)
        kv[own, cols] = finish_head(oraw[:, cols], ocos[...], osin[...]).astype(BF16)
        return carry

    lax.fori_loop(0, KVH, own_keys, 0)
    kv[own, pl.ds(512, 512)] = oraw[:, pl.ds(512, 512)].astype(BF16)

    for seg in range(4):
        for copy in x_remote(seg):
            copy.wait_recv()

    def turn(n, carry):
        here = pl.ds(pl.multiple_of(n * 256, 256), 256)
        mine = pl.ds(pl.multiple_of((n // 2) * 1024 + c * 512 + (n % 2) * 256, 256), 256)
        xt[here, pl.ds(512, 512)] = x_v[pl.ds(0, 512), here].T
        xt[here, pl.ds(1024, 128)] = jnp.concatenate([ps_v[:, mine], x_v[pl.ds(512, 64), here]], axis=0).T
        return carry

    lax.fori_loop(0, 8, turn, 0)

    stat_copy(10).wait_recv()
    sums = st_s[2] + st_r[10]
    count, total, square = sums[0:1], sums[1:2], sums[2:3]
    members = jnp.maximum(count, 1.0)
    mean = total / members
    spread = jnp.sqrt(jnp.maximum(square / members - mean * mean, 0.0))
    mine = onehot[0:1]
    own_mean = jnp.sum(mine * mean, axis=1, keepdims=True)
    own_spread = jnp.sum(mine * spread, axis=1, keepdims=True)
    advantage = (rew[...] - own_mean) / jnp.maximum(own_spread, 0.5)
    weight = advantage / lens[...].astype(F32)
    token = lax.broadcasted_iota(jnp.int32, (RLEN, 128), 0)
    live = token < jnp.broadcast_to(lens[...], (RLEN, 128))
    coef = jnp.where(live, jnp.broadcast_to(weight, (RLEN, 128)), 0.0)
    for half in range(2):
        late[half].wait()
        rows = pl.ds(DBASE + half * 512, 512)
        for n in range(8):
            cols = pl.ds(n * 128, 128)
            w_v[rows, cols] = (w_v[rows, cols].astype(F32) * coef).astype(BF16)
    late[2].wait()
    late[3].wait()
    gathered(0).wait_recv()
    for k in range(1, 4):
        forwarded(k).wait_recv()

    def attend(h, b):
        count = PLEN + 128 * (b + 1)
        rows = pl.ds(b * 128, 128)
        keys = kv[pl.ds(0, count), pl.ds(pl.multiple_of(h * 128, 128), 128)]
        vals = kv[pl.ds(0, count), pl.ds(pl.multiple_of(512 + h * 128, 128), 128)]
        cols = [pl.ds(pl.multiple_of((h * 4 + j) * 128, 128), 128) for j in range(4)]
        part = [pl.ds(pl.multiple_of((h % 2) * 512 + j * 128, 128), 128) for j in range(4)]
        start = (h // 2) * 512 + b * 128
        qrows = pl.ds(pl.multiple_of(start, 128), 128)
        drows = pl.ds(pl.multiple_of(DBASE + start, 128), 128)
        q = jnp.concatenate([w_v[qrows, cc] for cc in part], axis=0)
        do = jnp.concatenate([w_v[drows, cc] for cc in part], axis=0)
        s = lax.dot_general(keys, q, NT, preferred_element_type=F32)
        key = lax.broadcasted_iota(jnp.int32, (128, 512), 0)
        query = lax.broadcasted_iota(jnp.int32, (128, 512), 1) % 128
        s = jnp.concatenate(
            [s[: count - 128], jnp.where(key <= query, s[count - 128 :], -jnp.inf)], axis=0
        )
        peak = jnp.max(s, axis=0, keepdims=True)
        e = jnp.exp2((s - peak) * EXP2_SCALE)
        inverse = 1.0 / jnp.sum(e, axis=0, keepdims=True)
        dp = lax.dot_general(vals, do, NT, preferred_element_type=F32)
        delta = jnp.sum(e * dp, axis=0, keepdims=True) * inverse
        p = e * inverse
        ds = (p * (dp - delta)).astype(BF16)
        gv = jnp.dot(p.astype(BF16), do, preferred_element_type=F32)
        gk = jnp.dot(ds, q, preferred_element_type=F32)
        if b == 3:
            dv[...] = gv
            dk[...] = gk
        else:
            dv[pl.ds(0, count)] += gv
            dk[pl.ds(0, count)] += gk
        dq = (jnp.dot(kt[:, pl.ds(0, count)], ds, preferred_element_type=F32) * SCALE).T.astype(BF16)
        for j, cc in enumerate(cols):
            dq_o[rows, cc] = dq[j * 128 : (j + 1) * 128]

    def g_copy(h, part):
        mine = (pl.ds(0, 512), pl.ds(1024, 64))[part]
        theirs = (pl.ds(512, 512), pl.ds(1088, 64))[part]
        return rcopy(g_b.at[h, mine], g_b.at[h, theirs], gs.at[h, part], gr.at[h, part], core_peer())

    def pg_copy(h, k):
        return rcopy(pgs.at[h, (pr + k) % 8], pgr.at[h, k - 1], pss.at[h, k - 1], psr.at[h, k - 1], prompt_peer(k))

    def a1_copy(h, k):
        return rcopy(sa.at[h, (y + k) % 4], ra1.at[h, k - 1], a1s.at[h, k - 1], a1r.at[h, k - 1], y_peer(k))

    def b1_copy(h, k):
        return rcopy(sb.at[h, (z + k) % 4], rb1.at[h, k - 1], b1s.at[h, k - 1], b1r.at[h, k - 1], z_peer(k))

    def c1_copy(h, k):
        return rcopy(sc.at[h, (x + k) % 4], rc1.at[h, k - 1], c1s.at[h, k - 1], c1r.at[h, k - 1], x_peer(k))

    def a2_copy(h, k):
        return rcopy(sa2.at[h, (z + k) % 4], ra2.at[h, k - 1], a2s.at[h, k - 1], a2r.at[h, k - 1], z_peer(k))

    def b2_copy(h, k):
        return rcopy(sb2.at[h, (y + k) % 4], rb2.at[h, k - 1], b2s.at[h, k - 1], b2r.at[h, k - 1], y_peer(k))

    def c2_copy(h, k):
        return rcopy(sc2.at[h, (z + k) % 4], rc2.at[h, k - 1], c2s.at[h, k - 1], c2r.at[h, k - 1], z_peer(k))

    def x3_copy(h, k):
        return rcopy(s3.at[h, (x + k) % 2], r3.at[h, k - 1], x3s.at[h, k - 1], x3r.at[h, k - 1], x_peer(k))

    def c3_copy(h, slot):
        k = slot + 1 if slot < 3 else slot - 3
        dev = y_peer(k) if slot < 3 else cross_peer(k)
        return rcopy(c3.at[h, (y + k) % 4], rc3.at[h, slot], c3s.at[h, slot], c3r.at[h, slot], dev)

    def finish(h):
        cols = pl.ds(pl.multiple_of(h * 128, 128), 128)
        for t in range(8):
            pgs[h, t, :, pl.ds(0, 128)] = (dk[pl.ds(t * 64, 64)] * SCALE).astype(BF16)
            pgs[h, t, :, pl.ds(128, 128)] = dv[pl.ds(t * 64, 64)].astype(BF16)
        for k in (4, 3, 5, 2, 6, 1, 7):
            pg_copy(h, k).start()
        g_b[h, pl.ds(0, 512), pl.ds(0, 128)] = head_backward(
            dk[own] * SCALE, oraw[:, cols], ocos[...], osin[...]
        ).astype(BF16)
        g_b[h, pl.ds(0, 512), pl.ds(128, 128)] = dv[own].astype(BF16)
        g_copy(h, 0).start()

        @pl.when(h > 0)
        def _():
            for k in range(1, 4):
                a1_copy(h - 1, k).start()


    def prompt_rows(h):
        cols = pl.ds(pl.multiple_of(h * 128, 128), 128)
        total = pgs[h, pr].astype(F32)
        for k in range(1, 8):
            pg_copy(h, k).wait_recv()
            total = total + pgr[h, k - 1].astype(F32)
        g_b[h, pl.ds(1024, 64), pl.ds(0, 128)] = head_backward(
            total[:, :128], praw[:, cols], cos_t[prow, :], sin_t[prow, :]
        ).astype(BF16)
        g_b[h, pl.ds(1024, 64), pl.ds(128, 128)] = total[:, 128:].astype(BF16)
        g_copy(h, 1).start()

    def emit(h, seg, out):
        out = out.astype(BF16)
        for zz in range(4):
            for xx in range(2):
                at = zz * 128 + xx * 64
                sa[h, seg, zz, xx] = out[at : at + 48, :128]
                sb[h, zz, seg, xx] = out[at : at + 48, 128:]
                sc[h, xx, zz, seg] = out[at + 48 : at + 64, :128]
                sc[h, xx + 2, zz, seg] = out[at + 48 : at + 64, 128:]

    def contract(h):
        g_copy(h, 0).wait_recv()
        g_copy(h, 1).wait_recv()

        def segment(seg, carry):
            rows = pl.ds(pl.multiple_of(seg * 512, 512), 512)
            emit(h, seg, jnp.dot(xt[rows, :], g_b[h], preferred_element_type=F32))
            return carry

        lax.fori_loop(0, 4, segment, 0)
        for k in (2, 1, 3):
            b1_copy(h, k).start()
            c1_copy(h, k).start()

    def contract_last(h):
        g_copy(h, 0).wait_recv()

        def responses(seg, carry):
            rows = pl.ds(pl.multiple_of(seg * 512, 512), 512)
            cols = pl.ds(pl.multiple_of(seg * 256, 256), 256)
            oraw[:, cols] = jnp.dot(
                xt[rows, pl.ds(0, 1024)], g_b[h, pl.ds(0, 1024)], preferred_element_type=F32
            )
            return carry

        lax.fori_loop(0, 4, responses, 0)
        second_a(h - 2)
        prompt_rows(h)
        second_bc(h - 1)
        g_copy(h, 1).wait_recv()

        def prompts(i, carry):
            seg = (y + 2 + i) % 4
            rows = pl.ds(pl.multiple_of(seg * 512, 512), 512)
            cols = pl.ds(pl.multiple_of(seg * 256, 256), 256)
            part = jnp.dot(
                xt[rows, pl.ds(1024, 128)], g_b[h, pl.ds(1024, 128)], preferred_element_type=F32
            )
            emit(h, seg, oraw[:, cols] + part)

            @pl.when(i != 2)
            def _():
                a1_copy(h, (2 + i) % 4).start()

            return carry

        lax.fori_loop(0, 4, prompts, 0)
        for k in (2, 1, 3):
            b1_copy(h, k).start()
            c1_copy(h, k).start()

    def four(own_block, got, h):
        return (own_block.astype(F32) + got[h, 0].astype(F32)) + (
            got[h, 1].astype(F32) + got[h, 2].astype(F32)
        )

    def second_bc(h):
        for k in range(1, 4):
            c1_copy(h, k).wait_recv()
        sc2[h] = four(sc[h, x], rc1, h).astype(BF16)
        for k in (2, 1, 3):
            c2_copy(h, k).start()
        for k in range(1, 4):
            b1_copy(h, k).wait_recv()
        sb2[h] = four(sb[h, z], rb1, h).astype(BF16)
        for k in (2, 1, 3):
            b2_copy(h, k).start()

    def second_a(h):
        for k in range(1, 4):
            a1_copy(h, k).wait_recv()
        sa2[h] = four(sa[h, y], ra1, h).astype(BF16)
        for k in (2, 1, 3):
            a2_copy(h, k).start()

    def third(h):
        for k in range(1, 4):
            c2_copy(h, k).wait_recv()
        c3[h] = four(sc2[h, z], rc2, h).astype(BF16)
        for slot in (5, 4, 6, 1, 3, 0, 2):
            c3_copy(h, slot).start()
        for k in range(1, 4):
            a2_copy(h, k).wait_recv()
            b2_copy(h, k).wait_recv()
        s3[h, :, 0] = four(sa2[h, z], ra2, h).astype(BF16)
        s3[h, :, 1] = four(sb2[h, y], rb2, h).astype(BF16)
        for k in (2, 1, 3):
            x3_copy(h, k).start()

    def output(h):
        cols = pl.ds(pl.multiple_of(h * 128, 128), 128)
        for slot in range(7):
            c3_copy(h, slot).wait_recv()
        mine = four(c3[h, y], rc3, h)
        other = (rc3[h, 3].astype(F32) + rc3[h, 4].astype(F32)) + (
            rc3[h, 5].astype(F32) + rc3[h, 6].astype(F32)
        )
        gk_o[pl.ds(48, 16), cols] = jnp.where(grp == 0, mine, other)
        gv_o[pl.ds(48, 16), cols] = jnp.where(grp == 0, other, mine)
        for k in range(1, 4):
            x3_copy(h, k).wait_recv()
        total = four(s3[h, xlo], r3, h)
        gk_o[pl.ds(0, 48), cols] = total[0]
        gv_o[pl.ds(0, 48), cols] = total[1]

    def head(h, carry):
        kt[...] = kv[:, pl.ds(pl.multiple_of(h * 128, 128), 128)].T
        attend(h, 3)

        @pl.when(h > 2)
        def _():
            second_a(h - 3)

        attend(h, 2)
        attend(h, 1)

        @pl.when(h > 0)
        def _():
            prompt_rows(h - 1)

        @pl.when(h > 1)
        def _():
            second_bc(h - 2)

        attend(h, 0)

        @pl.when(h > 2)
        def _():
            third(h - 3)

        @pl.when(h > 0)
        def _():
            contract(h - 1)

        finish(h)
        return carry

    def wrap(h, carry):
        output(h)
        for part in range(2):
            g_copy(h, part).wait_send()
        for k in range(1, 8):
            pg_copy(h, k).wait_send()
            c3_copy(h, k - 1).wait_send()
        for k in range(1, 4):
            for copy in (a1_copy, b1_copy, c1_copy, a2_copy, b2_copy, c2_copy, x3_copy):
                copy(h, k).wait_send()
        return carry

    lax.fori_loop(0, KVH, head, 0)
    contract_last(3)
    third(1)
    second_a(2)
    for slot in range(11):
        stat_copy(slot).wait_send()
    for k in range(4):
        gather(k).wait_send()
    for k in range(1, 4):
        forward(k).wait_send()
    for seg in range(4):
        for copy in x_remote(seg):
            copy.wait_send()
    lax.fori_loop(0, 1, wrap, 0)
    second_bc(3)
    second_a(3)
    third(2)
    lax.fori_loop(1, 2, wrap, 0)
    third(3)
    lax.fori_loop(2, KVH, wrap, 0)


def body(
    prompt_states, response_states, queries, grad_output, key_weight, value_weight,
    rewards, lengths, group_ids,
):
    cosine, sine = rotary_tables()
    hbm = pl.BlockSpec(memory_space=pltpu.HBM)
    vmem = pl.BlockSpec(memory_space=pltpu.VMEM)
    dma = pltpu.SemaphoreType.DMA
    scratch = [
        pltpu.VMEM((PSH, D), BF16),
        pltpu.VMEM((RLEN, D), BF16),
        pltpu.VMEM((D, 1024), BF16),
        pltpu.VMEM((PLEN + RLEN, 128), F32),
        pltpu.VMEM((PLEN + RLEN, 128), F32),
        pltpu.VMEM((576, 2048), BF16),
        pltpu.VMEM((2048, 1152), BF16),
        pltpu.VMEM((PSH, 1024), F32),
        pltpu.VMEM((RLEN, 1024), F32),
        pltpu.VMEM((1024, 1024), BF16),
        pltpu.VMEM((128, 1024), BF16),
        pltpu.VMEM((1024, 128), F32),
        pltpu.VMEM((1024, 128), F32),
        pltpu.VMEM((KVH, 1152, 256), BF16),
        pltpu.VMEM((KVH, 8, PSH, 256), BF16),
        pltpu.VMEM((KVH, 7, PSH, 256), BF16),
        pltpu.VMEM((KVH, 4, 4, 2, 48, 128), BF16),
        pltpu.VMEM((KVH, 4, 4, 2, 48, 128), BF16),
        pltpu.VMEM((KVH, 4, 4, 4, 16, 128), BF16),
        pltpu.VMEM((KVH, 3, 4, 2, 48, 128), BF16),
        pltpu.VMEM((KVH, 3, 4, 2, 48, 128), BF16),
        pltpu.VMEM((KVH, 3, 4, 4, 16, 128), BF16),
        pltpu.VMEM((KVH, 4, 2, 48, 128), BF16),
        pltpu.VMEM((KVH, 4, 2, 48, 128), BF16),
        pltpu.VMEM((KVH, 4, 4, 16, 128), BF16),
        pltpu.VMEM((KVH, 3, 2, 48, 128), BF16),
        pltpu.VMEM((KVH, 3, 2, 48, 128), BF16),
        pltpu.VMEM((KVH, 3, 4, 16, 128), BF16),
        pltpu.VMEM((KVH, 2, 2, 48, 128), BF16),
        pltpu.VMEM((KVH, 3, 2, 48, 128), BF16),
        pltpu.VMEM((KVH, 4, 16, 128), BF16),
        pltpu.VMEM((KVH, 7, 16, 128), BF16),
        pltpu.VMEM((3, 8, 128), F32),
        pltpu.VMEM((11, 8, 128), F32),
        dma((10,)), dma((8,)), dma((8,)), dma((7,)), dma((7,)),
        dma((11,)), dma((11,)), dma((KVH, 2)), dma((KVH, 2)), dma((KVH, 7)), dma((KVH, 7)),
        dma((KVH, 7)), dma((KVH, 7)),
    ] + [dma((KVH, 3)) for _ in range(14)]
    dq, gk, gv = pl.pallas_call(
        kernel,
        out_shape=(
            jax.ShapeDtypeStruct((RLEN, 2048), BF16),
            jax.ShapeDtypeStruct((64, 512), F32),
            jax.ShapeDtypeStruct((64, 512), F32),
        ),
        in_specs=[hbm] * 8 + [vmem] * 3,
        out_specs=(vmem, vmem, vmem),
        scratch_shapes=scratch,
        compiler_params=pltpu.CompilerParams(
            collective_id=0, has_side_effects=True, vmem_limit_bytes=51 * 2**20
        ),
        name="surrogate_grad",
    )(
        *[pltpu.with_memory_space_constraint(a, pltpu.HBM) for a in (prompt_states[0], response_states[0, 0], queries[0, 0], grad_output[0, 0])],
        key_weight, value_weight, *[pltpu.with_memory_space_constraint(jnp.asarray(a), pltpu.HBM) for a in (cosine, sine)],
        rewards, lengths, group_ids,
    )
    return dq[None, None], gk, gv


def solution(mesh):
    row = P("grp", ("prompt", "resp"))
    tokens = P("grp", ("prompt", "resp"), None, None)
    return jax.shard_map(
        body,
        mesh=mesh,
        in_specs=(P("grp", "prompt", None), tokens, tokens, tokens, P(), P(), row, row, row),
        out_specs=(tokens, P(("prompt", "resp"), None), P(("prompt", "resp"), None)),
        check_vma=False,
    )
```

```python
import functools
import math

import jax
import jax.numpy as jnp
import numpy as np
from jax import lax
from jax.experimental import pallas as pl
from jax.experimental.pallas import tpu as pltpu
from jax.sharding import PartitionSpec as P

HEAD_DIM = 128
KVH = 4
RLEN = 512
PLEN = 512
PSH = 64
D = 4096
NADV = 8
DBASE = 1024
THETA = 1000000.0
EPS = 1e-06
SCALE = 1.0 / math.sqrt(HEAD_DIM)
EXP2_SCALE = math.log2(math.e) / math.sqrt(HEAD_DIM)

F32 = jnp.float32
BF16 = jnp.bfloat16
NT = (((1,), (1,)), ((), ()))
MESH = pl.DeviceIdType.MESH


def rotary_tables():
    half = HEAD_DIM // 2
    steps = np.arange(half, dtype=np.float32)
    freq = np.power(np.float32(THETA), np.float32(-2.0) * steps / np.float32(2.0 * half))
    positions = np.arange(PLEN + RLEN, dtype=np.float32)
    angle = (positions[:, None] * freq.astype(np.float32)[None, :]).astype(np.float64)
    cosine, sine = np.cos(angle), np.sin(angle)
    return (
        np.concatenate([cosine, cosine], axis=1).astype(np.float32),
        np.concatenate([-sine, sine], axis=1).astype(np.float32),
    )


def finish_head(raw, cosine, sine):
    factor = lax.rsqrt(jnp.mean(raw * raw, axis=-1, keepdims=True) + EPS)
    normed = raw * factor
    return normed * cosine + pltpu.roll(normed, HEAD_DIM // 2, 1) * sine


def head_backward(grad, raw, cosine, sine):
    factor = lax.rsqrt(jnp.mean(raw * raw, axis=-1, keepdims=True) + EPS)
    normed = raw * factor
    unturned = grad * cosine - pltpu.roll(grad, HEAD_DIM // 2, 1) * sine
    inner = jnp.mean(unturned * normed, axis=-1, keepdims=True)
    return factor * (unturned - normed * inner)


def kernel(
    ps_h, st_h, q_h, go_h, wk_h, wv_h, cos_h, sin_h, rew, lens, ids,
    dq_o, gk_o, gv_o,
    ps_v, st_v, w_v, cos_t, sin_t, x_v, xt, praw, oraw, kv, kt, dk, dv,
    g_b, pgs, pgr, sa, sb, sc, ra1, rb1, rc1, sa2, sb2, sc2, ra2, rb2, rc2, s3, r3, c3, rc3,
    st_s, st_r,
    lsem, xs, xr, ags, agr, sts, strr, gs, gr, pss, psr, c3s, c3r,
    a1s, a1r, b1s, b1r, c1s, c1r, a2s, a2r, b2s, b2r, c2s, c2r, x3s, x3r,
):
    grp = lax.axis_index("grp")
    pr = lax.axis_index("prompt")
    rs = lax.axis_index("resp")
    y = pr // 2
    c = pr % 2
    z = rs // 2
    xlo = rs % 2
    x = grp * 2 + xlo

    def prompt_peer(k):
        return (grp, (pr + k) % 8, rs)

    def core_peer():
        return (grp, y * 2 + (1 - c), rs)

    def y_peer(k):
        return (grp, ((y + k) % 4) * 2 + c, rs)

    def z_peer(k):
        return (grp, pr, ((z + k) % 4) * 2 + xlo)

    def x_peer(k):
        other = (x + k) % 4
        return (other // 2, pr, z * 2 + other % 2)

    def cross_peer(k):
        return (1 - grp, ((y + k) % 4) * 2 + c, rs)

    def pair_peer():
        return (grp, pr, z * 2 + (1 - xlo))

    def rcopy(src, dst, send, recv, dev):
        return pltpu.make_async_remote_copy(
            src_ref=src, dst_ref=dst, send_sem=send, recv_sem=recv,
            device_id=dev, device_id_type=MESH,
        )

    loads = [
        pltpu.make_async_copy(ps_h, ps_v, lsem.at[0]),
        pltpu.make_async_copy(wk_h, w_v.at[:, pl.ds(0, 512)], lsem.at[1]),
        pltpu.make_async_copy(wv_h, w_v.at[:, pl.ds(512, 512)], lsem.at[2]),
        pltpu.make_async_copy(st_h, st_v, lsem.at[3]),
        pltpu.make_async_copy(cos_h, cos_t, lsem.at[4]),
        pltpu.make_async_copy(sin_h, sin_t, lsem.at[5]),
    ]
    for load in loads[:3] + loads[4:6]:
        load.start()

    def x_remote(seg):
        cols = pl.ds(pl.multiple_of(seg * 1024 + (1 - c) * 512, 512), 512)
        here = pl.ds(seg * 512, 512)
        return (
            rcopy(st_v.at[:, cols], x_v.at[pl.ds(0, 512), here], xs.at[seg], xr.at[seg], core_peer()),
            rcopy(ps_v.at[:, cols], x_v.at[pl.ds(512, 64), here], xs.at[4 + seg], xr.at[4 + seg], core_peer()),
        )

    barrier = pltpu.get_barrier_semaphore()
    for k in range(1, 8):
        pl.semaphore_signal(barrier, inc=1, device_id=prompt_peer(k), device_id_type=MESH)
    for k in range(1, 4):
        pl.semaphore_signal(barrier, inc=1, device_id=z_peer(k), device_id_type=MESH)
        pl.semaphore_signal(barrier, inc=1, device_id=x_peer(k), device_id_type=MESH)
        pl.semaphore_signal(barrier, inc=1, device_id=cross_peer(k), device_id_type=MESH)
    pl.semaphore_wait(barrier, 16)

    lane = lax.broadcasted_iota(jnp.int32, (8, 128), 1)
    row = lax.broadcasted_iota(jnp.int32, (8, 128), 0)
    reward = jnp.broadcast_to(rew[...], (8, 128))
    onehot = jnp.where(lane == jnp.broadcast_to(ids[...], (8, 128)), 1.0, 0.0).astype(F32)
    st_s[0] = onehot * jnp.where(
        row == 0, 1.0, jnp.where(row == 1, reward, jnp.where(row == 2, reward * reward, 0.0))
    )

    def stat_copy(slot):
        if slot < 7:
            return rcopy(st_s.at[0], st_r.at[slot], sts.at[slot], strr.at[slot], prompt_peer(slot + 1))
        if slot < 10:
            return rcopy(st_s.at[1], st_r.at[slot], sts.at[slot], strr.at[slot], z_peer(slot - 6))
        return rcopy(st_s.at[2], st_r.at[slot], sts.at[slot], strr.at[slot], pair_peer())

    for slot in range(7):
        stat_copy(slot).start()

    loads[0].wait()
    loads[1].wait()
    loads[3].start()

    def prompt_tile(n, carry):
        cols = pl.ds(pl.multiple_of(n * 256, 256), 256)
        praw[:, cols] = jnp.dot(ps_v[...], w_v[:, cols], preferred_element_type=F32)
        return carry

    lax.fori_loop(0, 2, prompt_tile, 0)
    loads[2].wait()
    lax.fori_loop(2, 4, prompt_tile, 0)
    prow = pl.ds(pl.multiple_of(pr * PSH, PSH), PSH)
    loads[4].wait()
    loads[5].wait()
    pcos, psin = cos_t[prow, :], sin_t[prow, :]
    for h in range(KVH):
        cols = pl.ds(h * 128, 128)
        kv[prow, cols] = finish_head(praw[:, cols], pcos, psin).astype(BF16)
    kv[prow, pl.ds(512, 512)] = praw[:, pl.ds(512, 512)].astype(BF16)

    def shard(index):
        return kv.at[pl.ds(pl.multiple_of(index * PSH, PSH), PSH)]

    def y_shard(k, core):
        return shard(((y + 4 - k) % 4) * 2 + core)

    def gather(k):
        dev = core_peer() if k == 0 else y_peer(k)
        return rcopy(shard(pr), shard(pr), ags.at[k], agr.at[k], dev)

    def gathered(k):
        theirs = shard(y * 2 + (1 - c)) if k == 0 else y_shard(k, c)
        return rcopy(theirs, theirs, ags.at[k], agr.at[k], core_peer())

    def forward(k):
        return rcopy(y_shard(k, c), y_shard(k, c), ags.at[3 + k], agr.at[3 + k], core_peer())

    def forwarded(k):
        theirs = y_shard(k, 1 - c)
        return rcopy(theirs, theirs, ags.at[3 + k], agr.at[3 + k], core_peer())

    for k in (2, 1, 3, 0):
        gather(k).start()

    for slot in range(7):
        stat_copy(slot).wait_recv()
    st_s[1] = st_s[0] + (
        ((st_r[0] + st_r[1]) + (st_r[2] + st_r[3])) + ((st_r[4] + st_r[5]) + st_r[6])
    )
    for slot in range(7, 10):
        stat_copy(slot).start()

    loads[3].wait()
    for seg in range(4):
        for copy in x_remote(seg):
            copy.start()

    def own_tile(n, carry):
        cols = pl.ds(pl.multiple_of(n * 256, 256), 256)
        oraw[:, cols] = jnp.dot(st_v[...], w_v[:, cols], preferred_element_type=F32)
        for t in range(2):
            here = pl.ds(pl.multiple_of(n * 512 + t * 256, 256), 256)
            mine = pl.ds(pl.multiple_of(n * 1024 + c * 512 + t * 256, 256), 256)
            xt[here, pl.ds(0, 512)] = st_v[:, mine].T
        return carry

    lax.fori_loop(0, 4, own_tile, 0)
    late = [
        pltpu.make_async_copy(
            array.at[:, pl.ds(half * 1024, 1024)], w_v.at[pl.ds(base + half * 512, 512)], lsem.at[6 + n * 2 + half]
        )
        for n, (array, base) in enumerate(((go_h, DBASE), (q_h, 0)))
        for half in range(2)
    ]
    for load in late:
        load.start()
    for k in (1, 3, 2):
        gathered(k).wait_recv()
        forward(k).start()

    for slot in range(7, 10):
        stat_copy(slot).wait_recv()
    st_s[2] = (st_s[1] + st_r[7]) + (st_r[8] + st_r[9])
    stat_copy(10).start()

    own = pl.ds(PLEN, RLEN)
    ocos, osin = cos_t.at[own], sin_t.at[own]

    def own_keys(h, carry):
        cols = pl.ds(pl.multiple_of(h * 128, 128), 128)
        kv[own, cols] = finish_head(oraw[:, cols], ocos[...], osin[...]).astype(BF16)
        return carry

    lax.fori_loop(0, KVH, own_keys, 0)
    kv[own, pl.ds(512, 512)] = oraw[:, pl.ds(512, 512)].astype(BF16)

    for seg in range(4):
        for copy in x_remote(seg):
            copy.wait_recv()

    def turn(n, carry):
        here = pl.ds(pl.multiple_of(n * 256, 256), 256)
        mine = pl.ds(pl.multiple_of((n // 2) * 1024 + c * 512 + (n % 2) * 256, 256), 256)
        xt[here, pl.ds(512, 512)] = x_v[pl.ds(0, 512), here].T
        xt[here, pl.ds(1024, 128)] = jnp.concatenate([ps_v[:, mine], x_v[pl.ds(512, 64), here]], axis=0).T
        return carry

    lax.fori_loop(0, 8, turn, 0)

    stat_copy(10).wait_recv()
    sums = st_s[2] + st_r[10]
    count, total, square = sums[0:1], sums[1:2], sums[2:3]
    members = jnp.maximum(count, 1.0)
    mean = total / members
    spread = jnp.sqrt(jnp.maximum(square / members - mean * mean, 0.0))
    mine = onehot[0:1]
    own_mean = jnp.sum(mine * mean, axis=1, keepdims=True)
    own_spread = jnp.sum(mine * spread, axis=1, keepdims=True)
    advantage = (rew[...] - own_mean) / jnp.maximum(own_spread, 0.5)
    weight = advantage / lens[...].astype(F32)
    token = lax.broadcasted_iota(jnp.int32, (RLEN, 128), 0)
    live = token < jnp.broadcast_to(lens[...], (RLEN, 128))
    coef = jnp.where(live, jnp.broadcast_to(weight, (RLEN, 128)), 0.0)
    for half in range(2):
        late[half].wait()
        rows = pl.ds(DBASE + half * 512, 512)
        for n in range(8):
            cols = pl.ds(n * 128, 128)
            w_v[rows, cols] = (w_v[rows, cols].astype(F32) * coef).astype(BF16)
    late[2].wait()
    late[3].wait()
    gathered(0).wait_recv()
    for k in range(1, 4):
        forwarded(k).wait_recv()

    def attend(h, b):
        count = PLEN + 128 * (b + 1)
        rows = pl.ds(b * 128, 128)
        keys = kv[pl.ds(0, count), pl.ds(pl.multiple_of(h * 128, 128), 128)]
        vals = kv[pl.ds(0, count), pl.ds(pl.multiple_of(512 + h * 128, 128), 128)]
        cols = [pl.ds(pl.multiple_of((h * 4 + j) * 128, 128), 128) for j in range(4)]
        part = [pl.ds(pl.multiple_of((h % 2) * 512 + j * 128, 128), 128) for j in range(4)]
        start = (h // 2) * 512 + b * 128
        qrows = pl.ds(pl.multiple_of(start, 128), 128)
        drows = pl.ds(pl.multiple_of(DBASE + start, 128), 128)
        q = jnp.concatenate([w_v[qrows, cc] for cc in part], axis=0)
        do = jnp.concatenate([w_v[drows, cc] for cc in part], axis=0)
        s = lax.dot_general(keys, q, NT, preferred_element_type=F32)
        key = lax.broadcasted_iota(jnp.int32, (128, 512), 0)
        query = lax.broadcasted_iota(jnp.int32, (128, 512), 1) % 128
        s = jnp.concatenate(
            [s[: count - 128], jnp.where(key <= query, s[count - 128 :], -jnp.inf)], axis=0
        )
        peak = jnp.max(s, axis=0, keepdims=True)
        e = jnp.exp2((s - peak) * EXP2_SCALE)
        inverse = 1.0 / jnp.sum(e, axis=0, keepdims=True)
        dp = lax.dot_general(vals, do, NT, preferred_element_type=F32)
        delta = jnp.sum(e * dp, axis=0, keepdims=True) * inverse
        p = e * inverse
        ds = (p * (dp - delta)).astype(BF16)
        gv = jnp.dot(p.astype(BF16), do, preferred_element_type=F32)
        gk = jnp.dot(ds, q, preferred_element_type=F32)
        if b == 3:
            dv[...] = gv
            dk[...] = gk
        else:
            dv[pl.ds(0, count)] += gv
            dk[pl.ds(0, count)] += gk
        dq = (jnp.dot(kt[:, pl.ds(0, count)], ds, preferred_element_type=F32) * SCALE).T.astype(BF16)
        for j, cc in enumerate(cols):
            dq_o[rows, cc] = dq[j * 128 : (j + 1) * 128]

    def g_copy(h, part):
        mine = (pl.ds(0, 512), pl.ds(1024, 64))[part]
        theirs = (pl.ds(512, 512), pl.ds(1088, 64))[part]
        return rcopy(g_b.at[h, mine], g_b.at[h, theirs], gs.at[h, part], gr.at[h, part], core_peer())

    def pg_copy(h, k):
        return rcopy(pgs.at[h, (pr + k) % 8], pgr.at[h, k - 1], pss.at[h, k - 1], psr.at[h, k - 1], prompt_peer(k))

    def a1_copy(h, k):
        return rcopy(sa.at[h, (y + k) % 4], ra1.at[h, k - 1], a1s.at[h, k - 1], a1r.at[h, k - 1], y_peer(k))

    def b1_copy(h, k):
        return rcopy(sb.at[h, (z + k) % 4], rb1.at[h, k - 1], b1s.at[h, k - 1], b1r.at[h, k - 1], z_peer(k))

    def c1_copy(h, k):
        return rcopy(sc.at[h, (x + k) % 4], rc1.at[h, k - 1], c1s.at[h, k - 1], c1r.at[h, k - 1], x_peer(k))

    def a2_copy(h, k):
        return rcopy(sa2.at[h, (z + k) % 4], ra2.at[h, k - 1], a2s.at[h, k - 1], a2r.at[h, k - 1], z_peer(k))

    def b2_copy(h, k):
        return rcopy(sb2.at[h, (y + k) % 4], rb2.at[h, k - 1], b2s.at[h, k - 1], b2r.at[h, k - 1], y_peer(k))

    def c2_copy(h, k):
        return rcopy(sc2.at[h, (z + k) % 4], rc2.at[h, k - 1], c2s.at[h, k - 1], c2r.at[h, k - 1], z_peer(k))

    def x3_copy(h, k):
        return rcopy(s3.at[h, (x + k) % 2], r3.at[h, k - 1], x3s.at[h, k - 1], x3r.at[h, k - 1], x_peer(k))

    def c3_copy(h, slot):
        k = slot + 1 if slot < 3 else slot - 3
        dev = y_peer(k) if slot < 3 else cross_peer(k)
        return rcopy(c3.at[h, (y + k) % 4], rc3.at[h, slot], c3s.at[h, slot], c3r.at[h, slot], dev)

    def finish(h):
        cols = pl.ds(pl.multiple_of(h * 128, 128), 128)
        for t in range(8):
            pgs[h, t, :, pl.ds(0, 128)] = (dk[pl.ds(t * 64, 64)] * SCALE).astype(BF16)
            pgs[h, t, :, pl.ds(128, 128)] = dv[pl.ds(t * 64, 64)].astype(BF16)
        for k in (4, 3, 5, 2, 6, 1, 7):
            pg_copy(h, k).start()
        g_b[h, pl.ds(0, 512), pl.ds(0, 128)] = head_backward(
            dk[own] * SCALE, oraw[:, cols], ocos[...], osin[...]
        ).astype(BF16)
        g_b[h, pl.ds(0, 512), pl.ds(128, 128)] = dv[own].astype(BF16)
        g_copy(h, 0).start()

        @pl.when(h > 0)
        def _():
            for k in range(1, 4):
                a1_copy(h - 1, k).start()


    def prompt_rows(h):
        cols = pl.ds(pl.multiple_of(h * 128, 128), 128)
        total = pgs[h, pr].astype(F32)
        for k in range(1, 8):
            pg_copy(h, k).wait_recv()
            total = total + pgr[h, k - 1].astype(F32)
        g_b[h, pl.ds(1024, 64), pl.ds(0, 128)] = head_backward(
            total[:, :128], praw[:, cols], cos_t[prow, :], sin_t[prow, :]
        ).astype(BF16)
        g_b[h, pl.ds(1024, 64), pl.ds(128, 128)] = total[:, 128:].astype(BF16)
        g_copy(h, 1).start()

    def emit(h, seg, out):
        out = out.astype(BF16)
        for zz in range(4):
            for xx in range(2):
                at = zz * 128 + xx * 64
                sa[h, seg, zz, xx] = out[at : at + 48, :128]
                sb[h, zz, seg, xx] = out[at : at + 48, 128:]
                sc[h, xx, zz, seg] = out[at + 48 : at + 64, :128]
                sc[h, xx + 2, zz, seg] = out[at + 48 : at + 64, 128:]

    def contract(h):
        g_copy(h, 0).wait_recv()
        g_copy(h, 1).wait_recv()

        def segment(seg, carry):
            rows = pl.ds(pl.multiple_of(seg * 512, 512), 512)
            emit(h, seg, jnp.dot(xt[rows, :], g_b[h], preferred_element_type=F32))
            return carry

        lax.fori_loop(0, 4, segment, 0)
        for k in (2, 1, 3):
            b1_copy(h, k).start()
            c1_copy(h, k).start()

    def contract_last(h):
        g_copy(h, 0).wait_recv()

        def responses(seg, carry):
            rows = pl.ds(pl.multiple_of(seg * 512, 512), 512)
            cols = pl.ds(pl.multiple_of(seg * 256, 256), 256)
            oraw[:, cols] = jnp.dot(
                xt[rows, pl.ds(0, 1024)], g_b[h, pl.ds(0, 1024)], preferred_element_type=F32
            )
            return carry

        lax.fori_loop(0, 4, responses, 0)
        second_a(h - 2)
        prompt_rows(h)
        second_bc(h - 1)
        g_copy(h, 1).wait_recv()

        def prompts(i, carry):
            seg = (y + 2 + i) % 4
            rows = pl.ds(pl.multiple_of(seg * 512, 512), 512)
            cols = pl.ds(pl.multiple_of(seg * 256, 256), 256)
            part = jnp.dot(
                xt[rows, pl.ds(1024, 128)], g_b[h, pl.ds(1024, 128)], preferred_element_type=F32
            )
            emit(h, seg, oraw[:, cols] + part)

            @pl.when(i != 2)
            def _():
                a1_copy(h, (2 + i) % 4).start()

            return carry

        lax.fori_loop(0, 4, prompts, 0)
        for k in (2, 1, 3):
            b1_copy(h, k).start()
            c1_copy(h, k).start()

    def four(own_block, got, h):
        return (own_block.astype(F32) + got[h, 0].astype(F32)) + (
            got[h, 1].astype(F32) + got[h, 2].astype(F32)
        )

    def second_bc(h):
        for k in range(1, 4):
            c1_copy(h, k).wait_recv()
        sc2[h] = four(sc[h, x], rc1, h).astype(BF16)
        for k in (2, 1, 3):
            c2_copy(h, k).start()
        for k in range(1, 4):
            b1_copy(h, k).wait_recv()
        sb2[h] = four(sb[h, z], rb1, h).astype(BF16)
        for k in (2, 1, 3):
            b2_copy(h, k).start()

    def second_a(h):
        for k in range(1, 4):
            a1_copy(h, k).wait_recv()
        sa2[h] = four(sa[h, y], ra1, h).astype(BF16)
        for k in (2, 1, 3):
            a2_copy(h, k).start()

    def third(h):
        for k in range(1, 4):
            c2_copy(h, k).wait_recv()
        c3[h] = four(sc2[h, z], rc2, h).astype(BF16)
        for slot in (5, 4, 6, 1, 3, 0, 2):
            c3_copy(h, slot).start()
        for k in range(1, 4):
            a2_copy(h, k).wait_recv()
            b2_copy(h, k).wait_recv()
        s3[h, :, 0] = four(sa2[h, z], ra2, h).astype(BF16)
        s3[h, :, 1] = four(sb2[h, y], rb2, h).astype(BF16)
        for k in (2, 1, 3):
            x3_copy(h, k).start()

    def output(h):
        cols = pl.ds(pl.multiple_of(h * 128, 128), 128)
        for slot in range(7):
            c3_copy(h, slot).wait_recv()
        mine = four(c3[h, y], rc3, h)
        other = (rc3[h, 3].astype(F32) + rc3[h, 4].astype(F32)) + (
            rc3[h, 5].astype(F32) + rc3[h, 6].astype(F32)
        )
        gk_o[pl.ds(48, 16), cols] = jnp.where(grp == 0, mine, other)
        gv_o[pl.ds(48, 16), cols] = jnp.where(grp == 0, other, mine)
        for k in range(1, 4):
            x3_copy(h, k).wait_recv()
        total = four(s3[h, xlo], r3, h)
        gk_o[pl.ds(0, 48), cols] = total[0]
        gv_o[pl.ds(0, 48), cols] = total[1]

    def head(h, carry):
        kt[...] = kv[:, pl.ds(pl.multiple_of(h * 128, 128), 128)].T
        attend(h, 3)

        @pl.when(h > 2)
        def _():
            second_a(h - 3)

        attend(h, 2)
        attend(h, 1)

        @pl.when(h > 0)
        def _():
            prompt_rows(h - 1)

        @pl.when(h > 1)
        def _():
            second_bc(h - 2)

        attend(h, 0)

        @pl.when(h > 2)
        def _():
            third(h - 3)

        @pl.when(h > 0)
        def _():
            contract(h - 1)

        finish(h)
        return carry

    def wrap(h, carry):
        output(h)
        for part in range(2):
            g_copy(h, part).wait_send()
        for k in range(1, 8):
            pg_copy(h, k).wait_send()
            c3_copy(h, k - 1).wait_send()
        for k in range(1, 4):
            for copy in (a1_copy, b1_copy, c1_copy, a2_copy, b2_copy, c2_copy, x3_copy):
                copy(h, k).wait_send()
        return carry

    lax.fori_loop(0, KVH, head, 0)
    contract_last(3)
    third(1)
    second_a(2)
    for slot in range(11):
        stat_copy(slot).wait_send()
    for k in range(4):
        gather(k).wait_send()
    for k in range(1, 4):
        forward(k).wait_send()
    for seg in range(4):
        for copy in x_remote(seg):
            copy.wait_send()
    lax.fori_loop(0, 1, wrap, 0)
    second_bc(3)
    second_a(3)
    third(2)
    lax.fori_loop(1, 2, wrap, 0)
    third(3)
    lax.fori_loop(2, KVH, wrap, 0)


def body(
    prompt_states, response_states, queries, grad_output, key_weight, value_weight,
    rewards, lengths, group_ids,
):
    cosine, sine = rotary_tables()
    hbm = pl.BlockSpec(memory_space=pltpu.HBM)
    vmem = pl.BlockSpec(memory_space=pltpu.VMEM)
    dma = pltpu.SemaphoreType.DMA
    scratch = [
        pltpu.VMEM((PSH, D), BF16),
        pltpu.VMEM((RLEN, D), BF16),
        pltpu.VMEM((D, 1024), BF16),
        pltpu.VMEM((PLEN + RLEN, 128), F32),
        pltpu.VMEM((PLEN + RLEN, 128), F32),
        pltpu.VMEM((576, 2048), BF16),
        pltpu.VMEM((2048, 1152), BF16),
        pltpu.VMEM((PSH, 1024), F32),
        pltpu.VMEM((RLEN, 1024), F32),
        pltpu.VMEM((1024, 1024), BF16),
        pltpu.VMEM((128, 1024), BF16),
        pltpu.VMEM((1024, 128), F32),
        pltpu.VMEM((1024, 128), F32),
        pltpu.VMEM((KVH, 1152, 256), BF16),
        pltpu.VMEM((KVH, 8, PSH, 256), BF16),
        pltpu.VMEM((KVH, 7, PSH, 256), BF16),
        pltpu.VMEM((KVH, 4, 4, 2, 48, 128), BF16),
        pltpu.VMEM((KVH, 4, 4, 2, 48, 128), BF16),
        pltpu.VMEM((KVH, 4, 4, 4, 16, 128), BF16),
        pltpu.VMEM((KVH, 3, 4, 2, 48, 128), BF16),
        pltpu.VMEM((KVH, 3, 4, 2, 48, 128), BF16),
        pltpu.VMEM((KVH, 3, 4, 4, 16, 128), BF16),
        pltpu.VMEM((KVH, 4, 2, 48, 128), BF16),
        pltpu.VMEM((KVH, 4, 2, 48, 128), BF16),
        pltpu.VMEM((KVH, 4, 4, 16, 128), BF16),
        pltpu.VMEM((KVH, 3, 2, 48, 128), BF16),
        pltpu.VMEM((KVH, 3, 2, 48, 128), BF16),
        pltpu.VMEM((KVH, 3, 4, 16, 128), BF16),
        pltpu.VMEM((KVH, 2, 2, 48, 128), BF16),
        pltpu.VMEM((KVH, 3, 2, 48, 128), BF16),
        pltpu.VMEM((KVH, 4, 16, 128), BF16),
        pltpu.VMEM((KVH, 7, 16, 128), BF16),
        pltpu.VMEM((3, 8, 128), F32),
        pltpu.VMEM((11, 8, 128), F32),
        dma((10,)), dma((8,)), dma((8,)), dma((7,)), dma((7,)),
        dma((11,)), dma((11,)), dma((KVH, 2)), dma((KVH, 2)), dma((KVH, 7)), dma((KVH, 7)),
        dma((KVH, 7)), dma((KVH, 7)),
    ] + [dma((KVH, 3)) for _ in range(14)]
    dq, gk, gv = pl.pallas_call(
        kernel,
        out_shape=(
            jax.ShapeDtypeStruct((RLEN, 2048), BF16),
            jax.ShapeDtypeStruct((64, 512), F32),
            jax.ShapeDtypeStruct((64, 512), F32),
        ),
        in_specs=[hbm] * 8 + [vmem] * 3,
        out_specs=(vmem, vmem, vmem),
        scratch_shapes=scratch,
        compiler_params=pltpu.CompilerParams(
            collective_id=0, has_side_effects=True, vmem_limit_bytes=51 * 2**20
        ),
        name="surrogate_grad",
    )(
        *[pltpu.with_memory_space_constraint(a, pltpu.HBM) for a in (prompt_states[0], response_states[0, 0], queries[0, 0], grad_output[0, 0])],
        key_weight, value_weight, *[pltpu.with_memory_space_constraint(jnp.asarray(a), pltpu.HBM) for a in (cosine, sine)],
        rewards, lengths, group_ids,
    )
    return dq[None, None], gk, gv


def solution(mesh):
    row = P("grp", ("prompt", "resp"))
    tokens = P("grp", ("prompt", "resp"), None, None)
    return jax.shard_map(
        body,
        mesh=mesh,
        in_specs=(P("grp", "prompt", None), tokens, tokens, tokens, P(), P(), row, row, row),
        out_specs=(tokens, P(("prompt", "resp"), None), P(("prompt", "resp"), None)),
        check_vma=False,
    )
```

```python
import functools
import math

import jax
import jax.numpy as jnp
import numpy as np
from jax import lax
from jax.experimental import pallas as pl
from jax.experimental.pallas import tpu as pltpu
from jax.sharding import PartitionSpec as P

HEAD_DIM = 128
KVH = 4
RLEN = 512
PLEN = 512
PSH = 64
D = 4096
NADV = 8
DBASE = 1024
THETA = 1000000.0
EPS = 1e-06
SCALE = 1.0 / math.sqrt(HEAD_DIM)
EXP2_SCALE = math.log2(math.e) / math.sqrt(HEAD_DIM)

F32 = jnp.float32
BF16 = jnp.bfloat16
NT = (((1,), (1,)), ((), ()))
MESH = pl.DeviceIdType.MESH


def rotary_tables():
    half = HEAD_DIM // 2
    steps = np.arange(half, dtype=np.float32)
    freq = np.power(np.float32(THETA), np.float32(-2.0) * steps / np.float32(2.0 * half))
    positions = np.arange(PLEN + RLEN, dtype=np.float32)
    angle = (positions[:, None] * freq.astype(np.float32)[None, :]).astype(np.float64)
    cosine, sine = np.cos(angle), np.sin(angle)
    return (
        np.concatenate([cosine, cosine], axis=1).astype(np.float32),
        np.concatenate([-sine, sine], axis=1).astype(np.float32),
    )


def finish_head(raw, cosine, sine):
    factor = lax.rsqrt(jnp.mean(raw * raw, axis=-1, keepdims=True) + EPS)
    normed = raw * factor
    return normed * cosine + pltpu.roll(normed, HEAD_DIM // 2, 1) * sine


def head_backward(grad, raw, cosine, sine):
    factor = lax.rsqrt(jnp.mean(raw * raw, axis=-1, keepdims=True) + EPS)
    normed = raw * factor
    unturned = grad * cosine - pltpu.roll(grad, HEAD_DIM // 2, 1) * sine
    inner = jnp.mean(unturned * normed, axis=-1, keepdims=True)
    return factor * (unturned - normed * inner)


def kernel(
    ps_h, st_h, q_h, go_h, wk_h, wv_h, cos_h, sin_h, rew, lens, ids,
    dq_o, gk_o, gv_o,
    ps_v, st_v, w_v, cos_t, sin_t, x_v, xt, praw, oraw, kv, kt, dk, dv,
    g_b, pgs, pgr, sa, sb, sc, ra1, rb1, rc1, sa2, sb2, sc2, ra2, rb2, rc2, s3, r3, c3, rc3,
    st_s, st_r,
    lsem, xs, xr, ags, agr, sts, strr, gs, gr, pss, psr, c3s, c3r,
    a1s, a1r, b1s, b1r, c1s, c1r, a2s, a2r, b2s, b2r, c2s, c2r, x3s, x3r,
):
    grp = lax.axis_index("grp")
    pr = lax.axis_index("prompt")
    rs = lax.axis_index("resp")
    y = pr // 2
    c = pr % 2
    z = rs // 2
    xlo = rs % 2
    x = grp * 2 + xlo

    def prompt_peer(k):
        return (grp, (pr + k) % 8, rs)

    def core_peer():
        return (grp, y * 2 + (1 - c), rs)

    def y_peer(k):
        return (grp, ((y + k) % 4) * 2 + c, rs)

    def z_peer(k):
        return (grp, pr, ((z + k) % 4) * 2 + xlo)

    def x_peer(k):
        other = (x + k) % 4
        return (other // 2, pr, z * 2 + other % 2)

    def cross_peer(k):
        return (1 - grp, ((y + k) % 4) * 2 + c, rs)

    def pair_peer():
        return (grp, pr, z * 2 + (1 - xlo))

    def rcopy(src, dst, send, recv, dev):
        return pltpu.make_async_remote_copy(
            src_ref=src, dst_ref=dst, send_sem=send, recv_sem=recv,
            device_id=dev, device_id_type=MESH,
        )

    loads = [
        pltpu.make_async_copy(ps_h, ps_v, lsem.at[0]),
        pltpu.make_async_copy(wk_h, w_v.at[:, pl.ds(0, 512)], lsem.at[1]),
        pltpu.make_async_copy(wv_h, w_v.at[:, pl.ds(512, 512)], lsem.at[2]),
        pltpu.make_async_copy(st_h, st_v, lsem.at[3]),
        pltpu.make_async_copy(cos_h, cos_t, lsem.at[4]),
        pltpu.make_async_copy(sin_h, sin_t, lsem.at[5]),
    ]
    for load in loads[:3] + loads[4:6]:
        load.start()

    def x_remote(seg):
        cols = pl.ds(pl.multiple_of(seg * 1024 + (1 - c) * 512, 512), 512)
        here = pl.ds(seg * 512, 512)
        return (
            rcopy(st_v.at[:, cols], x_v.at[pl.ds(0, 512), here], xs.at[seg], xr.at[seg], core_peer()),
            rcopy(ps_v.at[:, cols], x_v.at[pl.ds(512, 64), here], xs.at[4 + seg], xr.at[4 + seg], core_peer()),
        )

    barrier = pltpu.get_barrier_semaphore()
    for k in range(1, 8):
        pl.semaphore_signal(barrier, inc=1, device_id=prompt_peer(k), device_id_type=MESH)
    for k in range(1, 4):
        pl.semaphore_signal(barrier, inc=1, device_id=z_peer(k), device_id_type=MESH)
        pl.semaphore_signal(barrier, inc=1, device_id=x_peer(k), device_id_type=MESH)
        pl.semaphore_signal(barrier, inc=1, device_id=cross_peer(k), device_id_type=MESH)
    pl.semaphore_wait(barrier, 16)

    lane = lax.broadcasted_iota(jnp.int32, (8, 128), 1)
    row = lax.broadcasted_iota(jnp.int32, (8, 128), 0)
    reward = jnp.broadcast_to(rew[...], (8, 128))
    onehot = jnp.where(lane == jnp.broadcast_to(ids[...], (8, 128)), 1.0, 0.0).astype(F32)
    st_s[0] = onehot * jnp.where(
        row == 0, 1.0, jnp.where(row == 1, reward, jnp.where(row == 2, reward * reward, 0.0))
    )

    def stat_copy(slot):
        if slot < 7:
            return rcopy(st_s.at[0], st_r.at[slot], sts.at[slot], strr.at[slot], prompt_peer(slot + 1))
        if slot < 10:
            return rcopy(st_s.at[1], st_r.at[slot], sts.at[slot], strr.at[slot], z_peer(slot - 6))
        return rcopy(st_s.at[2], st_r.at[slot], sts.at[slot], strr.at[slot], pair_peer())

    for slot in range(7):
        stat_copy(slot).start()

    loads[0].wait()
    loads[1].wait()
    loads[3].start()

    def prompt_tile(n, carry):
        cols = pl.ds(pl.multiple_of(n * 256, 256), 256)
        praw[:, cols] = jnp.dot(ps_v[...], w_v[:, cols], preferred_element_type=F32)
        return carry

    lax.fori_loop(0, 2, prompt_tile, 0)
    loads[2].wait()
    lax.fori_loop(2, 4, prompt_tile, 0)
    prow = pl.ds(pl.multiple_of(pr * PSH, PSH), PSH)
    loads[4].wait()
    loads[5].wait()
    pcos, psin = cos_t[prow, :], sin_t[prow, :]
    for h in range(KVH):
        cols = pl.ds(h * 128, 128)
        kv[prow, cols] = finish_head(praw[:, cols], pcos, psin).astype(BF16)
    kv[prow, pl.ds(512, 512)] = praw[:, pl.ds(512, 512)].astype(BF16)

    def shard(index):
        return kv.at[pl.ds(pl.multiple_of(index * PSH, PSH), PSH)]

    def y_shard(k, core):
        return shard(((y + 4 - k) % 4) * 2 + core)

    def gather(k):
        dev = core_peer() if k == 0 else y_peer(k)
        return rcopy(shard(pr), shard(pr), ags.at[k], agr.at[k], dev)

    def gathered(k):
        theirs = shard(y * 2 + (1 - c)) if k == 0 else y_shard(k, c)
        return rcopy(theirs, theirs, ags.at[k], agr.at[k], core_peer())

    def forward(k):
        return rcopy(y_shard(k, c), y_shard(k, c), ags.at[3 + k], agr.at[3 + k], core_peer())

    def forwarded(k):
        theirs = y_shard(k, 1 - c)
        return rcopy(theirs, theirs, ags.at[3 + k], agr.at[3 + k], core_peer())

    for k in (1, 2, 3, 0):
        gather(k).start()

    for slot in range(7):
        stat_copy(slot).wait_recv()
    st_s[1] = st_s[0] + (
        ((st_r[0] + st_r[1]) + (st_r[2] + st_r[3])) + ((st_r[4] + st_r[5]) + st_r[6])
    )
    for slot in range(7, 10):
        stat_copy(slot).start()

    loads[3].wait()
    for seg in range(4):
        for copy in x_remote(seg):
            copy.start()

    def own_tile(n, carry):
        cols = pl.ds(pl.multiple_of(n * 256, 256), 256)
        oraw[:, cols] = jnp.dot(st_v[...], w_v[:, cols], preferred_element_type=F32)
        for t in range(2):
            here = pl.ds(pl.multiple_of(n * 512 + t * 256, 256), 256)
            mine = pl.ds(pl.multiple_of(n * 1024 + c * 512 + t * 256, 256), 256)
            xt[here, pl.ds(0, 512)] = st_v[:, mine].T
        return carry

    lax.fori_loop(0, 4, own_tile, 0)
    late = [
        pltpu.make_async_copy(
            array.at[:, pl.ds(half * 1024, 1024)], w_v.at[pl.ds(base + half * 512, 512)], lsem.at[6 + n * 2 + half]
        )
        for n, (array, base) in enumerate(((go_h, DBASE), (q_h, 0)))
        for half in range(2)
    ]
    for load in late:
        load.start()
    for k in range(1, 4):
        gathered(k).wait_recv()
        forward(k).start()

    for slot in range(7, 10):
        stat_copy(slot).wait_recv()
    st_s[2] = (st_s[1] + st_r[7]) + (st_r[8] + st_r[9])
    stat_copy(10).start()

    own = pl.ds(PLEN, RLEN)
    ocos, osin = cos_t.at[own], sin_t.at[own]

    def own_keys(h, carry):
        cols = pl.ds(pl.multiple_of(h * 128, 128), 128)
        kv[own, cols] = finish_head(oraw[:, cols], ocos[...], osin[...]).astype(BF16)
        return carry

    lax.fori_loop(0, KVH, own_keys, 0)
    kv[own, pl.ds(512, 512)] = oraw[:, pl.ds(512, 512)].astype(BF16)

    for seg in range(4):
        for copy in x_remote(seg):
            copy.wait_recv()

    def turn(n, carry):
        here = pl.ds(pl.multiple_of(n * 256, 256), 256)
        mine = pl.ds(pl.multiple_of((n // 2) * 1024 + c * 512 + (n % 2) * 256, 256), 256)
        xt[here, pl.ds(512, 512)] = x_v[pl.ds(0, 512), here].T
        xt[here, pl.ds(1024, 128)] = jnp.concatenate([ps_v[:, mine], x_v[pl.ds(512, 64), here]], axis=0).T
        return carry

    lax.fori_loop(0, 8, turn, 0)

    stat_copy(10).wait_recv()
    sums = st_s[2] + st_r[10]
    count, total, square = sums[0:1], sums[1:2], sums[2:3]
    members = jnp.maximum(count, 1.0)
    mean = total / members
    spread = jnp.sqrt(jnp.maximum(square / members - mean * mean, 0.0))
    mine = onehot[0:1]
    own_mean = jnp.sum(mine * mean, axis=1, keepdims=True)
    own_spread = jnp.sum(mine * spread, axis=1, keepdims=True)
    advantage = (rew[...] - own_mean) / jnp.maximum(own_spread, 0.5)
    weight = advantage / lens[...].astype(F32)
    token = lax.broadcasted_iota(jnp.int32, (RLEN, 128), 0)
    live = token < jnp.broadcast_to(lens[...], (RLEN, 128))
    coef = jnp.where(live, jnp.broadcast_to(weight, (RLEN, 128)), 0.0)
    for half in range(2):
        late[half].wait()
        rows = pl.ds(DBASE + half * 512, 512)
        for n in range(8):
            cols = pl.ds(n * 128, 128)
            w_v[rows, cols] = (w_v[rows, cols].astype(F32) * coef).astype(BF16)
    late[2].wait()
    late[3].wait()
    gathered(0).wait_recv()
    for k in range(1, 4):
        forwarded(k).wait_recv()

    def attend(h, b):
        count = PLEN + 128 * (b + 1)
        rows = pl.ds(b * 128, 128)
        keys = kv[pl.ds(0, count), pl.ds(pl.multiple_of(h * 128, 128), 128)]
        vals = kv[pl.ds(0, count), pl.ds(pl.multiple_of(512 + h * 128, 128), 128)]
        cols = [pl.ds(pl.multiple_of((h * 4 + j) * 128, 128), 128) for j in range(4)]
        part = [pl.ds(pl.multiple_of((h % 2) * 512 + j * 128, 128), 128) for j in range(4)]
        start = (h // 2) * 512 + b * 128
        qrows = pl.ds(pl.multiple_of(start, 128), 128)
        drows = pl.ds(pl.multiple_of(DBASE + start, 128), 128)
        q = jnp.concatenate([w_v[qrows, cc] for cc in part], axis=0)
        do = jnp.concatenate([w_v[drows, cc] for cc in part], axis=0)
        s = lax.dot_general(keys, q, NT, preferred_element_type=F32)
        key = lax.broadcasted_iota(jnp.int32, (128, 512), 0)
        query = lax.broadcasted_iota(jnp.int32, (128, 512), 1) % 128
        s = jnp.concatenate(
            [s[: count - 128], jnp.where(key <= query, s[count - 128 :], -jnp.inf)], axis=0
        )
        peak = jnp.max(s, axis=0, keepdims=True)
        e = jnp.exp2((s - peak) * EXP2_SCALE)
        inverse = 1.0 / jnp.sum(e, axis=0, keepdims=True)
        dp = lax.dot_general(vals, do, NT, preferred_element_type=F32)
        delta = jnp.sum(e * dp, axis=0, keepdims=True) * inverse
        p = e * inverse
        ds = (p * (dp - delta)).astype(BF16)
        gv = jnp.dot(p.astype(BF16), do, preferred_element_type=F32)
        gk = jnp.dot(ds, q, preferred_element_type=F32)
        if b == 3:
            dv[...] = gv
            dk[...] = gk
        else:
            dv[pl.ds(0, count)] += gv
            dk[pl.ds(0, count)] += gk
        dq = (jnp.dot(kt[:, pl.ds(0, count)], ds, preferred_element_type=F32) * SCALE).T.astype(BF16)
        for j, cc in enumerate(cols):
            dq_o[rows, cc] = dq[j * 128 : (j + 1) * 128]

    def g_copy(h, part):
        mine = (pl.ds(0, 512), pl.ds(1024, 64))[part]
        theirs = (pl.ds(512, 512), pl.ds(1088, 64))[part]
        return rcopy(g_b.at[h, mine], g_b.at[h, theirs], gs.at[h, part], gr.at[h, part], core_peer())

    def pg_copy(h, k):
        return rcopy(pgs.at[h, (pr + k) % 8], pgr.at[h, k - 1], pss.at[h, k - 1], psr.at[h, k - 1], prompt_peer(k))

    def a1_copy(h, k):
        return rcopy(sa.at[h, (y + k) % 4], ra1.at[h, k - 1], a1s.at[h, k - 1], a1r.at[h, k - 1], y_peer(k))

    def b1_copy(h, k):
        return rcopy(sb.at[h, (z + k) % 4], rb1.at[h, k - 1], b1s.at[h, k - 1], b1r.at[h, k - 1], z_peer(k))

    def c1_copy(h, k):
        return rcopy(sc.at[h, (x + k) % 4], rc1.at[h, k - 1], c1s.at[h, k - 1], c1r.at[h, k - 1], x_peer(k))

    def a2_copy(h, k):
        return rcopy(sa2.at[h, (z + k) % 4], ra2.at[h, k - 1], a2s.at[h, k - 1], a2r.at[h, k - 1], z_peer(k))

    def b2_copy(h, k):
        return rcopy(sb2.at[h, (y + k) % 4], rb2.at[h, k - 1], b2s.at[h, k - 1], b2r.at[h, k - 1], y_peer(k))

    def c2_copy(h, k):
        return rcopy(sc2.at[h, (z + k) % 4], rc2.at[h, k - 1], c2s.at[h, k - 1], c2r.at[h, k - 1], z_peer(k))

    def x3_copy(h, k):
        return rcopy(s3.at[h, (x + k) % 2], r3.at[h, k - 1], x3s.at[h, k - 1], x3r.at[h, k - 1], x_peer(k))

    def c3_copy(h, slot):
        k = slot + 1 if slot < 3 else slot - 3
        dev = y_peer(k) if slot < 3 else cross_peer(k)
        return rcopy(c3.at[h, (y + k) % 4], rc3.at[h, slot], c3s.at[h, slot], c3r.at[h, slot], dev)

    def finish(h):
        cols = pl.ds(pl.multiple_of(h * 128, 128), 128)
        for t in range(8):
            pgs[h, t, :, pl.ds(0, 128)] = (dk[pl.ds(t * 64, 64)] * SCALE).astype(BF16)
            pgs[h, t, :, pl.ds(128, 128)] = dv[pl.ds(t * 64, 64)].astype(BF16)
        for k in (4, 3, 5, 2, 6, 1, 7):
            pg_copy(h, k).start()
        g_b[h, pl.ds(0, 512), pl.ds(0, 128)] = head_backward(
            dk[own] * SCALE, oraw[:, cols], ocos[...], osin[...]
        ).astype(BF16)
        g_b[h, pl.ds(0, 512), pl.ds(128, 128)] = dv[own].astype(BF16)
        g_copy(h, 0).start()

        @pl.when(h > 0)
        def _():
            for k in range(1, 4):
                a1_copy(h - 1, k).start()


    def prompt_rows(h):
        cols = pl.ds(pl.multiple_of(h * 128, 128), 128)
        total = pgs[h, pr].astype(F32)
        for k in range(1, 8):
            pg_copy(h, k).wait_recv()
            total = total + pgr[h, k - 1].astype(F32)
        g_b[h, pl.ds(1024, 64), pl.ds(0, 128)] = head_backward(
            total[:, :128], praw[:, cols], cos_t[prow, :], sin_t[prow, :]
        ).astype(BF16)
        g_b[h, pl.ds(1024, 64), pl.ds(128, 128)] = total[:, 128:].astype(BF16)
        g_copy(h, 1).start()

    def emit(h, seg, out):
        out = out.astype(BF16)
        for zz in range(4):
            for xx in range(2):
                at = zz * 128 + xx * 64
                sa[h, seg, zz, xx] = out[at : at + 48, :128]
                sb[h, zz, seg, xx] = out[at : at + 48, 128:]
                sc[h, xx, zz, seg] = out[at + 48 : at + 64, :128]
                sc[h, xx + 2, zz, seg] = out[at + 48 : at + 64, 128:]

    def contract(h):
        g_copy(h, 0).wait_recv()
        g_copy(h, 1).wait_recv()

        def segment(seg, carry):
            rows = pl.ds(pl.multiple_of(seg * 512, 512), 512)
            emit(h, seg, jnp.dot(xt[rows, :], g_b[h], preferred_element_type=F32))
            return carry

        lax.fori_loop(0, 4, segment, 0)
        for k in (2, 1, 3):
            b1_copy(h, k).start()
            c1_copy(h, k).start()

    def contract_last(h):
        g_copy(h, 0).wait_recv()

        def responses(seg, carry):
            rows = pl.ds(pl.multiple_of(seg * 512, 512), 512)
            cols = pl.ds(pl.multiple_of(seg * 256, 256), 256)
            oraw[:, cols] = jnp.dot(
                xt[rows, pl.ds(0, 1024)], g_b[h, pl.ds(0, 1024)], preferred_element_type=F32
            )
            return carry

        lax.fori_loop(0, 4, responses, 0)
        second_a(h - 2)
        prompt_rows(h)
        second_bc(h - 1)
        g_copy(h, 1).wait_recv()

        def prompts(i, carry):
            k = (2 + i) * (1 - i // 2) + (3 - i) * (i // 2)
            seg = (y + k) % 4
            rows = pl.ds(pl.multiple_of(seg * 512, 512), 512)
            cols = pl.ds(pl.multiple_of(seg * 256, 256), 256)
            part = jnp.dot(
                xt[rows, pl.ds(1024, 128)], g_b[h, pl.ds(1024, 128)], preferred_element_type=F32
            )
            emit(h, seg, oraw[:, cols] + part)

            @pl.when(i < 3)
            def _():
                a1_copy(h, k).start()

            return carry

        lax.fori_loop(0, 4, prompts, 0)
        for k in (2, 1, 3):
            b1_copy(h, k).start()
            c1_copy(h, k).start()

    def four(own_block, got, h):
        return (own_block.astype(F32) + got[h, 0].astype(F32)) + (
            got[h, 1].astype(F32) + got[h, 2].astype(F32)
        )

    def second_bc(h):
        for k in range(1, 4):
            c1_copy(h, k).wait_recv()
        sc2[h] = four(sc[h, x], rc1, h).astype(BF16)
        for k in (2, 1, 3):
            c2_copy(h, k).start()
        for k in range(1, 4):
            b1_copy(h, k).wait_recv()
        sb2[h] = four(sb[h, z], rb1, h).astype(BF16)
        for k in (2, 1, 3):
            b2_copy(h, k).start()

    def second_a(h):
        for k in range(1, 4):
            a1_copy(h, k).wait_recv()
        sa2[h] = four(sa[h, y], ra1, h).astype(BF16)
        for k in (2, 1, 3):
            a2_copy(h, k).start()

    def third(h):
        for k in range(1, 4):
            c2_copy(h, k).wait_recv()
        c3[h] = four(sc2[h, z], rc2, h).astype(BF16)
        for slot in (5, 4, 6, 1, 3, 0, 2):
            c3_copy(h, slot).start()
        for k in range(1, 4):
            a2_copy(h, k).wait_recv()
            b2_copy(h, k).wait_recv()
        s3[h, :, 0] = four(sa2[h, z], ra2, h).astype(BF16)
        s3[h, :, 1] = four(sb2[h, y], rb2, h).astype(BF16)
        for k in (2, 1, 3):
            x3_copy(h, k).start()

    def output(h):
        cols = pl.ds(pl.multiple_of(h * 128, 128), 128)
        for slot in range(7):
            c3_copy(h, slot).wait_recv()
        mine = four(c3[h, y], rc3, h)
        other = (rc3[h, 3].astype(F32) + rc3[h, 4].astype(F32)) + (
            rc3[h, 5].astype(F32) + rc3[h, 6].astype(F32)
        )
        gk_o[pl.ds(48, 16), cols] = jnp.where(grp == 0, mine, other)
        gv_o[pl.ds(48, 16), cols] = jnp.where(grp == 0, other, mine)
        for k in range(1, 4):
            x3_copy(h, k).wait_recv()
        total = four(s3[h, xlo], r3, h)
        gk_o[pl.ds(0, 48), cols] = total[0]
        gv_o[pl.ds(0, 48), cols] = total[1]

    def head(h, carry):
        kt[...] = kv[:, pl.ds(pl.multiple_of(h * 128, 128), 128)].T
        attend(h, 3)

        @pl.when(h > 2)
        def _():
            second_a(h - 3)

        attend(h, 2)
        attend(h, 1)

        @pl.when(h > 0)
        def _():
            prompt_rows(h - 1)

        @pl.when(h > 1)
        def _():
            second_bc(h - 2)

        attend(h, 0)

        @pl.when(h > 2)
        def _():
            third(h - 3)

        @pl.when(h > 0)
        def _():
            contract(h - 1)

        finish(h)
        return carry

    def wrap(h, carry):
        output(h)
        for part in range(2):
            g_copy(h, part).wait_send()
        for k in range(1, 8):
            pg_copy(h, k).wait_send()
            c3_copy(h, k - 1).wait_send()
        for k in range(1, 4):
            for copy in (a1_copy, b1_copy, c1_copy, a2_copy, b2_copy, c2_copy, x3_copy):
                copy(h, k).wait_send()
        return carry

    lax.fori_loop(0, KVH, head, 0)
    contract_last(3)
    third(1)
    second_a(2)
    for slot in range(11):
        stat_copy(slot).wait_send()
    for k in range(4):
        gather(k).wait_send()
    for k in range(1, 4):
        forward(k).wait_send()
    for seg in range(4):
        for copy in x_remote(seg):
            copy.wait_send()
    lax.fori_loop(0, 1, wrap, 0)
    second_bc(3)
    second_a(3)
    third(2)
    lax.fori_loop(1, 2, wrap, 0)
    third(3)
    lax.fori_loop(2, KVH, wrap, 0)


def body(
    prompt_states, response_states, queries, grad_output, key_weight, value_weight,
    rewards, lengths, group_ids,
):
    cosine, sine = rotary_tables()
    hbm = pl.BlockSpec(memory_space=pltpu.HBM)
    vmem = pl.BlockSpec(memory_space=pltpu.VMEM)
    dma = pltpu.SemaphoreType.DMA
    scratch = [
        pltpu.VMEM((PSH, D), BF16),
        pltpu.VMEM((RLEN, D), BF16),
        pltpu.VMEM((D, 1024), BF16),
        pltpu.VMEM((PLEN + RLEN, 128), F32),
        pltpu.VMEM((PLEN + RLEN, 128), F32),
        pltpu.VMEM((576, 2048), BF16),
        pltpu.VMEM((2048, 1152), BF16),
        pltpu.VMEM((PSH, 1024), F32),
        pltpu.VMEM((RLEN, 1024), F32),
        pltpu.VMEM((1024, 1024), BF16),
        pltpu.VMEM((128, 1024), BF16),
        pltpu.VMEM((1024, 128), F32),
        pltpu.VMEM((1024, 128), F32),
        pltpu.VMEM((KVH, 1152, 256), BF16),
        pltpu.VMEM((KVH, 8, PSH, 256), BF16),
        pltpu.VMEM((KVH, 7, PSH, 256), BF16),
        pltpu.VMEM((KVH, 4, 4, 2, 48, 128), BF16),
        pltpu.VMEM((KVH, 4, 4, 2, 48, 128), BF16),
        pltpu.VMEM((KVH, 4, 4, 4, 16, 128), BF16),
        pltpu.VMEM((KVH, 3, 4, 2, 48, 128), BF16),
        pltpu.VMEM((KVH, 3, 4, 2, 48, 128), BF16),
        pltpu.VMEM((KVH, 3, 4, 4, 16, 128), BF16),
        pltpu.VMEM((KVH, 4, 2, 48, 128), BF16),
        pltpu.VMEM((KVH, 4, 2, 48, 128), BF16),
        pltpu.VMEM((KVH, 4, 4, 16, 128), BF16),
        pltpu.VMEM((KVH, 3, 2, 48, 128), BF16),
        pltpu.VMEM((KVH, 3, 2, 48, 128), BF16),
        pltpu.VMEM((KVH, 3, 4, 16, 128), BF16),
        pltpu.VMEM((KVH, 2, 2, 48, 128), BF16),
        pltpu.VMEM((KVH, 3, 2, 48, 128), BF16),
        pltpu.VMEM((KVH, 4, 16, 128), BF16),
        pltpu.VMEM((KVH, 7, 16, 128), BF16),
        pltpu.VMEM((3, 8, 128), F32),
        pltpu.VMEM((11, 8, 128), F32),
        dma((10,)), dma((8,)), dma((8,)), dma((7,)), dma((7,)),
        dma((11,)), dma((11,)), dma((KVH, 2)), dma((KVH, 2)), dma((KVH, 7)), dma((KVH, 7)),
        dma((KVH, 7)), dma((KVH, 7)),
    ] + [dma((KVH, 3)) for _ in range(14)]
    dq, gk, gv = pl.pallas_call(
        kernel,
        out_shape=(
            jax.ShapeDtypeStruct((RLEN, 2048), BF16),
            jax.ShapeDtypeStruct((64, 512), F32),
            jax.ShapeDtypeStruct((64, 512), F32),
        ),
        in_specs=[hbm] * 8 + [vmem] * 3,
        out_specs=(vmem, vmem, vmem),
        scratch_shapes=scratch,
        compiler_params=pltpu.CompilerParams(
            collective_id=0, has_side_effects=True, vmem_limit_bytes=51 * 2**20
        ),
        name="surrogate_grad",
    )(
        *[pltpu.with_memory_space_constraint(a, pltpu.HBM) for a in (prompt_states[0], response_states[0, 0], queries[0, 0], grad_output[0, 0])],
        key_weight, value_weight, *[pltpu.with_memory_space_constraint(jnp.asarray(a), pltpu.HBM) for a in (cosine, sine)],
        rewards, lengths, group_ids,
    )
    return dq[None, None], gk, gv


def solution(mesh):
    row = P("grp", ("prompt", "resp"))
    tokens = P("grp", ("prompt", "resp"), None, None)
    return jax.shard_map(
        body,
        mesh=mesh,
        in_specs=(P("grp", "prompt", None), tokens, tokens, tokens, P(), P(), row, row, row),
        out_specs=(tokens, P(("prompt", "resp"), None), P(("prompt", "resp"), None)),
        check_vma=False,
    )
```
